128 devices in a mesh: inp: 32 (over z, x, core), head: 4 (over y).
Axes of the slice: x: 4, y: 4, z: 4, core: 2. Of those that a mesh axis runs over, the one named last changes fastest.
Arguments:
- inputs: bfloat16 [262144, 256], P('inp'), may hold values from -6 to 6
- input_modality: int32 [2048], P('inp'), may hold values from 0 to 2
- queries: bfloat16 [262144, 256], P(('inp', 'head')), may hold values from -6 to 6
- query_modality: int32 [2048], P(('inp', 'head')), may hold values from 0 to 2
- modality_embed: float32 [3, 256], replicated, may hold values from -3 to 3
- latents: float32 [512, 1024], replicated, may hold values from -6 to 6
- ln_in_gain: float32 [256], replicated, may hold values from 0.1 to 1.9
- ln_lat_gain: float32 [1024], replicated, may hold values from 0.1 to 1.9
- enc_wq: bfloat16 [1024, 1024], P(None, 'head'), may hold values from -0.75 to 0.75
- enc_wkv: bfloat16 [2, 256, 1024], P(None, None, 'head'), may hold values from -0.375 to 0.375
- enc_bias: float32 [3, 16, 512], P(None, 'head'), may hold values from -4 to 320, as said below
- enc_wo: bfloat16 [1024, 1024], P('head'), may hold values from -0.1875 to 0.1875
- self_gain: float32 [1024], replicated, may hold values from 0.1 to 1.9
- self_wqkv: bfloat16 [3, 1024, 1024], P(None, None, 'head'), may hold values from -0.1875 to 0.1875
- self_bias: float32 [16, 512, 512], P('head', 'inp'), may hold values from -4 to 320, as said below
- self_wo: bfloat16 [1024, 1024], P('head'), may hold values from -0.1875 to 0.1875
- mlp_gain: float32 [1024], replicated, may hold values from 0.1 to 1.9
- mlp_w1: bfloat16 [1024, 4096], P(None, 'head'), may hold values from -0.1875 to 0.1875
- mlp_w2: bfloat16 [4096, 1024], P('head'), may hold values from -0.09375 to 0.09375
- dec_gain: float32 [1024], replicated, may hold values from 0.1 to 1.9
- dec_wkv: bfloat16 [2, 1024, 1024], replicated, may hold values from -0.1875 to 0.1875
- query_gain: float32 [256], replicated, may hold values from 0.1 to 1.9
- dec_wq: bfloat16 [256, 1024], replicated, may hold values from -0.375 to 0.375
- dec_bias: float32 [3, 16, 512], replicated, may hold values from -4 to 320, as said below
- dec_wo: bfloat16 [1024, 256], replicated, may hold values from -0.375 to 0.375
Outputs:
- decoded: float32 [262144, 256], P(('inp', 'head'))
The draws below stay inside these ranges and needn't reach their ends.
Inputs may be any that keep to these rules, and one draw needn't show every extreme that they name: `enc_bias`: score biases. `self_bias`: score biases. `dec_bias`: score biases.
All inputs are finite; a program needn't handle non-finite values.
Results may differ from the reference program's by a relative error of at most 0.017.
Values may be sent and summed in bfloat16 or wider, within the bound.
No kernel may reach another device: no remote copies, remote signals or barrier semaphores. Data moves between devices by JAX's collectives and lax.ppermute only.
A program may use at most 192 MiB of HBM per device.

```python
import math
import jax
import jax.numpy as jnp
from jax import lax

C_IN = 256
D = 1024
HEADS = 16
HSZ = 64
NLAT = 512
FFN = 4096
MODS = 3
MBLK = 128
POINTS = 262144
QUERIES = 262144


def draw_inputs(key, part):
    key = jax.random.fold_in(key, 41)
    subkeys = jax.random.split(key, 1)
    noise = jnp.clip(jax.random.normal(subkeys[0], (POINTS, C_IN), jnp.float32), -6.0, 6.0)
    return noise.astype(jnp.bfloat16)


def draw_enc_wq(key, part):
    key = jax.random.fold_in(key, 43)
    subkeys = jax.random.split(key, 1)
    spread = 4.0 / math.sqrt(D)
    noise = jnp.clip(jax.random.normal(subkeys[0], (D, D), jnp.float32), -6.0, 6.0) * spread
    return noise.astype(jnp.bfloat16)


def draw_enc_wkv(key, part):
    key = jax.random.fold_in(key, 47)
    spread = 1.0 / math.sqrt(C_IN)
    noise = jnp.clip(jax.random.normal(key, (2, C_IN, D), jnp.float32), -6.0, 6.0) * spread
    return noise.astype(jnp.bfloat16)


def drawn_bias(key, full_shape):
    return jnp.clip(jax.random.normal(key, full_shape, jnp.float32), -4.0, 4.0)


def draw_enc_bias(key, part):
    own_key = jax.random.fold_in(key, 11)
    return drawn_bias(own_key, (MODS, HEADS, NLAT))


def draw_self_bias(key, part):
    own_key = jax.random.fold_in(key, 37)
    return drawn_bias(own_key, (HEADS, NLAT, NLAT))


def draw_dec_bias(key, part):
    own_key = jax.random.fold_in(key, 23)
    return drawn_bias(own_key, (MODS, HEADS, NLAT))


def set_ends(values, rng, low, top_value):
    longest = values.shape.index(max(values.shape))
    spots = []
    for shift in (0, 1):
        where = [jax.random.randint(jax.random.fold_in(rng, axis), (), 0, length) for axis, length in enumerate(values.shape)]
        where[longest] = (where[longest] + shift) % values.shape[longest]
        spots.append(tuple(where))
    return values.at[spots[0]].set(low).at[spots[1]].set(top_value)


def block_scale(stream_key, extent, shards, least, high):
    level = 1.0
    for axis_at, parts in shards:
        draws = jax.random.uniform(jax.random.fold_in(jax.random.fold_in(stream_key, 6), axis_at), (parts,), jnp.float32, least / len(shards), high / len(shards))
        level = level * jnp.repeat(jnp.exp(draws), extent[axis_at] // parts).reshape((-1,) + (1,) * (len(extent) - 1 - axis_at))
    return level


def gaussian(rng, dims, scale, limit, cuts=(), kind=jnp.bfloat16):
    entries = jax.random.normal(rng, dims, jnp.float32) * scale
    if len(cuts) > 0:
        entries = block_scale(rng, dims, cuts, -0.22, 0.18) * entries
    return jnp.clip(entries, min=-limit, max=limit).astype(kind)


def setup_inputs(seed: int = 0) -> dict:
    seeds = jax.random.split(jax.random.key(seed), 26)
    return {
        "inputs": draw_inputs(jax.random.fold_in(seeds[25], 71), 0),
        "input_modality": set_ends(jax.random.randint(seeds[1], (POINTS // MBLK,), 0, MODS), jax.random.fold_in(seeds[1], 1), 0, MODS - 1).astype(jnp.int32),
        "queries": gaussian(seeds[2], (QUERIES, C_IN), 1.0, 6.0, ((0, 128),)),
        "query_modality": set_ends(jax.random.randint(seeds[3], (QUERIES // MBLK,), 0, MODS), jax.random.fold_in(seeds[3], 1), 0, MODS - 1).astype(jnp.int32),
        "modality_embed": gaussian(seeds[4], (MODS, C_IN), 0.5, 3.0, (), jnp.float32),
        "latents": gaussian(seeds[5], (NLAT, D), 1.0, 6.0, (), jnp.float32),
        "ln_in_gain": jnp.clip(1.0 + 0.18 * jax.random.normal(seeds[6], (C_IN,), jnp.float32), 0.1, 1.9),
        "ln_lat_gain": jnp.clip(1.0 + 0.18 * jax.random.normal(seeds[7], (D,), jnp.float32), 0.1, 1.9),
        "enc_wq": draw_enc_wq(jax.random.fold_in(seeds[25], 71), 0),
        "enc_wkv": draw_enc_wkv(jax.random.fold_in(seeds[25], 71), 0),
        "enc_bias": draw_enc_bias(jax.random.fold_in(seeds[25], 71), 0),
        "enc_wo": gaussian(seeds[11], (D, D), D ** -0.5, 0.1875, ((0, 4),)),
        "self_gain": jnp.clip(1.0 + 0.18 * jax.random.normal(seeds[12], (D,), jnp.float32), 0.1, 1.9),
        "self_wqkv": gaussian(seeds[13], (3, D, D), D ** -0.5, 0.1875, ((2, 4),)),
        "self_bias": draw_self_bias(jax.random.fold_in(seeds[25], 71), 0),
        "self_wo": gaussian(seeds[15], (D, D), D ** -0.5, 0.1875, ((0, 4),)),
        "mlp_gain": jnp.clip(1.0 + 0.18 * jax.random.normal(seeds[16], (D,), jnp.float32), 0.1, 1.9),
        "mlp_w1": gaussian(seeds[17], (D, FFN), D ** -0.5, 0.1875, ((1, 4),)),
        "mlp_w2": gaussian(seeds[18], (FFN, D), FFN ** -0.5, 0.09375, ((0, 4),)),
        "dec_gain": jnp.clip(1.0 + 0.18 * jax.random.normal(seeds[19], (D,), jnp.float32), 0.1, 1.9),
        "dec_wkv": gaussian(seeds[20], (2, D, D), D ** -0.5, 0.1875),
        "query_gain": jnp.clip(1.0 + 0.18 * jax.random.normal(seeds[21], (C_IN,), jnp.float32), 0.1, 1.9),
        "dec_wq": gaussian(seeds[22], (C_IN, D), C_IN ** -0.5, 0.375),
        "dec_bias": draw_dec_bias(jax.random.fold_in(seeds[25], 71), 0),
        "dec_wo": gaussian(seeds[24], (D, C_IN), (D // 4) ** -0.5, 0.375),
    }


EPSILON = 1e-05

def layer_norm(values, gain):
    centered = values - lax.optimization_barrier(jnp.mean(values, axis=-1, keepdims=True))
    variance = lax.optimization_barrier(jnp.mean(centered * centered, axis=-1, keepdims=True))
    return centered * lax.rsqrt(variance + EPSILON) * gain

def rounded(values):
    return lax.optimization_barrier(values.astype(jnp.bfloat16))

def widen(values):
    return values.astype(jnp.float32)

def enc_scores(query_heads, key_block, bias_block, scale):
    scores = jnp.einsum('ihd,phd->ihp', query_heads, widen(key_block)) * scale
    lat_count, head_count, width = scores.shape
    scores = scores.reshape(lat_count, head_count, width // MBLK, MBLK) + jnp.transpose(bias_block, (2, 1, 0))[..., None]
    return scores.reshape(lat_count, head_count, width)

def softmax_mix(scores, values):
    row_top = lax.optimization_barrier(jnp.max(scores, axis=-1, keepdims=True))
    weights = jnp.exp(scores - row_top)
    totals = lax.optimization_barrier(jnp.sum(weights, axis=-1))
    mixed = jnp.einsum('hij,jhd->ihd', widen(rounded(weights)), widen(values))
    return mixed / jnp.transpose(totals)[..., None]

def reference(inputs, input_modality, queries, query_modality, modality_embed, latents, ln_in_gain, ln_lat_gain, enc_wq, enc_wkv, enc_bias, enc_wo, self_gain, self_wqkv, self_bias, self_wo, mlp_gain, mlp_w1, mlp_w2, dec_gain, dec_wkv, query_gain, dec_wq, dec_bias, dec_wo):
    scale = 1.0 / math.sqrt(HSZ)
    point_embedded = widen(inputs) + jnp.repeat(modality_embed[input_modality], MBLK, axis=0)
    normed_in = rounded(layer_norm(point_embedded, ln_in_gain))
    enc_keys = rounded(jnp.dot(normed_in, enc_wkv[0], preferred_element_type=jnp.float32))
    enc_values = rounded(jnp.dot(normed_in, enc_wkv[1], preferred_element_type=jnp.float32))
    normed_lat = rounded(layer_norm(latents, ln_lat_gain))
    latent_query = rounded(jnp.dot(normed_lat, enc_wq, preferred_element_type=jnp.float32))
    query_heads = widen(latent_query).reshape(NLAT, HEADS, HSZ)
    block_size = math.gcd(POINTS, 4096)
    block_count = POINTS // block_size
    key_blocks = enc_keys.reshape(block_count, block_size, HEADS, HSZ)
    value_blocks = enc_values.reshape(block_count, block_size, HEADS, HSZ)
    bias_blocks = enc_bias[input_modality].reshape(block_count, block_size // MBLK, HEADS, NLAT)

    def find_max(running, pieces):
        key_block, bias_block = pieces
        scores = enc_scores(query_heads, key_block, bias_block, scale)
        return (jnp.maximum(running, lax.optimization_barrier(jnp.max(scores, axis=-1))), None)
    start_max = jnp.full((NLAT, HEADS), -jnp.inf, jnp.float32)
    enc_max, ignored = lax.scan(find_max, start_max, (key_blocks, bias_blocks))

    def accumulate(carry, pieces):
        totals, summed = carry
        key_block, value_block, bias_block = pieces
        weights = jnp.exp(enc_scores(query_heads, key_block, bias_block, scale) - enc_max[..., None])
        totals = totals + lax.optimization_barrier(jnp.sum(weights, axis=-1))
        summed = summed + jnp.einsum('ihp,phd->ihd', widen(rounded(weights)), widen(value_block))
        return ((totals, summed), None)
    start_carry = (jnp.zeros((NLAT, HEADS), jnp.float32), jnp.zeros((NLAT, HEADS, HSZ), jnp.float32))
    (enc_total, enc_summed), ignored = lax.scan(accumulate, start_carry, (key_blocks, value_blocks, bias_blocks))
    enc_attn = rounded((enc_summed / enc_total[..., None]).reshape(NLAT, D))
    lat_one = latents + jnp.dot(enc_attn, enc_wo, preferred_element_type=jnp.float32)
    normed_one = rounded(layer_norm(lat_one, self_gain))
    self_q = rounded(jnp.dot(normed_one, self_wqkv[0], preferred_element_type=jnp.float32)).reshape(NLAT, HEADS, HSZ)
    self_k = rounded(jnp.dot(normed_one, self_wqkv[1], preferred_element_type=jnp.float32)).reshape(NLAT, HEADS, HSZ)
    self_v = rounded(jnp.dot(normed_one, self_wqkv[2], preferred_element_type=jnp.float32)).reshape(NLAT, HEADS, HSZ)
    self_scores = jnp.einsum('ihd,jhd->hij', widen(self_q), widen(self_k)) * scale + self_bias
    self_attn = rounded(softmax_mix(self_scores, self_v).reshape(NLAT, D))
    lat_two = lat_one + jnp.dot(self_attn, self_wo, preferred_element_type=jnp.float32)
    normed_two = rounded(layer_norm(lat_two, mlp_gain))
    mlp_hidden = rounded(jax.nn.gelu(jnp.dot(normed_two, mlp_w1, preferred_element_type=jnp.float32), approximate=True))
    lat_three = lat_two + jnp.dot(mlp_hidden, mlp_w2, preferred_element_type=jnp.float32)
    normed_three = rounded(layer_norm(lat_three, dec_gain))
    dec_keys = rounded(jnp.dot(normed_three, dec_wkv[0], preferred_element_type=jnp.float32)).reshape(NLAT, HEADS, HSZ)
    dec_values = rounded(jnp.dot(normed_three, dec_wkv[1], preferred_element_type=jnp.float32)).reshape(NLAT, HEADS, HSZ)
    query_embedded = widen(queries) + jnp.repeat(modality_embed[query_modality], MBLK, axis=0)
    normed_query = rounded(layer_norm(query_embedded, query_gain))
    dec_query = rounded(jnp.dot(normed_query, dec_wq, preferred_element_type=jnp.float32))
    dec_size = math.gcd(QUERIES, 2048)
    dec_count = QUERIES // dec_size

    def decode_block(pieces):
        query_block, embed_block, bias_block = pieces
        scores = jnp.einsum('qhd,jhd->hqj', widen(query_block), widen(dec_keys)) * scale
        scores = scores.reshape(HEADS, dec_size // MBLK, MBLK, NLAT) + jnp.transpose(bias_block, (1, 0, 2))[:, :, None, :]
        scores = scores.reshape(HEADS, dec_size, NLAT)
        mixed = rounded(softmax_mix(scores, dec_values).reshape(dec_size, D))
        return embed_block + jnp.dot(mixed, dec_wo, preferred_element_type=jnp.float32)
    decoded = lax.map(decode_block, (dec_query.reshape(dec_count, dec_size, HEADS, HSZ), query_embedded.reshape(dec_count, dec_size, C_IN), dec_bias[query_modality].reshape(dec_count, dec_size // MBLK, HEADS, NLAT)))
    return decoded.reshape(QUERIES, C_IN)
```

```python
import functools
import math

import jax
import jax.numpy as jnp
from jax import lax
from jax.experimental import pallas as pl
from jax.experimental.pallas import tpu as pltpu
from jax.sharding import PartitionSpec as P

HSZ = 64
MODS = 3
MBLK = 128
EPSILON = 1e-05
LOG2E = 1.4426950408889634
SCALE2 = LOG2E / math.sqrt(HSZ)
NEG_FLOOR = -1e30
BF = jnp.bfloat16
F32 = jnp.float32
MIB = 2**20
EXTRA = 128


def dot(a, b):
    return jnp.dot(a, b, preferred_element_type=F32)


def dot_nt(a, b):
    return lax.dot_general(a, b, (((1,), (1,)), ((), ())), preferred_element_type=F32)


def layer_norm(values, gain):
    centered = values - jnp.mean(values, axis=-1, keepdims=True)
    variance = jnp.mean(centered * centered, axis=-1, keepdims=True)
    return centered * lax.rsqrt(variance + EPSILON) * gain


def three_parts(values):
    high = values.astype(BF)
    rest = values - high.astype(F32)
    mid = rest.astype(BF)
    low = (rest - mid.astype(F32)).astype(BF)
    return high.astype(F32), mid.astype(F32), low.astype(F32)


def bias_rows(bias, rows):
    index = lax.broadcasted_iota(jnp.int32, (rows, bias.shape[1]), 0)
    block = jnp.zeros((rows, bias.shape[1]), F32)
    for part, piece in enumerate(three_parts(bias)):
        for mod in range(MODS):
            block = jnp.where(index == MODS * part + mod, piece[mod : mod + 1, :], block)
    return block


def modality_hot(mod, shape, dim):
    index = lax.broadcasted_iota(jnp.int32, shape, dim)
    hit = (index == mod) | (index == mod + MODS) | (index == mod + 2 * MODS)
    return jnp.where(hit, 1.0, 0.0).astype(BF)


def embed_norm(mod_ref, first, x_ref, table_ref, gain, n_ref):
    for b in range(x_ref.shape[0] // MBLK):
        rows = slice(b * MBLK, (b + 1) * MBLK)
        mod = mod_ref[first + b]
        embedded = x_ref[rows, :].astype(F32) + table_ref[pl.ds(mod, 1), :]
        n_ref[rows, :] = layer_norm(embedded, gain).astype(BF)


def encode_kernel(
    heads,
    mod_ref,
    x_ref,
    table_ref,
    gain_ref,
    lat_ref,
    lat_gain_ref,
    wq_ref,
    wkv_ref,
    bias_ref,
    out_ref,
    qx_ref,
    wvt_ref,
    n_ref,
    hot_ref,
    m_ref,
    acc_ref,
):
    step = pl.program_id(0)
    blocks = x_ref.shape[0] // MBLK
    lat_count = lat_ref.shape[0]

    @pl.when(step == 0)
    def _():
        normed = layer_norm(lat_ref[...], lat_gain_ref[...]).astype(BF)
        query = (dot(normed, wq_ref[...]) * SCALE2).T
        qx_ref[...] = jnp.zeros(qx_ref.shape, BF)
        for h in range(heads):
            half = (h % 2) * HSZ
            qx_ref[h, half : half + HSZ, :] = query[h * HSZ : (h + 1) * HSZ, :].astype(BF)
            qx_ref[h, 128:144, :] = bias_rows(bias_ref[:, h, :] * LOG2E, 16).astype(BF)
        wvt_ref[...] = wkv_ref[1].T
        m_ref[...] = jnp.full(m_ref.shape, NEG_FLOOR, F32)
        acc_ref[...] = jnp.zeros(acc_ref.shape, F32)

    embed_norm(mod_ref, step * blocks, x_ref, table_ref, gain_ref[...], n_ref)
    for b in range(blocks):
        mod = mod_ref[step * blocks + b]
        hot_ref[b * MBLK : (b + 1) * MBLK, :] = modality_hot(mod, (MBLK, 128), 1)
    normed = n_ref[...]
    hot = hot_ref[...]
    keys = dot(normed, wkv_ref[0]).astype(BF)
    values_t = dot_nt(wvt_ref[...], normed).astype(BF)
    ones = jnp.ones((HSZ, x_ref.shape[0]), BF)
    for h in range(heads):
        pair = (h // 2) * 128
        left = jnp.concatenate([keys[:, pair : pair + 128], hot], axis=1)
        scores = dot(left, qx_ref[h])
        old = m_ref[h]
        new = jnp.maximum(old, jnp.max(scores, axis=0, keepdims=True))
        m_ref[h] = new
        weights = jnp.exp2(scores - new).astype(BF)
        values_h = jnp.concatenate([values_t[h * HSZ : (h + 1) * HSZ, :], ones], axis=0)
        acc_ref[h] = acc_ref[h] * jnp.exp2(old - new) + dot(values_h, weights)

    @pl.when(step == pl.num_programs(0) - 1)
    def _():
        index = lax.broadcasted_iota(jnp.int32, (EXTRA, lat_count), 0)
        extra = jnp.zeros((EXTRA, lat_count), F32)
        pieces = []
        for h in range(heads):
            acc = acc_ref[h]
            total = acc[HSZ : HSZ + 1, :]
            pieces.append(acc[:HSZ, :] / total)
            for part, piece in enumerate(three_parts(m_ref[h] + jnp.log2(total))):
                extra = jnp.where(index == heads * part + h, piece, extra)
        out_ref[...] = jnp.concatenate(pieces + [extra], axis=0).T.astype(BF)


def encode(inputs, input_modality, table, gain, latents, lat_gain, wq, wkv, bias):
    points, width = inputs.shape
    heads = bias.shape[1]
    lat_count, lat_width = latents.shape
    cols = heads * HSZ
    tile = math.gcd(points, 1024)
    whole = lambda *shape: pl.BlockSpec(shape, lambda i, mod: (0,) * len(shape))
    return pl.pallas_call(
        functools.partial(encode_kernel, heads),
        grid_spec=pltpu.PrefetchScalarGridSpec(
            num_scalar_prefetch=1,
            grid=(points // tile,),
            in_specs=[
                pl.BlockSpec((tile, width), lambda i, mod: (i, 0)),
                whole(MODS, width),
                whole(1, width),
                whole(lat_count, lat_width),
                whole(1, lat_width),
                whole(lat_width, cols),
                whole(2, width, cols),
                whole(MODS, heads, lat_count),
            ],
            out_specs=whole(lat_count, cols + EXTRA),
            scratch_shapes=[
                pltpu.VMEM((heads, 256, lat_count), BF),
                pltpu.VMEM((cols, width), BF),
                pltpu.VMEM((tile, width), BF),
                pltpu.VMEM((tile, 128), BF),
                pltpu.VMEM((heads, 1, lat_count), F32),
                pltpu.VMEM((heads, 128, lat_count), F32),
            ],
        ),
        out_shape=jax.ShapeDtypeStruct((lat_count, cols + EXTRA), BF),
        compiler_params=pltpu.CompilerParams(vmem_limit_bytes=48 * MIB),
        name="encode",
    )(input_modality, inputs, table, gain, latents, lat_gain, wq, wkv, bias)


def small_call(kernel, name, outs, *args):
    return pl.pallas_call(
        kernel,
        out_shape=outs,
        in_specs=[pl.BlockSpec(memory_space=pltpu.VMEM)] * len(args),
        out_specs=jax.tree.map(lambda _: pl.BlockSpec(memory_space=pltpu.VMEM), outs),
        compiler_params=pltpu.CompilerParams(vmem_limit_bytes=24 * MIB),
        name=name,
    )(*args)


def merge_kernel(heads, part_ref, wo_ref, out_ref):
    cols = heads * HSZ
    extra = part_ref[:, :, cols:].astype(F32)
    sources, rows, _ = extra.shape
    lse = extra[:, :, :heads]
    for part in range(1, 3):
        lse = lse + extra[:, :, heads * part : heads * (part + 1)]
    top = jnp.max(lse, axis=0, keepdims=True)
    factor = jnp.exp2(lse - top)
    factor = factor / jnp.sum(factor, axis=0, keepdims=True)
    lane = lax.broadcasted_iota(jnp.int32, (sources, rows, cols), 2)
    spread = jnp.zeros((sources, rows, cols), F32)
    for h in range(heads):
        spread = jnp.where(lane // HSZ == h, factor[:, :, h : h + 1], spread)
    attended = jnp.sum(part_ref[:, :, :cols].astype(F32) * spread, axis=0)
    out_ref[...] = dot(attended.astype(BF), wo_ref[...])


def project_kernel(a_ref, b_ref, c_ref, d_ref, lat_ref, gain_ref, w_ref, lat_out, q_out, kv_out):
    lat = lat_ref[...] + ((a_ref[...] + b_ref[...]) + (c_ref[...] + d_ref[...]))
    lat_out[...] = lat
    normed = layer_norm(lat, gain_ref[...]).astype(BF)
    cols = w_ref.shape[2]
    q_out[...] = (dot(normed, w_ref[0]) * SCALE2).astype(BF)
    kv_out[:, :cols] = dot(normed, w_ref[1]).astype(BF)
    kv_out[:, cols:] = dot(normed, w_ref[2]).astype(BF)


def attend_kernel(heads, q_ref, kv_ref, bias_ref, wo_ref, out_ref):
    cols = heads * HSZ
    query = q_ref[...]
    rows = query.shape[0]
    keys = kv_ref[:, :cols]
    values = kv_ref[:, cols:]
    lane = lax.broadcasted_iota(jnp.int32, (rows, cols), 1) // HSZ
    mixed = jnp.zeros((rows, cols), F32)
    for h in range(heads):
        own = jnp.where(lane == h, query.astype(F32), 0.0).astype(BF)
        scores = dot_nt(own, keys) + bias_ref[h] * LOG2E
        weights = jnp.exp2(scores - jnp.max(scores, axis=1, keepdims=True))
        total = jnp.sum(weights, axis=1, keepdims=True)
        mixed = jnp.where(lane == h, dot(weights.astype(BF), values) / total, mixed)
    out_ref[...] = dot(mixed.astype(BF), wo_ref[...])


def mlp_kernel(a_ref, b_ref, c_ref, d_ref, lat_ref, gain_ref, w1_ref, w2_ref, lat_out, out_ref):
    lat = lat_ref[...] + ((a_ref[...] + b_ref[...]) + (c_ref[...] + d_ref[...]))
    lat_out[...] = lat
    normed = layer_norm(lat, gain_ref[...]).astype(BF)
    hidden = jax.nn.gelu(dot(normed, w1_ref[...]), approximate=True).astype(BF)
    out_ref[...] = dot(hidden, w2_ref[...])


def last_kernel(a_ref, b_ref, c_ref, d_ref, lat_ref, gain_ref, out_ref):
    lat = lat_ref[...] + ((a_ref[...] + b_ref[...]) + (c_ref[...] + d_ref[...]))
    out_ref[...] = layer_norm(lat, gain_ref[...]).astype(BF)


def query_kernel(
    heads,
    mod_ref,
    x_ref,
    table_ref,
    gain_ref,
    wq_ref,
    bias_ref,
    wo_ref,
    qt_ref,
    hot_ref,
    bias_out,
    wot_ref,
    wqt_ref,
    n_ref,
):
    step = pl.program_id(0)
    blocks = x_ref.shape[0] // MBLK

    @pl.when(step == 0)
    def _():
        wqt_ref[...] = wq_ref[...].T
        wot_ref[...] = wo_ref[...].T
        for h in range(heads):
            bias_out[h] = bias_rows(bias_ref[:, h, :] * LOG2E, 128).T.astype(BF)

    embed_norm(mod_ref, step * blocks, x_ref, table_ref, gain_ref[...], n_ref)
    for b in range(blocks):
        mod = mod_ref[step * blocks + b]
        hot_ref[:, b * MBLK : (b + 1) * MBLK] = modality_hot(mod, (128, MBLK), 0)
    qt_ref[...] = (dot_nt(wqt_ref[...], n_ref[...]) * SCALE2).astype(BF)


def prepare_queries(queries, query_modality, table, gain, wq, bias, wo):
    count, width = queries.shape
    heads, lat_count = bias.shape[1:]
    cols = heads * HSZ
    tile = math.gcd(count, 512)
    whole = lambda *shape: pl.BlockSpec(shape, lambda i, mod: (0,) * len(shape))
    return pl.pallas_call(
        functools.partial(query_kernel, heads),
        grid_spec=pltpu.PrefetchScalarGridSpec(
            num_scalar_prefetch=1,
            grid=(count // tile,),
            in_specs=[
                pl.BlockSpec((tile, width), lambda i, mod: (i, 0)),
                whole(MODS, width),
                whole(1, width),
                whole(width, cols),
                whole(MODS, heads, lat_count),
                whole(cols, width),
            ],
            out_specs=[
                pl.BlockSpec((cols, tile), lambda i, mod: (0, i)),
                pl.BlockSpec((128, tile), lambda i, mod: (0, i)),
                whole(heads, lat_count, 128),
                whole(width, cols),
            ],
            scratch_shapes=[
                pltpu.VMEM((cols, width), BF),
                pltpu.VMEM((tile, width), BF),
            ],
        ),
        out_shape=[
            jax.ShapeDtypeStruct((cols, count), BF),
            jax.ShapeDtypeStruct((128, count), BF),
            jax.ShapeDtypeStruct((heads, lat_count, 128), BF),
            jax.ShapeDtypeStruct((width, cols), BF),
        ],
        compiler_params=pltpu.CompilerParams(vmem_limit_bytes=32 * MIB),
        name="queries",
    )(query_modality, queries, table, gain, wq, bias, wo)


def decode_kernel(
    heads,
    mod_ref,
    x_ref,
    table_ref,
    lat_ref,
    wkv_ref,
    bias_ref,
    qt_ref,
    hot_ref,
    wot_ref,
    out_ref,
    kx_ref,
    vx_ref,
    mix_ref,
):
    step = pl.program_id(0)
    blocks = x_ref.shape[0] // MBLK
    lat_count = lat_ref.shape[0]

    @pl.when(step == 0)
    def _():
        normed = lat_ref[...]
        ones = jnp.ones((HSZ, lat_count), BF)
        lane = lax.broadcasted_iota(jnp.int32, (lat_count, 128), 1) // HSZ
        for pair in range(heads // 2):
            cols = slice(pair * 128, (pair + 1) * 128)
            keys = dot(normed, wkv_ref[0, :, cols])
            values = dot(normed, wkv_ref[1, :, cols]).T.astype(BF)
            for half in range(2):
                h = 2 * pair + half
                kx_ref[h, :, :128] = jnp.where(lane == half, keys, 0.0).astype(BF)
                kx_ref[h, :, 128:] = bias_ref[h]
                vx_ref[h, :HSZ, :] = values[half * HSZ : (half + 1) * HSZ, :]
                vx_ref[h, HSZ:, :] = ones

    hot = hot_ref[...]
    for h in range(heads):
        pair = (h // 2) * 128
        right = jnp.concatenate([qt_ref[pair : pair + 128, :], hot], axis=0)
        scores = dot(kx_ref[h], right)
        weights = jnp.exp2(scores - jnp.max(scores, axis=0, keepdims=True)).astype(BF)
        mixed = dot(vx_ref[h], weights)
        mix_ref[h * HSZ : (h + 1) * HSZ, :] = (mixed[:HSZ, :] / mixed[HSZ:, :]).astype(BF)
    decoded = dot(wot_ref[...], mix_ref[...]).T
    for b in range(blocks):
        rows = slice(b * MBLK, (b + 1) * MBLK)
        mod = mod_ref[step * blocks + b]
        embedded = x_ref[rows, :].astype(F32) + table_ref[pl.ds(mod, 1), :]
        out_ref[rows, :] = embedded + decoded[rows, :]


def decode(queries, query_modality, table, normed, wkv, prepared):
    queries_t, hot, bias, wo_t = prepared
    count, width = queries.shape
    heads, lat_count = bias.shape[:2]
    cols = heads * HSZ
    tile = math.gcd(count, 512)
    whole = lambda *shape: pl.BlockSpec(shape, lambda i, mod: (0,) * len(shape))
    return pl.pallas_call(
        functools.partial(decode_kernel, heads),
        grid_spec=pltpu.PrefetchScalarGridSpec(
            num_scalar_prefetch=1,
            grid=(count // tile,),
            in_specs=[
                pl.BlockSpec((tile, width), lambda i, mod: (i, 0)),
                whole(MODS, width),
                whole(lat_count, normed.shape[1]),
                whole(*wkv.shape),
                whole(heads, lat_count, 128),
                pl.BlockSpec((cols, tile), lambda i, mod: (0, i)),
                pl.BlockSpec((128, tile), lambda i, mod: (0, i)),
                whole(width, cols),
            ],
            out_specs=pl.BlockSpec((tile, width), lambda i, mod: (i, 0)),
            scratch_shapes=[
                pltpu.VMEM((heads, lat_count, 256), BF),
                pltpu.VMEM((heads, 128, lat_count), BF),
                pltpu.VMEM((cols, tile), BF),
            ],
        ),
        out_shape=jax.ShapeDtypeStruct((count, width), F32),
        compiler_params=pltpu.CompilerParams(vmem_limit_bytes=56 * MIB),
        name="decode",
    )(query_modality, queries, table, normed, wkv, bias, queries_t, hot, wo_t)


def share(rows):
    copies = jnp.broadcast_to(rows[None], (lax.axis_size("inp"),) + rows.shape)
    return lax.all_to_all(copies, "inp", 0, 0)


def head_parts(part):
    size = lax.axis_size("head")
    moved = [
        lax.ppermute(part, "head", [(i, (i + k) % size) for i in range(size)])
        for k in range(1, size)
    ]
    return [part] + moved


def body(
    inputs,
    input_modality,
    queries,
    query_modality,
    modality_embed,
    latents,
    ln_in_gain,
    ln_lat_gain,
    enc_wq,
    enc_wkv,
    enc_bias,
    enc_wo,
    self_gain,
    self_wqkv,
    self_bias,
    self_wo,
    mlp_gain,
    mlp_w1,
    mlp_w2,
    dec_gain,
    dec_wkv,
    query_gain,
    dec_wq,
    dec_bias,
    dec_wo,
):
    lat_count, width = latents.shape
    lat_rows = lat_count // lax.axis_size("inp")
    row_first = lax.axis_index("inp") * lat_rows
    heads = enc_bias.shape[1]
    cols = heads * HSZ
    row = lambda v: v.reshape(1, -1)
    shape = jax.ShapeDtypeStruct

    own = encode(
        inputs,
        input_modality,
        modality_embed,
        row(ln_in_gain),
        latents,
        row(ln_lat_gain),
        enc_wq,
        enc_wkv,
        enc_bias,
    )
    parts = lax.all_to_all(own.reshape(-1, lat_rows, own.shape[1]), "inp", 0, 0)
    enc_part = small_call(
        functools.partial(merge_kernel, heads), "merge", shape((lat_rows, width), F32), parts, enc_wo
    )
    prepared = prepare_queries(
        queries, query_modality, modality_embed, row(query_gain), dec_wq, dec_bias, dec_wo
    )
    latent_rows = lax.dynamic_slice_in_dim(latents, row_first, lat_rows, 0)
    lat_one, self_q, self_kv = small_call(
        project_kernel,
        "project",
        [
            shape((lat_rows, width), F32),
            shape((lat_rows, cols), BF),
            shape((lat_rows, 2 * cols), BF),
        ],
        *head_parts(enc_part),
        latent_rows,
        row(self_gain),
        self_wqkv,
    )
    all_kv = share(self_kv).reshape(lat_count, 2 * cols)
    self_part = small_call(
        functools.partial(attend_kernel, heads),
        "attend",
        shape((lat_rows, width), F32),
        self_q,
        all_kv,
        self_bias,
        self_wo,
    )
    lat_two, mlp_part = small_call(
        mlp_kernel,
        "mlp",
        [shape((lat_rows, width), F32), shape((lat_rows, width), F32)],
        *head_parts(self_part),
        lat_one,
        row(mlp_gain),
        mlp_w1,
        mlp_w2,
    )
    normed = small_call(
        last_kernel,
        "last",
        shape((lat_rows, width), BF),
        *head_parts(mlp_part),
        lat_two,
        row(dec_gain),
    )
    all_normed = share(normed).reshape(lat_count, width)
    return decode(queries, query_modality, modality_embed, all_normed, dec_wkv, prepared)


def solution(mesh):
    placed = (
        P("inp", None),
        P("inp"),
        P(("inp", "head"), None),
        P(("inp", "head")),
        P(),
        P(),
        P(),
        P(),
        P(None, "head"),
        P(None, None, "head"),
        P(None, "head", None),
        P("head", None),
        P(),
        P(None, None, "head"),
        P("head", "inp", None),
        P("head", None),
        P(),
        P(None, "head"),
        P("head", None),
        P(),
        P(),
        P(),
        P(),
        P(),
        P(),
    )
    return jax.shard_map(
        body, mesh=mesh, in_specs=placed, out_specs=P(("inp", "head"), None), check_vma=False
    )
```

```python
import functools
import math

import jax
import jax.numpy as jnp
from jax import lax
from jax.experimental import pallas as pl
from jax.experimental.pallas import tpu as pltpu
from jax.sharding import PartitionSpec as P

HSZ = 64
MODS = 3
MBLK = 128
EPSILON = 1e-05
LOG2E = 1.4426950408889634
SCALE2 = LOG2E / math.sqrt(HSZ)
NEG_FLOOR = -1e30
BF = jnp.bfloat16
F32 = jnp.float32
MIB = 2**20
EXTRA = 128
SMALL_TOTAL = 2.0**-95


def dot(a, b):
    return jnp.dot(a, b, preferred_element_type=F32)


def dot_nt(a, b):
    return lax.dot_general(a, b, (((1,), (1,)), ((), ())), preferred_element_type=F32)


def layer_norm(values, gain):
    centered = values - jnp.mean(values, axis=-1, keepdims=True)
    variance = jnp.mean(centered * centered, axis=-1, keepdims=True)
    return centered * lax.rsqrt(variance + EPSILON) * gain


def three_parts(values):
    high = values.astype(BF)
    rest = values - high.astype(F32)
    mid = rest.astype(BF)
    low = (rest - mid.astype(F32)).astype(BF)
    return high.astype(F32), mid.astype(F32), low.astype(F32)


def bias_rows(bias, rows):
    index = lax.broadcasted_iota(jnp.int32, (rows, bias.shape[1]), 0)
    block = jnp.zeros((rows, bias.shape[1]), F32)
    for part, piece in enumerate(three_parts(bias)):
        for mod in range(MODS):
            block = jnp.where(index == MODS * part + mod, piece[mod : mod + 1, :], block)
    return block


def modality_hot(mod, shape, dim):
    index = lax.broadcasted_iota(jnp.int32, shape, dim)
    hit = (index == mod) | (index == mod + MODS) | (index == mod + 2 * MODS)
    return hit, index


def head_sums(count, lanes):
    row = lax.broadcasted_iota(jnp.int32, (count * HSZ, lanes), 0) // HSZ
    lane = lax.broadcasted_iota(jnp.int32, (count * HSZ, lanes), 1) // (lanes // count)
    return jnp.where(row == lane, 1.0, 0.0).astype(BF)


def embed_norm(mod_ref, first, b, x_ref, table_ref, gain):
    embedded = x_ref[b * MBLK : (b + 1) * MBLK, :].astype(F32)
    embedded = embedded + table_ref[pl.ds(mod_ref[first + b], 1), :]
    return layer_norm(embedded, gain).astype(BF)


def encode_kernel(
    heads,
    mod_ref,
    x_ref,
    next_ref,
    table_ref,
    gain_ref,
    lat_ref,
    lat_gain_ref,
    wq_ref,
    wkv_ref,
    bias_ref,
    out_ref,
    qx_ref,
    norm_ref,
    wvt_ref,
    n_ref,
    hot_ref,
    k_ref,
    vt_ref,
    p_ref,
    part_ref,
    shift_ref,
    m_ref,
    acc_ref,
):
    step = pl.program_id(0)
    last = pl.num_programs(0) - 1
    points = x_ref.shape[0]
    blocks = points // MBLK
    lat_count = lat_ref.shape[0]
    slot = lax.rem(step, 2)
    row16 = lax.broadcasted_iota(jnp.int32, (16, lat_count), 0)
    gain = gain_ref[...]

    def project(at, into):
        normed = n_ref[...]
        keys = dot(normed, wkv_ref[0])
        k_ref[into] = keys.astype(BF)
        vt_ref[into] = dot_nt(wvt_ref[...], normed).astype(BF)
        lengths = dot((keys * keys).astype(BF), head_sums(heads, 128))
        longest = jnp.sqrt(jnp.max(lengths, axis=0, keepdims=True))
        present = [jnp.bool_(False)] * MODS
        for b in range(blocks):
            mod = mod_ref[at * blocks + b]
            hit, index = modality_hot(mod, (MBLK, 128), 1)
            hit = jnp.where(hit | (index == 16), 1.0, 0.0)
            hot_ref[into, b * MBLK : (b + 1) * MBLK, :] = hit.astype(BF)
            present = [p | (mod == m) for m, p in enumerate(present)]
        for h in range(heads):
            bound = jnp.full((1, lat_count), NEG_FLOOR, F32)
            for m in range(MODS):
                held = jnp.where(present[m], bias_ref[m, h : h + 1, :] * LOG2E, NEG_FLOOR)
                bound = jnp.maximum(bound, held)
            lane = h * (128 // heads)
            bound = bound + norm_ref[h : h + 1, :] * longest[:, lane : lane + 1]
            shift_ref[into, h] = bound.astype(BF).astype(F32)

    @pl.when(step == 0)
    def _():
        normed = layer_norm(lat_ref[...], lat_gain_ref[...]).astype(BF)
        query = (dot(normed, wq_ref[...]) * SCALE2).T
        qx_ref[...] = jnp.zeros(qx_ref.shape, BF)
        for h in range(heads):
            half = (h % 2) * HSZ
            own = query[h * HSZ : (h + 1) * HSZ, :]
            qx_ref[h, half : half + HSZ, :] = own.astype(BF)
            qx_ref[h, 128:144, :] = bias_rows(bias_ref[:, h, :] * LOG2E, 16).astype(BF)
            norm_ref[h : h + 1, :] = jnp.sqrt(jnp.sum(own * own, axis=0, keepdims=True))
        wvt_ref[...] = wkv_ref[1].T
        m_ref[...] = jnp.full(m_ref.shape, NEG_FLOOR, F32)
        acc_ref[...] = jnp.zeros(acc_ref.shape, F32)
        for b in range(blocks):
            n_ref[b * MBLK : (b + 1) * MBLK, :] = embed_norm(
                mod_ref, 0, b, x_ref, table_ref, gain
            )
        project(0, 0)

    following = jnp.minimum(step + 1, last)
    hot = hot_ref[slot]
    ones = jnp.ones((HSZ, points), BF)
    for h in range(heads):
        qx_ref[h, 144:160, :] = jnp.where(row16 == 0, -shift_ref[slot, h], 0.0).astype(BF)
    per_head = -(-blocks // heads)
    for h in range(heads + 1):
        if h < heads:
            pair = (h // 2) * 128
            left = jnp.concatenate([k_ref[slot, :, pair : pair + 128], hot], axis=1)
            p_ref[h % 2] = jnp.exp2(dot(left, qx_ref[h])).astype(BF)
        if h > 0:
            values_h = vt_ref[slot, (h - 1) * HSZ : h * HSZ, :]
            values_h = jnp.concatenate([values_h, ones], axis=0)
            part_ref[h - 1] = dot(values_h, p_ref[(h - 1) % 2])
        for b in range(h * per_head, min((h + 1) * per_head, blocks)):
            n_ref[b * MBLK : (b + 1) * MBLK, :] = embed_norm(
                mod_ref, following * blocks, b, next_ref, table_ref, gain
            )
    project(following, 1 - slot)
    least = jnp.min(part_ref[:, HSZ : HSZ + 1, :])

    @pl.when(least < SMALL_TOTAL)
    def _():
        def exact(h, _):
            pair = pl.multiple_of((h // 2) * 128, 128)
            qx_ref[h, 144:160, :] = jnp.zeros((16, lat_count), BF)
            left = jnp.concatenate([k_ref[slot, :, pl.ds(pair, 128)], hot_ref[slot]], axis=1)
            scores = dot(left, qx_ref[h])
            top = jnp.max(scores, axis=0, keepdims=True)
            weights = jnp.exp2(scores - top).astype(BF)
            values_h = vt_ref[slot, pl.ds(pl.multiple_of(h * HSZ, HSZ), HSZ), :]
            values_h = jnp.concatenate([values_h, jnp.ones((HSZ, points), BF)], axis=0)
            part_ref[h] = dot(values_h, weights)
            shift_ref[slot, h] = top
            return 0

        lax.fori_loop(0, heads, exact, 0)

    for h in range(heads):
        old = m_ref[h]
        own = shift_ref[slot, h]
        new = jnp.maximum(old, own)
        m_ref[h] = new
        acc_ref[h] = acc_ref[h] * jnp.exp2(old - new) + part_ref[h] * jnp.exp2(own - new)

    @pl.when(step == last)
    def _():
        index = lax.broadcasted_iota(jnp.int32, (EXTRA, lat_count), 0)
        extra = jnp.zeros((EXTRA, lat_count), F32)
        pieces = []
        for h in range(heads):
            acc = acc_ref[h]
            total = acc[HSZ : HSZ + 1, :]
            pieces.append(acc[:HSZ, :] / total)
            for part, piece in enumerate(three_parts(m_ref[h] + jnp.log2(total))):
                extra = jnp.where(index == heads * part + h, piece, extra)
        out_ref[...] = jnp.concatenate(pieces + [extra], axis=0).T.astype(BF)


def encode(inputs, input_modality, table, gain, latents, lat_gain, wq, wkv, bias):
    points, width = inputs.shape
    heads = bias.shape[1]
    lat_count, lat_width = latents.shape
    cols = heads * HSZ
    tile = math.gcd(points, 1024)
    steps = points // tile
    whole = lambda *shape: pl.BlockSpec(shape, lambda i, mod: (0,) * len(shape))
    return pl.pallas_call(
        functools.partial(encode_kernel, heads),
        grid_spec=pltpu.PrefetchScalarGridSpec(
            num_scalar_prefetch=1,
            grid=(steps,),
            in_specs=[
                pl.BlockSpec((tile, width), lambda i, mod: (0, 0)),
                pl.BlockSpec((tile, width), lambda i, mod: (jnp.minimum(i + 1, steps - 1), 0)),
                whole(MODS, width),
                whole(1, width),
                whole(lat_count, lat_width),
                whole(1, lat_width),
                whole(lat_width, cols),
                whole(2, width, cols),
                whole(MODS, heads, lat_count),
            ],
            out_specs=whole(lat_count, cols + EXTRA),
            scratch_shapes=[
                pltpu.VMEM((heads, 256, lat_count), BF),
                pltpu.VMEM((heads, lat_count), F32),
                pltpu.VMEM((cols, width), BF),
                pltpu.VMEM((tile, width), BF),
                pltpu.VMEM((2, tile, 128), BF),
                pltpu.VMEM((2, tile, cols), BF),
                pltpu.VMEM((2, cols, tile), BF),
                pltpu.VMEM((2, tile, lat_count), BF),
                pltpu.VMEM((heads, 128, lat_count), F32),
                pltpu.VMEM((2, heads, 1, lat_count), F32),
                pltpu.VMEM((heads, 1, lat_count), F32),
                pltpu.VMEM((heads, 128, lat_count), F32),
            ],
        ),
        out_shape=jax.ShapeDtypeStruct((lat_count, cols + EXTRA), BF),
        compiler_params=pltpu.CompilerParams(vmem_limit_bytes=58 * MIB),
        name="encode",
    )(input_modality, inputs, inputs, table, gain, latents, lat_gain, wq, wkv, bias)


def small_call(kernel, name, outs, *args):
    return pl.pallas_call(
        kernel,
        out_shape=outs,
        in_specs=[pl.BlockSpec(memory_space=pltpu.VMEM)] * len(args),
        out_specs=jax.tree.map(lambda _: pl.BlockSpec(memory_space=pltpu.VMEM), outs),
        compiler_params=pltpu.CompilerParams(vmem_limit_bytes=24 * MIB),
        name=name,
    )(*args)


def merge_kernel(heads, part_ref, wo_ref, out_ref):
    cols = heads * HSZ
    extra = part_ref[:, :, cols:].astype(F32)
    sources, rows, _ = extra.shape
    lse = extra[:, :, :heads]
    for part in range(1, 3):
        lse = lse + extra[:, :, heads * part : heads * (part + 1)]
    top = jnp.max(lse, axis=0, keepdims=True)
    factor = jnp.exp2(lse - top)
    factor = factor / jnp.sum(factor, axis=0, keepdims=True)
    lane = lax.broadcasted_iota(jnp.int32, (sources, rows, cols), 2)
    spread = jnp.zeros((sources, rows, cols), F32)
    for h in range(heads):
        spread = jnp.where(lane // HSZ == h, factor[:, :, h : h + 1], spread)
    attended = jnp.sum(part_ref[:, :, :cols].astype(F32) * spread, axis=0)
    out_ref[...] = dot(attended.astype(BF), wo_ref[...])


def project_kernel(a_ref, b_ref, c_ref, d_ref, lat_ref, gain_ref, w_ref, lat_out, q_out, kv_out):
    lat = lat_ref[...] + ((a_ref[...] + b_ref[...]) + (c_ref[...] + d_ref[...]))
    lat_out[...] = lat
    normed = layer_norm(lat, gain_ref[...]).astype(BF)
    cols = w_ref.shape[2]
    q_out[...] = (dot(normed, w_ref[0]) * SCALE2).astype(BF)
    kv_out[:, :cols] = dot(normed, w_ref[1]).astype(BF)
    kv_out[:, cols:] = dot(normed, w_ref[2]).astype(BF)


def attend_kernel(heads, q_ref, kv_ref, bias_ref, wo_ref, out_ref):
    cols = heads * HSZ
    query = q_ref[...]
    rows = query.shape[0]
    keys = kv_ref[:, :cols]
    values = kv_ref[:, cols:]
    lane = lax.broadcasted_iota(jnp.int32, (rows, cols), 1) // HSZ
    mixed = jnp.zeros((rows, cols), F32)
    for h in range(heads):
        own = jnp.where(lane == h, query.astype(F32), 0.0).astype(BF)
        scores = dot_nt(own, keys) + bias_ref[h] * LOG2E
        weights = jnp.exp2(scores - jnp.max(scores, axis=1, keepdims=True))
        total = jnp.sum(weights, axis=1, keepdims=True)
        mixed = jnp.where(lane == h, dot(weights.astype(BF), values) / total, mixed)
    out_ref[...] = dot(mixed.astype(BF), wo_ref[...])


def mlp_kernel(a_ref, b_ref, c_ref, d_ref, lat_ref, gain_ref, w1_ref, w2_ref, lat_out, out_ref):
    lat = lat_ref[...] + ((a_ref[...] + b_ref[...]) + (c_ref[...] + d_ref[...]))
    lat_out[...] = lat
    normed = layer_norm(lat, gain_ref[...]).astype(BF)
    hidden = jax.nn.gelu(dot(normed, w1_ref[...]), approximate=True).astype(BF)
    out_ref[...] = dot(hidden, w2_ref[...])


def last_kernel(a_ref, b_ref, c_ref, d_ref, lat_ref, gain_ref, out_ref):
    lat = lat_ref[...] + ((a_ref[...] + b_ref[...]) + (c_ref[...] + d_ref[...]))
    out_ref[...] = layer_norm(lat, gain_ref[...]).astype(BF)


def query_kernel(
    heads,
    mod_ref,
    x_ref,
    table_ref,
    gain_ref,
    wq_ref,
    bias_ref,
    wo_ref,
    qt_ref,
    hot_ref,
    norm_ref,
    top_ref,
    bias_out,
    wot_ref,
    wqt_ref,
    bmax_ref,
    n_ref,
):
    step = pl.program_id(0)
    blocks = x_ref.shape[0] // MBLK
    lat_count = bias_ref.shape[2]

    @pl.when(step == 0)
    def _():
        wqt_ref[...] = wq_ref[...].T
        wot_ref[...] = wo_ref[...].T
        lane = lax.broadcasted_iota(jnp.int32, (lat_count, 128), 1)
        for h in range(heads):
            columns = bias_rows(bias_ref[:, h, :] * LOG2E, 128).T
            bias_out[h] = jnp.where(lane == 16 + h, 1.0, columns).astype(BF)
        for m in range(MODS):
            top = jnp.max(bias_ref[m] * LOG2E, axis=1, keepdims=True)
            bmax_ref[m] = jnp.broadcast_to(top, (heads, MBLK))

    for b in range(blocks):
        n_ref[b * MBLK : (b + 1) * MBLK, :] = embed_norm(
            mod_ref, step * blocks, b, x_ref, table_ref, gain_ref[...]
        )
        mod = mod_ref[step * blocks + b]
        hit, _ = modality_hot(mod, (16, MBLK), 0)
        hot_ref[:, b * MBLK : (b + 1) * MBLK] = jnp.where(hit, 1.0, 0.0).astype(BF)
        top_ref[:, b * MBLK : (b + 1) * MBLK] = bmax_ref[mod]
    query = dot_nt(wqt_ref[...], n_ref[...]) * SCALE2
    qt_ref[...] = query.astype(BF)
    for h in range(heads):
        own = query[h * HSZ : (h + 1) * HSZ, :]
        norm_ref[h : h + 1, :] = jnp.sqrt(jnp.sum(own * own, axis=0, keepdims=True))


def prepare_queries(queries, query_modality, table, gain, wq, bias, wo):
    count, width = queries.shape
    heads, lat_count = bias.shape[1:]
    cols = heads * HSZ
    tile = math.gcd(count, 512)
    whole = lambda *shape: pl.BlockSpec(shape, lambda i, mod: (0,) * len(shape))
    tiled = lambda rows: pl.BlockSpec((rows, tile), lambda i, mod: (0, i))
    return pl.pallas_call(
        functools.partial(query_kernel, heads),
        grid_spec=pltpu.PrefetchScalarGridSpec(
            num_scalar_prefetch=1,
            grid=(count // tile,),
            in_specs=[
                pl.BlockSpec((tile, width), lambda i, mod: (i, 0)),
                whole(MODS, width),
                whole(1, width),
                whole(width, cols),
                whole(MODS, heads, lat_count),
                whole(cols, width),
            ],
            out_specs=[
                tiled(cols),
                tiled(16),
                tiled(heads),
                tiled(heads),
                whole(heads, lat_count, 128),
                whole(width, cols),
            ],
            scratch_shapes=[
                pltpu.VMEM((cols, width), BF),
                pltpu.VMEM((MODS, heads, MBLK), F32),
                pltpu.VMEM((tile, width), BF),
            ],
        ),
        out_shape=[
            jax.ShapeDtypeStruct((cols, count), BF),
            jax.ShapeDtypeStruct((16, count), BF),
            jax.ShapeDtypeStruct((heads, count), F32),
            jax.ShapeDtypeStruct((heads, count), F32),
            jax.ShapeDtypeStruct((heads, lat_count, 128), BF),
            jax.ShapeDtypeStruct((width, cols), BF),
        ],
        compiler_params=pltpu.CompilerParams(vmem_limit_bytes=28 * MIB),
        name="queries",
    )(query_modality, queries, table, gain, wq, bias, wo)


def decode_kernel(
    heads,
    mod_ref,
    x_ref,
    table_ref,
    lat_ref,
    wkv_ref,
    bias_ref,
    qt_ref,
    onehot_ref,
    norm_ref,
    top_ref,
    wot_ref,
    out_ref,
    kx_ref,
    vx_ref,
    long_ref,
    hot_ref,
    p_ref,
    mix_ref,
):
    step = pl.program_id(0)
    tile = x_ref.shape[0]
    blocks = tile // MBLK
    lat_count = lat_ref.shape[0]

    @pl.when(step == 0)
    def _():
        normed = lat_ref[...]
        ones = jnp.ones((HSZ, lat_count), BF)
        lane = lax.broadcasted_iota(jnp.int32, (lat_count, 128), 1) // HSZ
        sums = head_sums(2, 128)
        for pair in range(heads // 2):
            cols = slice(pair * 128, (pair + 1) * 128)
            keys = dot(normed, wkv_ref[0, :, cols])
            values = dot(normed, wkv_ref[1, :, cols]).astype(BF).T
            lengths = dot((keys * keys).astype(BF), sums)
            longest = jnp.sqrt(jnp.max(lengths, axis=0, keepdims=True))
            for half in range(2):
                h = 2 * pair + half
                kx_ref[h, :, :128] = jnp.where(lane == half, keys, 0.0).astype(BF)
                kx_ref[h, :, 128:] = bias_ref[h]
                vx_ref[h, :HSZ, :] = values[half * HSZ : (half + 1) * HSZ, :]
                vx_ref[h, HSZ:, :] = ones
                long_ref[h : h + 1, :] = jnp.broadcast_to(
                    longest[:, half * HSZ : half * HSZ + 1], (1, 128)
                )
        hot_ref[...] = jnp.zeros(hot_ref.shape, BF)

    bound = norm_ref[...] * long_ref[:, :1] + top_ref[...]
    hot_ref[:16, :] = onehot_ref[...]
    hot_ref[16 : 16 + heads, :] = (-bound).astype(BF)
    hot = hot_ref[...]
    least = jnp.full((1, tile), 1.0, F32)
    for h in range(heads + 1):
        if h < heads:
            pair = (h // 2) * 128
            right = jnp.concatenate([qt_ref[pair : pair + 128, :], hot], axis=0)
            p_ref[h % 2] = jnp.exp2(dot(kx_ref[h], right)).astype(BF)
        if h > 0:
            mixed = dot(vx_ref[h - 1], p_ref[(h - 1) % 2])
            least = jnp.minimum(least, mixed[HSZ : HSZ + 1, :])
            mix_ref[(h - 1) * HSZ : h * HSZ, :] = (mixed[:HSZ, :] / mixed[HSZ:, :]).astype(BF)

    @pl.when(jnp.min(least) < SMALL_TOTAL)
    def _():
        hot_ref[16 : 16 + heads, :] = jnp.zeros((heads, tile), BF)

        def exact(h, _):
            pair = pl.multiple_of((h // 2) * 128, 128)
            right = jnp.concatenate([qt_ref[pl.ds(pair, 128), :], hot_ref[...]], axis=0)
            scores = dot(kx_ref[h], right)
            top = jnp.max(scores, axis=0, keepdims=True)
            mixed = dot(vx_ref[h], jnp.exp2(scores - top).astype(BF))
            mixed = (mixed[:HSZ, :] / mixed[HSZ:, :]).astype(BF)
            mix_ref[pl.ds(pl.multiple_of(h * HSZ, HSZ), HSZ), :] = mixed
            return 0

        lax.fori_loop(0, heads, exact, 0)

    decoded = dot(wot_ref[...], mix_ref[...]).T
    for b in range(blocks):
        rows = slice(b * MBLK, (b + 1) * MBLK)
        mod = mod_ref[step * blocks + b]
        embedded = x_ref[rows, :].astype(F32) + table_ref[pl.ds(mod, 1), :]
        out_ref[rows, :] = embedded + decoded[rows, :]


def decode(queries, query_modality, table, normed, wkv, prepared):
    queries_t, hot, norms, tops, bias, wo_t = prepared
    count, width = queries.shape
    heads, lat_count = bias.shape[:2]
    cols = heads * HSZ
    tile = math.gcd(count, 512)
    held = pl.BlockSpec(memory_space=pltpu.VMEM)
    tiled = lambda rows: pl.BlockSpec((rows, tile), lambda i, mod: (0, i))
    return pl.pallas_call(
        functools.partial(decode_kernel, heads),
        grid_spec=pltpu.PrefetchScalarGridSpec(
            num_scalar_prefetch=1,
            grid=(count // tile,),
            in_specs=[
                pl.BlockSpec((tile, width), lambda i, mod: (i, 0)),
                held,
                held,
                held,
                held,
                tiled(cols),
                tiled(16),
                tiled(heads),
                tiled(heads),
                held,
            ],
            out_specs=pl.BlockSpec((tile, width), lambda i, mod: (i, 0)),
            scratch_shapes=[
                pltpu.VMEM((heads, lat_count, 256), BF),
                pltpu.VMEM((heads, 128, lat_count), BF),
                pltpu.VMEM((heads, 128), F32),
                pltpu.VMEM((128, tile), BF),
                pltpu.VMEM((2, lat_count, tile), BF),
                pltpu.VMEM((cols, tile), BF),
            ],
        ),
        out_shape=jax.ShapeDtypeStruct((count, width), F32),
        compiler_params=pltpu.CompilerParams(vmem_limit_bytes=32 * MIB),
        name="decode",
    )(query_modality, queries, table, normed, wkv, bias, queries_t, hot, norms, tops, wo_t)


def share(rows):
    copies = jnp.broadcast_to(rows[None], (lax.axis_size("inp"),) + rows.shape)
    return lax.all_to_all(copies, "inp", 0, 0)


def head_parts(part):
    size = lax.axis_size("head")
    moved = [
        lax.ppermute(part, "head", [(i, (i + k) % size) for i in range(size)])
        for k in range(1, size)
    ]
    return [part] + moved


def body(
    inputs,
    input_modality,
    queries,
    query_modality,
    modality_embed,
    latents,
    ln_in_gain,
    ln_lat_gain,
    enc_wq,
    enc_wkv,
    enc_bias,
    enc_wo,
    self_gain,
    self_wqkv,
    self_bias,
    self_wo,
    mlp_gain,
    mlp_w1,
    mlp_w2,
    dec_gain,
    dec_wkv,
    query_gain,
    dec_wq,
    dec_bias,
    dec_wo,
):
    lat_count, width = latents.shape
    lat_rows = lat_count // lax.axis_size("inp")
    row_first = lax.axis_index("inp") * lat_rows
    heads = enc_bias.shape[1]
    cols = heads * HSZ
    row = lambda v: v.reshape(1, -1)
    shape = jax.ShapeDtypeStruct

    own = encode(
        inputs,
        input_modality,
        modality_embed,
        row(ln_in_gain),
        latents,
        row(ln_lat_gain),
        enc_wq,
        enc_wkv,
        enc_bias,
    )
    parts = lax.all_to_all(own.reshape(-1, lat_rows, own.shape[1]), "inp", 0, 0)
    enc_part = small_call(
        functools.partial(merge_kernel, heads), "merge", shape((lat_rows, width), F32), parts, enc_wo
    )
    prepared = prepare_queries(
        queries, query_modality, modality_embed, row(query_gain), dec_wq, dec_bias, dec_wo
    )
    latent_rows = lax.dynamic_slice_in_dim(latents, row_first, lat_rows, 0)
    lat_one, self_q, self_kv = small_call(
        project_kernel,
        "project",
        [
            shape((lat_rows, width), F32),
            shape((lat_rows, cols), BF),
            shape((lat_rows, 2 * cols), BF),
        ],
        *head_parts(enc_part),
        latent_rows,
        row(self_gain),
        self_wqkv,
    )
    all_kv = share(self_kv).reshape(lat_count, 2 * cols)
    self_part = small_call(
        functools.partial(attend_kernel, heads),
        "attend",
        shape((lat_rows, width), F32),
        self_q,
        all_kv,
        self_bias,
        self_wo,
    )
    lat_two, mlp_part = small_call(
        mlp_kernel,
        "mlp",
        [shape((lat_rows, width), F32), shape((lat_rows, width), F32)],
        *head_parts(self_part),
        lat_one,
        row(mlp_gain),
        mlp_w1,
        mlp_w2,
    )
    normed = small_call(
        last_kernel,
        "last",
        shape((lat_rows, width), BF),
        *head_parts(mlp_part),
        lat_two,
        row(dec_gain),
    )
    all_normed = share(normed).reshape(lat_count, width)
    return decode(queries, query_modality, modality_embed, all_normed, dec_wkv, prepared)


def solution(mesh):
    placed = (
        P("inp", None),
        P("inp"),
        P(("inp", "head"), None),
        P(("inp", "head")),
        P(),
        P(),
        P(),
        P(),
        P(None, "head"),
        P(None, None, "head"),
        P(None, "head", None),
        P("head", None),
        P(),
        P(None, None, "head"),
        P("head", "inp", None),
        P("head", None),
        P(),
        P(None, "head"),
        P("head", None),
        P(),
        P(),
        P(),
        P(),
        P(),
        P(),
    )
    return jax.shard_map(
        body, mesh=mesh, in_specs=placed, out_specs=P(("inp", "head"), None), check_vma=False
    )
```

```python
import functools
import math

import jax
import jax.numpy as jnp
from jax import lax
from jax.experimental import pallas as pl
from jax.experimental.pallas import tpu as pltpu
from jax.sharding import PartitionSpec as P

HSZ = 64
MODS = 3
MBLK = 128
EPSILON = 1e-05
LOG2E = 1.4426950408889634
SCALE2 = LOG2E / math.sqrt(HSZ)
NEG_FLOOR = -1e30
BF = jnp.bfloat16
F32 = jnp.float32
MIB = 2**20
EXTRA = 128
SMALL_TOTAL = 2.0**-95


def dot(a, b):
    return jnp.dot(a, b, preferred_element_type=F32)


def dot_nt(a, b):
    return lax.dot_general(a, b, (((1,), (1,)), ((), ())), preferred_element_type=F32)


def layer_norm(values, gain):
    centered = values - jnp.mean(values, axis=-1, keepdims=True)
    variance = jnp.mean(centered * centered, axis=-1, keepdims=True)
    return centered * lax.rsqrt(variance + EPSILON) * gain


def three_parts(values):
    high = values.astype(BF)
    rest = values - high.astype(F32)
    mid = rest.astype(BF)
    low = (rest - mid.astype(F32)).astype(BF)
    return high.astype(F32), mid.astype(F32), low.astype(F32)


def bias_rows(bias, rows):
    index = lax.broadcasted_iota(jnp.int32, (rows, bias.shape[1]), 0)
    block = jnp.zeros((rows, bias.shape[1]), F32)
    for part, piece in enumerate(three_parts(bias)):
        for mod in range(MODS):
            block = jnp.where(index == MODS * part + mod, piece[mod : mod + 1, :], block)
    return block


def modality_hot(mod, shape, dim):
    index = lax.broadcasted_iota(jnp.int32, shape, dim)
    hit = (index == mod) | (index == mod + MODS) | (index == mod + 2 * MODS)
    return hit, index


def head_sums(count, lanes):
    row = lax.broadcasted_iota(jnp.int32, (count * HSZ, lanes), 0) // HSZ
    lane = lax.broadcasted_iota(jnp.int32, (count * HSZ, lanes), 1) // (lanes // count)
    return jnp.where(row == lane, 1.0, 0.0).astype(BF)


def embed_norm(mod_ref, first, b, x_ref, table_ref, gain):
    embedded = x_ref[b * MBLK : (b + 1) * MBLK, :].astype(F32)
    embedded = embedded + table_ref[pl.ds(mod_ref[first + b], 1), :]
    return layer_norm(embedded, gain).astype(BF)


def part_rows(core, all_ref, own_ref, other_ref):
    for held, refs in enumerate(((own_ref, other_ref), (other_ref, own_ref))):

        @pl.when(core == held)
        def _():
            for block in range(all_ref.shape[0] // 16):
                rows = slice(block // 2 * 16, block // 2 * 16 + 16)
                refs[block % 2][rows, :] = all_ref[block * 16 : block * 16 + 16, :]


def join_rows(core, own_ref, other_ref, all_ref):
    for held, refs in enumerate(((own_ref, other_ref), (other_ref, own_ref))):

        @pl.when(core == held)
        def _():
            for block in range(all_ref.shape[0] // 16):
                all_ref[block * 16 : block * 16 + 16, :] = refs[block % 2][block // 2]


def encode_kernel(
    heads,
    mod_ref,
    core_ref,
    x_ref,
    next_ref,
    table_ref,
    gain_ref,
    lat_ref,
    lat_gain_ref,
    wq_ref,
    wkv_ref,
    bias_ref,
    keep_ref,
    send_ref,
    qx_ref,
    norm_ref,
    wvt_ref,
    n_ref,
    hot_ref,
    k_ref,
    vt_ref,
    p_ref,
    part_ref,
    shift_ref,
    m_ref,
    acc_ref,
    out_ref,
):
    step = pl.program_id(0)
    last = pl.num_programs(0) - 1
    points = x_ref.shape[0]
    blocks = points // MBLK
    lat_count = lat_ref.shape[0]
    slot = lax.rem(step, 2)
    row16 = lax.broadcasted_iota(jnp.int32, (16, lat_count), 0)
    gain = gain_ref[...]

    def project(at, into):
        normed = n_ref[...]
        keys = dot(normed, wkv_ref[0])
        k_ref[into] = keys.astype(BF)
        vt_ref[into] = dot_nt(wvt_ref[...], normed).astype(BF)
        lengths = dot((keys * keys).astype(BF), head_sums(heads, 128))
        longest = jnp.sqrt(jnp.max(lengths, axis=0, keepdims=True))
        present = [jnp.bool_(False)] * MODS
        for b in range(blocks):
            mod = mod_ref[at * blocks + b]
            hit, index = modality_hot(mod, (MBLK, 128), 1)
            hit = jnp.where(hit | (index == 16), 1.0, 0.0)
            hot_ref[into, b * MBLK : (b + 1) * MBLK, :] = hit.astype(BF)
            present = [p | (mod == m) for m, p in enumerate(present)]
        for h in range(heads):
            bound = jnp.full((1, lat_count), NEG_FLOOR, F32)
            for m in range(MODS):
                held = jnp.where(present[m], bias_ref[m, h : h + 1, :] * LOG2E, NEG_FLOOR)
                bound = jnp.maximum(bound, held)
            lane = h * (128 // heads)
            bound = bound + norm_ref[h : h + 1, :] * longest[:, lane : lane + 1]
            shift_ref[into, h] = bound.astype(BF).astype(F32)

    @pl.when(step == 0)
    def _():
        normed = layer_norm(lat_ref[...], lat_gain_ref[...]).astype(BF)
        query = (dot(normed, wq_ref[...]) * SCALE2).T
        qx_ref[...] = jnp.zeros(qx_ref.shape, BF)
        for h in range(heads):
            half = (h % 2) * HSZ
            own = query[h * HSZ : (h + 1) * HSZ, :]
            qx_ref[h, half : half + HSZ, :] = own.astype(BF)
            qx_ref[h, 128:144, :] = bias_rows(bias_ref[:, h, :] * LOG2E, 16).astype(BF)
            norm_ref[h : h + 1, :] = jnp.sqrt(jnp.sum(own * own, axis=0, keepdims=True))
        wvt_ref[...] = wkv_ref[1].T
        m_ref[...] = jnp.full(m_ref.shape, NEG_FLOOR, F32)
        acc_ref[...] = jnp.zeros(acc_ref.shape, F32)
        for b in range(blocks):
            n_ref[b * MBLK : (b + 1) * MBLK, :] = embed_norm(
                mod_ref, 0, b, x_ref, table_ref, gain
            )
        project(0, 0)

    following = jnp.minimum(step + 1, last)
    hot = hot_ref[slot]
    ones = jnp.ones((HSZ, points), BF)
    for h in range(heads):
        qx_ref[h, 144:160, :] = jnp.where(row16 == 0, -shift_ref[slot, h], 0.0).astype(BF)
    per_head = -(-blocks // heads)
    for h in range(heads + 1):
        if h < heads:
            pair = (h // 2) * 128
            left = jnp.concatenate([k_ref[slot, :, pair : pair + 128], hot], axis=1)
            p_ref[h % 2] = jnp.exp2(dot(left, qx_ref[h])).astype(BF)
        if h > 0:
            values_h = vt_ref[slot, (h - 1) * HSZ : h * HSZ, :]
            values_h = jnp.concatenate([values_h, ones], axis=0)
            part_ref[h - 1] = dot(values_h, p_ref[(h - 1) % 2])
        for b in range(h * per_head, min((h + 1) * per_head, blocks)):
            n_ref[b * MBLK : (b + 1) * MBLK, :] = embed_norm(
                mod_ref, following * blocks, b, next_ref, table_ref, gain
            )
    project(following, 1 - slot)
    least = jnp.min(part_ref[:, HSZ : HSZ + 1, :])

    @pl.when(least < SMALL_TOTAL)
    def _():
        def exact(h, _):
            pair = pl.multiple_of((h // 2) * 128, 128)
            qx_ref[h, 144:160, :] = jnp.zeros((16, lat_count), BF)
            left = jnp.concatenate([k_ref[slot, :, pl.ds(pair, 128)], hot_ref[slot]], axis=1)
            scores = dot(left, qx_ref[h])
            top = jnp.max(scores, axis=0, keepdims=True)
            weights = jnp.exp2(scores - top).astype(BF)
            values_h = vt_ref[slot, pl.ds(pl.multiple_of(h * HSZ, HSZ), HSZ), :]
            values_h = jnp.concatenate([values_h, jnp.ones((HSZ, points), BF)], axis=0)
            part_ref[h] = dot(values_h, weights)
            shift_ref[slot, h] = top
            return 0

        lax.fori_loop(0, heads, exact, 0)

    for h in range(heads):
        old = m_ref[h]
        own = shift_ref[slot, h]
        new = jnp.maximum(old, own)
        m_ref[h] = new
        acc_ref[h] = acc_ref[h] * jnp.exp2(old - new) + part_ref[h] * jnp.exp2(own - new)

    @pl.when(step == last)
    def _():
        index = lax.broadcasted_iota(jnp.int32, (EXTRA, lat_count), 0)
        extra = jnp.zeros((EXTRA, lat_count), F32)
        pieces = []
        for h in range(heads):
            acc = acc_ref[h]
            total = acc[HSZ : HSZ + 1, :]
            pieces.append(acc[:HSZ, :] / total)
            for part, piece in enumerate(three_parts(m_ref[h] + jnp.log2(total))):
                extra = jnp.where(index == heads * part + h, piece, extra)
        out_ref[...] = jnp.concatenate(pieces + [extra], axis=0).T.astype(BF)
        part_rows(core_ref[0], out_ref, keep_ref, send_ref)


def encode(core, inputs, input_modality, table, gain, latents, lat_gain, wq, wkv, bias):
    points, width = inputs.shape
    heads = bias.shape[1]
    lat_count, lat_width = latents.shape
    cols = heads * HSZ
    tile = math.gcd(points, 1024)
    steps = points // tile
    whole = lambda *shape: pl.BlockSpec(shape, lambda i, *_: (0,) * len(shape))
    return pl.pallas_call(
        functools.partial(encode_kernel, heads),
        grid_spec=pltpu.PrefetchScalarGridSpec(
            num_scalar_prefetch=2,
            grid=(steps,),
            in_specs=[
                pl.BlockSpec((tile, width), lambda i, *_: (0, 0)),
                pl.BlockSpec((tile, width), lambda i, *_: (jnp.minimum(i + 1, steps - 1), 0)),
                whole(MODS, width),
                whole(1, width),
                whole(lat_count, lat_width),
                whole(1, lat_width),
                whole(lat_width, cols),
                whole(2, width, cols),
                whole(MODS, heads, lat_count),
            ],
            out_specs=[whole(lat_count // 2, cols + EXTRA)] * 2,
            scratch_shapes=[
                pltpu.VMEM((heads, 256, lat_count), BF),
                pltpu.VMEM((heads, lat_count), F32),
                pltpu.VMEM((cols, width), BF),
                pltpu.VMEM((tile, width), BF),
                pltpu.VMEM((2, tile, 128), BF),
                pltpu.VMEM((2, tile, cols), BF),
                pltpu.VMEM((2, cols, tile), BF),
                pltpu.VMEM((2, tile, lat_count), BF),
                pltpu.VMEM((heads, 128, lat_count), F32),
                pltpu.VMEM((2, heads, 1, lat_count), F32),
                pltpu.VMEM((heads, 1, lat_count), F32),
                pltpu.VMEM((heads, 128, lat_count), F32),
                pltpu.VMEM((lat_count, cols + EXTRA), BF),
            ],
        ),
        out_shape=[jax.ShapeDtypeStruct((lat_count // 2, cols + EXTRA), BF)] * 2,
        compiler_params=pltpu.CompilerParams(vmem_limit_bytes=58 * MIB),
        name="encode",
    )(input_modality, core, inputs, inputs, table, gain, latents, lat_gain, wq, wkv, bias)


def small_call(kernel, name, outs, *args, scratch=()):
    space = lambda a: pltpu.SMEM if a.dtype == jnp.int32 else pltpu.VMEM
    return pl.pallas_call(
        kernel,
        out_shape=outs,
        in_specs=[pl.BlockSpec(memory_space=space(a)) for a in args],
        scratch_shapes=list(scratch),
        out_specs=jax.tree.map(lambda _: pl.BlockSpec(memory_space=pltpu.VMEM), outs),
        compiler_params=pltpu.CompilerParams(vmem_limit_bytes=24 * MIB),
        name=name,
    )(*args)


def log_totals(heads, extra):
    lse = extra[..., :heads]
    for part in range(1, 3):
        lse = lse + extra[..., heads * part : heads * (part + 1)]
    return lse


def per_head(heads, factor, shape):
    lane = lax.broadcasted_iota(jnp.int32, shape, len(shape) - 1) // HSZ
    spread = jnp.zeros(shape, F32)
    for h in range(heads):
        spread = jnp.where(lane == h, factor[..., h : h + 1], spread)
    return spread


def pair_kernel(heads, a_ref, b_ref, out_ref):
    cols = heads * HSZ
    rows = a_ref.shape[0]
    first = log_totals(heads, a_ref[:, cols:].astype(F32))
    second = log_totals(heads, b_ref[:, cols:].astype(F32))
    top = jnp.maximum(first, second)
    first, second = jnp.exp2(first - top), jnp.exp2(second - top)
    total = first + second
    joint = a_ref[:, :cols].astype(F32) * per_head(heads, first / total, (rows, cols))
    joint = joint + b_ref[:, :cols].astype(F32) * per_head(heads, second / total, (rows, cols))
    out_ref[:, :cols] = joint.astype(BF)
    lane = lax.broadcasted_iota(jnp.int32, (rows, EXTRA), 1)
    extra = jnp.zeros((rows, EXTRA), F32)
    for part, piece in enumerate(three_parts(top + jnp.log2(total))):
        for h in range(heads):
            extra = jnp.where(lane == heads * part + h, piece[:, h : h + 1], extra)
    out_ref[:, cols:] = extra.astype(BF)


def merge_kernel(heads, part_ref, wo_ref, out_ref):
    cols = heads * HSZ
    lse = log_totals(heads, part_ref[:, :, cols:].astype(F32))
    factor = jnp.exp2(lse - jnp.max(lse, axis=0, keepdims=True))
    factor = factor / jnp.sum(factor, axis=0, keepdims=True)
    spread = per_head(heads, factor, part_ref.shape[:2] + (cols,))
    attended = jnp.sum(part_ref[:, :, :cols].astype(F32) * spread, axis=0)
    out_ref[...] = dot(attended.astype(BF), wo_ref[...])


def project_kernel(a_ref, b_ref, c_ref, d_ref, lat_ref, gain_ref, w_ref, lat_out, q_out, kv_out):
    lat = lat_ref[...] + ((a_ref[...] + b_ref[...]) + (c_ref[...] + d_ref[...]))
    lat_out[...] = lat
    normed = layer_norm(lat, gain_ref[...]).astype(BF)
    cols = w_ref.shape[2]
    q_out[...] = (dot(normed, w_ref[0]) * SCALE2).astype(BF)
    keys = dot(normed, w_ref[1]).astype(BF)
    values = dot(normed, w_ref[2]).astype(BF)
    for copy in range(kv_out.shape[0]):
        kv_out[copy, :, :cols] = keys
        kv_out[copy, :, cols:] = values


def attend_kernel(heads, core_ref, q_ref, own_ref, other_ref, bias_ref, wo_ref, out_ref, kv_ref):
    join_rows(core_ref[0], own_ref, other_ref, kv_ref)
    cols = heads * HSZ
    query = q_ref[...]
    rows = query.shape[0]
    keys = kv_ref[:, :cols]
    values = kv_ref[:, cols:]
    lane = lax.broadcasted_iota(jnp.int32, (rows, cols), 1) // HSZ
    mixed = jnp.zeros((rows, cols), F32)
    for h in range(heads):
        own = jnp.where(lane == h, query.astype(F32), 0.0).astype(BF)
        scores = dot_nt(own, keys) + bias_ref[h] * LOG2E
        weights = jnp.exp2(scores - jnp.max(scores, axis=1, keepdims=True))
        total = jnp.sum(weights, axis=1, keepdims=True)
        mixed = jnp.where(lane == h, dot(weights.astype(BF), values) / total, mixed)
    out_ref[...] = dot(mixed.astype(BF), wo_ref[...])


def mlp_kernel(a_ref, b_ref, c_ref, d_ref, lat_ref, gain_ref, w1_ref, w2_ref, lat_out, out_ref):
    lat = lat_ref[...] + ((a_ref[...] + b_ref[...]) + (c_ref[...] + d_ref[...]))
    lat_out[...] = lat
    normed = layer_norm(lat, gain_ref[...]).astype(BF)
    hidden = jax.nn.gelu(dot(normed, w1_ref[...]), approximate=True).astype(BF)
    out_ref[...] = dot(hidden, w2_ref[...])


def last_kernel(a_ref, b_ref, c_ref, d_ref, lat_ref, gain_ref, out_ref):
    lat = lat_ref[...] + ((a_ref[...] + b_ref[...]) + (c_ref[...] + d_ref[...]))
    normed = layer_norm(lat, gain_ref[...]).astype(BF)
    for copy in range(out_ref.shape[0]):
        out_ref[copy] = normed


def query_kernel(
    heads,
    mod_ref,
    x_ref,
    table_ref,
    gain_ref,
    wq_ref,
    bias_ref,
    wo_ref,
    qt_ref,
    hot_ref,
    norm_ref,
    top_ref,
    bias_out,
    wot_ref,
    wqt_ref,
    bmax_ref,
    n_ref,
):
    step = pl.program_id(0)
    blocks = x_ref.shape[0] // MBLK
    lat_count = bias_ref.shape[2]

    @pl.when(step == 0)
    def _():
        wqt_ref[...] = wq_ref[...].T
        wot_ref[...] = wo_ref[...].T
        lane = lax.broadcasted_iota(jnp.int32, (lat_count, 128), 1)
        for h in range(heads):
            columns = bias_rows(bias_ref[:, h, :] * LOG2E, 128).T
            bias_out[h] = jnp.where(lane == 16 + h, 1.0, columns).astype(BF)
        for m in range(MODS):
            top = jnp.max(bias_ref[m] * LOG2E, axis=1, keepdims=True)
            bmax_ref[m] = jnp.broadcast_to(top, (heads, MBLK))

    for b in range(blocks):
        n_ref[b * MBLK : (b + 1) * MBLK, :] = embed_norm(
            mod_ref, step * blocks, b, x_ref, table_ref, gain_ref[...]
        )
        mod = mod_ref[step * blocks + b]
        hit, _ = modality_hot(mod, (16, MBLK), 0)
        hot_ref[:, b * MBLK : (b + 1) * MBLK] = jnp.where(hit, 1.0, 0.0).astype(BF)
        top_ref[:, b * MBLK : (b + 1) * MBLK] = bmax_ref[mod]
    query = dot_nt(wqt_ref[...], n_ref[...]) * SCALE2
    qt_ref[...] = query.astype(BF)
    for h in range(heads):
        own = query[h * HSZ : (h + 1) * HSZ, :]
        norm_ref[h : h + 1, :] = jnp.sqrt(jnp.sum(own * own, axis=0, keepdims=True))


def prepare_queries(queries, query_modality, table, gain, wq, bias, wo):
    count, width = queries.shape
    heads, lat_count = bias.shape[1:]
    cols = heads * HSZ
    tile = math.gcd(count, 512)
    whole = lambda *shape: pl.BlockSpec(shape, lambda i, mod: (0,) * len(shape))
    tiled = lambda rows: pl.BlockSpec((rows, tile), lambda i, mod: (0, i))
    return pl.pallas_call(
        functools.partial(query_kernel, heads),
        grid_spec=pltpu.PrefetchScalarGridSpec(
            num_scalar_prefetch=1,
            grid=(count // tile,),
            in_specs=[
                pl.BlockSpec((tile, width), lambda i, mod: (i, 0)),
                whole(MODS, width),
                whole(1, width),
                whole(width, cols),
                whole(MODS, heads, lat_count),
                whole(cols, width),
            ],
            out_specs=[
                tiled(cols),
                tiled(16),
                tiled(heads),
                tiled(heads),
                whole(heads, lat_count, 128),
                whole(width, cols),
            ],
            scratch_shapes=[
                pltpu.VMEM((cols, width), BF),
                pltpu.VMEM((MODS, heads, MBLK), F32),
                pltpu.VMEM((tile, width), BF),
            ],
        ),
        out_shape=[
            jax.ShapeDtypeStruct((cols, count), BF),
            jax.ShapeDtypeStruct((16, count), BF),
            jax.ShapeDtypeStruct((heads, count), F32),
            jax.ShapeDtypeStruct((heads, count), F32),
            jax.ShapeDtypeStruct((heads, lat_count, 128), BF),
            jax.ShapeDtypeStruct((width, cols), BF),
        ],
        compiler_params=pltpu.CompilerParams(vmem_limit_bytes=58 * MIB),
        name="queries",
    )(query_modality, queries, table, gain, wq, bias, wo)


def decode_kernel(
    heads,
    mod_ref,
    core_ref,
    x_ref,
    table_ref,
    own_ref,
    other_ref,
    wkv_ref,
    bias_ref,
    qt_ref,
    onehot_ref,
    norm_ref,
    top_ref,
    wot_ref,
    out_ref,
    lat_ref,
    kx_ref,
    vx_ref,
    long_ref,
    hot_ref,
    p_ref,
    mix_ref,
):
    step = pl.program_id(0)
    tile = x_ref.shape[0]
    blocks = tile // MBLK
    lat_count = lat_ref.shape[0]

    @pl.when(step == 0)
    def _():
        join_rows(core_ref[0], own_ref, other_ref, lat_ref)
        normed = lat_ref[...]
        ones = jnp.ones((HSZ, lat_count), BF)
        lane = lax.broadcasted_iota(jnp.int32, (lat_count, 128), 1) // HSZ
        sums = head_sums(2, 128)
        for pair in range(heads // 2):
            cols = slice(pair * 128, (pair + 1) * 128)
            keys = dot(normed, wkv_ref[0, :, cols])
            values = dot(normed, wkv_ref[1, :, cols]).astype(BF).T
            lengths = dot((keys * keys).astype(BF), sums)
            longest = jnp.sqrt(jnp.max(lengths, axis=0, keepdims=True))
            for half in range(2):
                h = 2 * pair + half
                kx_ref[h, :, :128] = jnp.where(lane == half, keys, 0.0).astype(BF)
                kx_ref[h, :, 128:] = bias_ref[h]
                vx_ref[h, :HSZ, :] = values[half * HSZ : (half + 1) * HSZ, :]
                vx_ref[h, HSZ:, :] = ones
                long_ref[h : h + 1, :] = jnp.broadcast_to(
                    longest[:, half * HSZ : half * HSZ + 1], (1, 128)
                )
        hot_ref[...] = jnp.zeros(hot_ref.shape, BF)

    bound = norm_ref[...] * long_ref[:, :1] + top_ref[...]
    hot_ref[:16, :] = onehot_ref[...]
    hot_ref[16 : 16 + heads, :] = (-bound).astype(BF)
    hot = hot_ref[...]
    least = jnp.full((1, tile), 1.0, F32)
    for h in range(heads + 1):
        if h < heads:
            pair = (h // 2) * 128
            right = jnp.concatenate([qt_ref[pair : pair + 128, :], hot], axis=0)
            p_ref[h % 2] = jnp.exp2(dot(kx_ref[h], right)).astype(BF)
        if h > 0:
            mixed = dot(vx_ref[h - 1], p_ref[(h - 1) % 2])
            least = jnp.minimum(least, mixed[HSZ : HSZ + 1, :])
            mix_ref[(h - 1) * HSZ : h * HSZ, :] = (mixed[:HSZ, :] / mixed[HSZ:, :]).astype(BF)

    @pl.when(jnp.min(least) < SMALL_TOTAL)
    def _():
        hot_ref[16 : 16 + heads, :] = jnp.zeros((heads, tile), BF)

        def exact(h, _):
            pair = pl.multiple_of((h // 2) * 128, 128)
            right = jnp.concatenate([qt_ref[pl.ds(pair, 128), :], hot_ref[...]], axis=0)
            scores = dot(kx_ref[h], right)
            top = jnp.max(scores, axis=0, keepdims=True)
            mixed = dot(vx_ref[h], jnp.exp2(scores - top).astype(BF))
            mixed = (mixed[:HSZ, :] / mixed[HSZ:, :]).astype(BF)
            mix_ref[pl.ds(pl.multiple_of(h * HSZ, HSZ), HSZ), :] = mixed
            return 0

        lax.fori_loop(0, heads, exact, 0)

    decoded = dot(wot_ref[...], mix_ref[...]).T
    for b in range(blocks):
        rows = slice(b * MBLK, (b + 1) * MBLK)
        mod = mod_ref[step * blocks + b]
        embedded = x_ref[rows, :].astype(F32) + table_ref[pl.ds(mod, 1), :]
        out_ref[rows, :] = embedded + decoded[rows, :]


def decode(core, queries, query_modality, table, own, other, wkv, prepared):
    queries_t, hot, norms, tops, bias, wo_t = prepared
    count, width = queries.shape
    heads, lat_count = bias.shape[:2]
    cols = heads * HSZ
    tile = math.gcd(count, 512)
    lat_width = wkv.shape[1]
    whole = lambda a: pl.BlockSpec(a.shape, lambda i, *_: (0,) * a.ndim)
    tiled = lambda rows: pl.BlockSpec((rows, tile), lambda i, *_: (0, i))
    return pl.pallas_call(
        functools.partial(decode_kernel, heads),
        grid_spec=pltpu.PrefetchScalarGridSpec(
            num_scalar_prefetch=2,
            grid=(count // tile,),
            in_specs=[
                pl.BlockSpec((tile, width), lambda i, *_: (i, 0)),
                whole(table),
                whole(own),
                whole(other),
                whole(wkv),
                whole(bias),
                tiled(cols),
                tiled(16),
                tiled(heads),
                tiled(heads),
                whole(wo_t),
            ],
            out_specs=pl.BlockSpec((tile, width), lambda i, *_: (i, 0)),
            scratch_shapes=[
                pltpu.VMEM((lat_count, lat_width), BF),
                pltpu.VMEM((heads, lat_count, 256), BF),
                pltpu.VMEM((heads, 128, lat_count), BF),
                pltpu.VMEM((heads, 128), F32),
                pltpu.VMEM((128, tile), BF),
                pltpu.VMEM((2, lat_count, tile), BF),
                pltpu.VMEM((cols, tile), BF),
            ],
        ),
        out_shape=jax.ShapeDtypeStruct((count, width), F32),
        compiler_params=pltpu.CompilerParams(vmem_limit_bytes=58 * MIB),
        name="decode",
    )(query_modality, core, queries, table, own, other, wkv, bias, queries_t, hot, norms, tops, wo_t)


def trade(parts):
    size = lax.axis_size("inp")
    groups = [list(range(core, size, 2)) for core in range(2)]
    return lax.all_to_all(parts, "inp", 0, 0, axis_index_groups=groups)


def other_core(rows):
    return lax.ppermute(rows, "inp", [(i, i ^ 1) for i in range(lax.axis_size("inp"))])


def head_parts(part):
    size = lax.axis_size("head")
    moved = [
        lax.ppermute(part, "head", [(i, (i + k) % size) for i in range(size)])
        for k in range(1, size)
    ]
    return [part] + moved


def body(
    inputs,
    input_modality,
    queries,
    query_modality,
    modality_embed,
    latents,
    ln_in_gain,
    ln_lat_gain,
    enc_wq,
    enc_wkv,
    enc_bias,
    enc_wo,
    self_gain,
    self_wqkv,
    self_bias,
    self_wo,
    mlp_gain,
    mlp_w1,
    mlp_w2,
    dec_gain,
    dec_wkv,
    query_gain,
    dec_wq,
    dec_bias,
    dec_wo,
):
    lat_count, width = latents.shape
    lat_rows = lat_count // lax.axis_size("inp")
    row_first = lax.axis_index("inp") * lat_rows
    heads = enc_bias.shape[1]
    cols = heads * HSZ
    row = lambda v: v.reshape(1, -1)
    shape = jax.ShapeDtypeStruct

    core = (lax.axis_index("inp") % 2).astype(jnp.int32).reshape(1)
    chips = lax.axis_size("inp") // 2
    keep, send = encode(
        core,
        inputs,
        input_modality,
        modality_embed,
        row(ln_in_gain),
        latents,
        row(ln_lat_gain),
        enc_wq,
        enc_wkv,
        enc_bias,
    )
    joint = small_call(
        functools.partial(pair_kernel, heads),
        "pair",
        shape(keep.shape, BF),
        keep,
        other_core(send),
    )
    joint, early = lax.optimization_barrier((joint, queries))
    parts = trade(joint.reshape(chips, lat_rows, joint.shape[1]))
    prepared = prepare_queries(
        early, query_modality, modality_embed, row(query_gain), dec_wq, dec_bias, dec_wo
    )
    parts, prepared = lax.optimization_barrier((parts, prepared))
    enc_part = small_call(
        functools.partial(merge_kernel, heads), "merge", shape((lat_rows, width), F32), parts, enc_wo
    )
    latent_rows = lax.dynamic_slice_in_dim(latents, row_first, lat_rows, 0)
    lat_one, self_q, self_kv = small_call(
        project_kernel,
        "project",
        [
            shape((lat_rows, width), F32),
            shape((lat_rows, cols), BF),
            shape((chips, lat_rows, 2 * cols), BF),
        ],
        *head_parts(enc_part),
        latent_rows,
        row(self_gain),
        self_wqkv,
    )
    own_kv = trade(self_kv)
    self_part = small_call(
        functools.partial(attend_kernel, heads),
        "attend",
        shape((lat_rows, width), F32),
        core,
        self_q,
        own_kv,
        other_core(own_kv),
        self_bias,
        self_wo,
        scratch=[pltpu.VMEM((lat_count, 2 * cols), BF)],
    )
    lat_two, mlp_part = small_call(
        mlp_kernel,
        "mlp",
        [shape((lat_rows, width), F32), shape((lat_rows, width), F32)],
        *head_parts(self_part),
        lat_one,
        row(mlp_gain),
        mlp_w1,
        mlp_w2,
    )
    normed = small_call(
        last_kernel,
        "last",
        shape((chips, lat_rows, width), BF),
        *head_parts(mlp_part),
        lat_two,
        row(dec_gain),
    )
    own = trade(normed)
    return decode(
        core, queries, query_modality, modality_embed, own, other_core(own), dec_wkv, prepared
    )


def solution(mesh):
    placed = (
        P("inp", None),
        P("inp"),
        P(("inp", "head"), None),
        P(("inp", "head")),
        P(),
        P(),
        P(),
        P(),
        P(None, "head"),
        P(None, None, "head"),
        P(None, "head", None),
        P("head", None),
        P(),
        P(None, None, "head"),
        P("head", "inp", None),
        P("head", None),
        P(),
        P(None, "head"),
        P("head", None),
        P(),
        P(),
        P(),
        P(),
        P(),
        P(),
    )
    return jax.shard_map(
        body, mesh=mesh, in_specs=placed, out_specs=P(("inp", "head"), None), check_vma=False
    )
```

```python
import functools
import math

import jax
import jax.numpy as jnp
from jax import lax
from jax.experimental import pallas as pl
from jax.experimental.pallas import tpu as pltpu
from jax.sharding import PartitionSpec as P

HSZ = 64
MODS = 3
MBLK = 128
EPSILON = 1e-05
LOG2E = 1.4426950408889634
SCALE2 = LOG2E / math.sqrt(HSZ)
NEG_FLOOR = -1e30
BF = jnp.bfloat16
F32 = jnp.float32
MIB = 2**20
EXTRA = 128
SMALL_TOTAL = 2.0**-95


def dot(a, b):
    return jnp.dot(a, b, preferred_element_type=F32)


def dot_nt(a, b):
    return lax.dot_general(a, b, (((1,), (1,)), ((), ())), preferred_element_type=F32)


def layer_norm(values, gain):
    centered = values - jnp.mean(values, axis=-1, keepdims=True)
    variance = jnp.mean(centered * centered, axis=-1, keepdims=True)
    return centered * lax.rsqrt(variance + EPSILON) * gain


def three_parts(values):
    high = values.astype(BF)
    rest = values - high.astype(F32)
    mid = rest.astype(BF)
    low = (rest - mid.astype(F32)).astype(BF)
    return high.astype(F32), mid.astype(F32), low.astype(F32)


def bias_rows(bias, rows):
    index = lax.broadcasted_iota(jnp.int32, (rows, bias.shape[1]), 0)
    block = jnp.zeros((rows, bias.shape[1]), F32)
    for part, piece in enumerate(three_parts(bias)):
        for mod in range(MODS):
            block = jnp.where(index == MODS * part + mod, piece[mod : mod + 1, :], block)
    return block


def modality_hot(mod, shape, dim):
    index = lax.broadcasted_iota(jnp.int32, shape, dim)
    hit = (index == mod) | (index == mod + MODS) | (index == mod + 2 * MODS)
    return hit, index


def head_sums(count, lanes):
    row = lax.broadcasted_iota(jnp.int32, (count * HSZ, lanes), 0) // HSZ
    lane = lax.broadcasted_iota(jnp.int32, (count * HSZ, lanes), 1) // (lanes // count)
    return jnp.where(row == lane, 1.0, 0.0).astype(BF)


def embed_norm(mod_ref, first, b, x_ref, table_ref, gain):
    embedded = x_ref[b * MBLK : (b + 1) * MBLK, :].astype(F32)
    embedded = embedded + table_ref[pl.ds(mod_ref[first + b], 1), :]
    return layer_norm(embedded, gain).astype(BF)


def part_rows(core, all_ref, own_ref, other_ref):
    for held, refs in enumerate(((own_ref, other_ref), (other_ref, own_ref))):

        @pl.when(core == held)
        def _():
            for block in range(all_ref.shape[0] // 16):
                rows = slice(block // 2 * 16, block // 2 * 16 + 16)
                refs[block % 2][rows, :] = all_ref[block * 16 : block * 16 + 16, :]


def join_rows(core, own_ref, other_ref, all_ref):
    for held, refs in enumerate(((own_ref, other_ref), (other_ref, own_ref))):

        @pl.when(core == held)
        def _():
            for block in range(all_ref.shape[0] // 16):
                all_ref[block * 16 : block * 16 + 16, :] = refs[block % 2][block // 2]


def encode_kernel(
    heads,
    mod_ref,
    core_ref,
    x_ref,
    next_ref,
    table_ref,
    gain_ref,
    lat_ref,
    lat_gain_ref,
    wq_ref,
    wkv_ref,
    bias_ref,
    keep_ref,
    send_ref,
    qx_ref,
    norm_ref,
    wvt_ref,
    n_ref,
    hot_ref,
    k_ref,
    vt_ref,
    p_ref,
    part_ref,
    shift_ref,
    m_ref,
    acc_ref,
    out_ref,
):
    step = pl.program_id(0)
    last = pl.num_programs(0) - 1
    points = x_ref.shape[0]
    blocks = points // MBLK
    lat_count = lat_ref.shape[0]
    slot = lax.rem(step, 2)
    row16 = lax.broadcasted_iota(jnp.int32, (16, lat_count), 0)
    gain = gain_ref[...]

    def project(at, into):
        normed = n_ref[...]
        keys = dot(normed, wkv_ref[0])
        k_ref[into] = keys.astype(BF)
        vt_ref[into] = dot_nt(wvt_ref[...], normed).astype(BF)
        lengths = dot((keys * keys).astype(BF), head_sums(heads, 128))
        longest = jnp.sqrt(jnp.max(lengths, axis=0, keepdims=True))
        present = [jnp.bool_(False)] * MODS
        for b in range(blocks):
            mod = mod_ref[at * blocks + b]
            hit, index = modality_hot(mod, (MBLK, 128), 1)
            hit = jnp.where(hit | (index == 16), 1.0, 0.0)
            hot_ref[into, b * MBLK : (b + 1) * MBLK, :] = hit.astype(BF)
            present = [p | (mod == m) for m, p in enumerate(present)]
        for h in range(heads):
            bound = jnp.full((1, lat_count), NEG_FLOOR, F32)
            for m in range(MODS):
                held = jnp.where(present[m], bias_ref[m, h : h + 1, :] * LOG2E, NEG_FLOOR)
                bound = jnp.maximum(bound, held)
            lane = h * (128 // heads)
            bound = bound + norm_ref[h : h + 1, :] * longest[:, lane : lane + 1]
            shift_ref[into, h] = bound.astype(BF).astype(F32)

    @pl.when(step == 0)
    def _():
        normed = layer_norm(lat_ref[...], lat_gain_ref[...]).astype(BF)
        query = (dot(normed, wq_ref[...]) * SCALE2).T
        qx_ref[...] = jnp.zeros(qx_ref.shape, BF)
        for h in range(heads):
            half = (h % 2) * HSZ
            own = query[h * HSZ : (h + 1) * HSZ, :]
            qx_ref[h, half : half + HSZ, :] = own.astype(BF)
            qx_ref[h, 128:144, :] = bias_rows(bias_ref[:, h, :] * LOG2E, 16).astype(BF)
            norm_ref[h : h + 1, :] = jnp.sqrt(jnp.sum(own * own, axis=0, keepdims=True))
        wvt_ref[...] = wkv_ref[1].T
        m_ref[...] = jnp.full(m_ref.shape, NEG_FLOOR, F32)
        acc_ref[...] = jnp.zeros(acc_ref.shape, F32)
        for b in range(blocks):
            n_ref[b * MBLK : (b + 1) * MBLK, :] = embed_norm(
                mod_ref, 0, b, x_ref, table_ref, gain
            )
        project(0, 0)

    following = jnp.minimum(step + 1, last)

    def main(prepare):
        hot = hot_ref[slot]
        ones = jnp.ones((HSZ, points), BF)
        for h in range(heads):
            qx_ref[h, 144:160, :] = jnp.where(row16 == 0, -shift_ref[slot, h], 0.0).astype(BF)
        per_head = -(-blocks // 2)
        for h in range(heads + 1):
            if h < heads:
                pair = (h // 2) * 128
                left = jnp.concatenate([k_ref[slot, :, pair : pair + 128], hot], axis=1)
                p_ref[h % 2] = jnp.exp2(dot(left, qx_ref[h])).astype(BF)
            if h > 0:
                values_h = vt_ref[slot, (h - 1) * HSZ : h * HSZ, :]
                values_h = jnp.concatenate([values_h, ones], axis=0)
                part_ref[h - 1] = dot(values_h, p_ref[(h - 1) % 2])
            for b in range(h * per_head, min((h + 1) * per_head, blocks) if prepare else 0):
                n_ref[b * MBLK : (b + 1) * MBLK, :] = embed_norm(
                    mod_ref, following * blocks, b, next_ref, table_ref, gain
                )
            if h == 2 and prepare:
                project(following, 1 - slot)

    pl.when(step < last)(functools.partial(main, True))
    pl.when(step == last)(functools.partial(main, False))
    least = jnp.min(part_ref[:, HSZ : HSZ + 1, :])

    @pl.when(least < SMALL_TOTAL)
    def _():
        def exact(h, _):
            pair = pl.multiple_of((h // 2) * 128, 128)
            qx_ref[h, 144:160, :] = jnp.zeros((16, lat_count), BF)
            left = jnp.concatenate([k_ref[slot, :, pl.ds(pair, 128)], hot_ref[slot]], axis=1)
            scores = dot(left, qx_ref[h])
            top = jnp.max(scores, axis=0, keepdims=True)
            weights = jnp.exp2(scores - top).astype(BF)
            values_h = vt_ref[slot, pl.ds(pl.multiple_of(h * HSZ, HSZ), HSZ), :]
            values_h = jnp.concatenate([values_h, jnp.ones((HSZ, points), BF)], axis=0)
            part_ref[h] = dot(values_h, weights)
            shift_ref[slot, h] = top
            return 0

        lax.fori_loop(0, heads, exact, 0)

    for h in range(heads):
        old = m_ref[h]
        own = shift_ref[slot, h]
        new = jnp.maximum(old, own)
        m_ref[h] = new
        acc_ref[h] = acc_ref[h] * jnp.exp2(old - new) + part_ref[h] * jnp.exp2(own - new)

    @pl.when(step == last)
    def _():
        index = lax.broadcasted_iota(jnp.int32, (EXTRA, lat_count), 0)
        extra = jnp.zeros((EXTRA, lat_count), F32)
        pieces = []
        for h in range(heads):
            acc = acc_ref[h]
            total = acc[HSZ : HSZ + 1, :]
            pieces.append(acc[:HSZ, :] / total)
            for part, piece in enumerate(three_parts(m_ref[h] + jnp.log2(total))):
                extra = jnp.where(index == heads * part + h, piece, extra)
        out_ref[...] = jnp.concatenate(pieces + [extra], axis=0).T.astype(BF)
        part_rows(core_ref[0], out_ref, keep_ref, send_ref)


def encode(core, inputs, input_modality, table, gain, latents, lat_gain, wq, wkv, bias):
    points, width = inputs.shape
    heads = bias.shape[1]
    lat_count, lat_width = latents.shape
    cols = heads * HSZ
    tile = math.gcd(points, 2048)
    steps = points // tile
    whole = lambda *shape: pl.BlockSpec(shape, lambda i, *_: (0,) * len(shape))
    return pl.pallas_call(
        functools.partial(encode_kernel, heads),
        grid_spec=pltpu.PrefetchScalarGridSpec(
            num_scalar_prefetch=2,
            grid=(steps,),
            in_specs=[
                pl.BlockSpec((tile, width), lambda i, *_: (0, 0)),
                pl.BlockSpec((tile, width), lambda i, *_: (jnp.minimum(i + 1, steps - 1), 0)),
                whole(MODS, width),
                whole(1, width),
                whole(lat_count, lat_width),
                whole(1, lat_width),
                whole(lat_width, cols),
                whole(2, width, cols),
                whole(MODS, heads, lat_count),
            ],
            out_specs=[whole(lat_count // 2, cols + EXTRA)] * 2,
            scratch_shapes=[
                pltpu.VMEM((heads, 256, lat_count), BF),
                pltpu.VMEM((heads, lat_count), F32),
                pltpu.VMEM((cols, width), BF),
                pltpu.VMEM((tile, width), BF),
                pltpu.VMEM((2, tile, 128), BF),
                pltpu.VMEM((2, tile, cols), BF),
                pltpu.VMEM((2, cols, tile), BF),
                pltpu.VMEM((2, tile, lat_count), BF),
                pltpu.VMEM((heads, 128, lat_count), F32),
                pltpu.VMEM((2, heads, 1, lat_count), F32),
                pltpu.VMEM((heads, 1, lat_count), F32),
                pltpu.VMEM((heads, 128, lat_count), F32),
                pltpu.VMEM((lat_count, cols + EXTRA), BF),
            ],
        ),
        out_shape=[jax.ShapeDtypeStruct((lat_count // 2, cols + EXTRA), BF)] * 2,
        compiler_params=pltpu.CompilerParams(vmem_limit_bytes=58 * MIB),
        name="encode",
    )(input_modality, core, inputs, inputs, table, gain, latents, lat_gain, wq, wkv, bias)


def small_call(kernel, name, outs, *args, scratch=()):
    space = lambda a: pltpu.SMEM if a.dtype == jnp.int32 else pltpu.VMEM
    return pl.pallas_call(
        kernel,
        out_shape=outs,
        in_specs=[pl.BlockSpec(memory_space=space(a)) for a in args],
        scratch_shapes=list(scratch),
        out_specs=jax.tree.map(lambda _: pl.BlockSpec(memory_space=pltpu.VMEM), outs),
        compiler_params=pltpu.CompilerParams(vmem_limit_bytes=14 * MIB),
        name=name,
    )(*args)


def log_totals(heads, extra):
    lse = extra[..., :heads]
    for part in range(1, 3):
        lse = lse + extra[..., heads * part : heads * (part + 1)]
    return lse


def per_head(heads, factor, shape):
    lane = lax.broadcasted_iota(jnp.int32, shape, len(shape) - 1) // HSZ
    spread = jnp.zeros(shape, F32)
    for h in range(heads):
        spread = jnp.where(lane == h, factor[..., h : h + 1], spread)
    return spread


def pair_kernel(heads, a_ref, b_ref, out_ref):
    cols = heads * HSZ
    rows = a_ref.shape[0]
    first = log_totals(heads, a_ref[:, cols:].astype(F32))
    second = log_totals(heads, b_ref[:, cols:].astype(F32))
    top = jnp.maximum(first, second)
    first, second = jnp.exp2(first - top), jnp.exp2(second - top)
    total = first + second
    joint = a_ref[:, :cols].astype(F32) * per_head(heads, first / total, (rows, cols))
    joint = joint + b_ref[:, :cols].astype(F32) * per_head(heads, second / total, (rows, cols))
    out_ref[:, :cols] = joint.astype(BF)
    lane = lax.broadcasted_iota(jnp.int32, (rows, EXTRA), 1)
    extra = jnp.zeros((rows, EXTRA), F32)
    for part, piece in enumerate(three_parts(top + jnp.log2(total))):
        for h in range(heads):
            extra = jnp.where(lane == heads * part + h, piece[:, h : h + 1], extra)
    out_ref[:, cols:] = extra.astype(BF)


def merge_kernel(heads, part_ref, wo_ref, out_ref):
    cols = heads * HSZ
    lse = log_totals(heads, part_ref[:, :, cols:].astype(F32))
    factor = jnp.exp2(lse - jnp.max(lse, axis=0, keepdims=True))
    factor = factor / jnp.sum(factor, axis=0, keepdims=True)
    spread = per_head(heads, factor, part_ref.shape[:2] + (cols,))
    attended = jnp.sum(part_ref[:, :, :cols].astype(F32) * spread, axis=0)
    out_ref[...] = dot(attended.astype(BF), wo_ref[...])


def project_kernel(a_ref, b_ref, c_ref, d_ref, lat_ref, gain_ref, w_ref, lat_out, q_out, kv_out):
    lat = lat_ref[...] + ((a_ref[...] + b_ref[...]) + (c_ref[...] + d_ref[...]))
    lat_out[...] = lat
    normed = layer_norm(lat, gain_ref[...]).astype(BF)
    cols = w_ref.shape[2]
    q_out[...] = (dot(normed, w_ref[0]) * SCALE2).astype(BF)
    keys = dot(normed, w_ref[1]).astype(BF)
    values = dot(normed, w_ref[2]).astype(BF)
    for copy in range(kv_out.shape[0]):
        kv_out[copy, :, :cols] = keys
        kv_out[copy, :, cols:] = values


def attend_kernel(heads, core_ref, q_ref, own_ref, other_ref, bias_ref, wo_ref, out_ref, kv_ref):
    join_rows(core_ref[0], own_ref, other_ref, kv_ref)
    cols = heads * HSZ
    query = q_ref[...]
    rows = query.shape[0]
    keys = kv_ref[:, :cols]
    values = kv_ref[:, cols:]
    lane = lax.broadcasted_iota(jnp.int32, (rows, cols), 1) // HSZ
    mixed = jnp.zeros((rows, cols), F32)
    for h in range(heads):
        own = jnp.where(lane == h, query.astype(F32), 0.0).astype(BF)
        scores = dot_nt(own, keys) + bias_ref[h] * LOG2E
        weights = jnp.exp2(scores - jnp.max(scores, axis=1, keepdims=True))
        total = jnp.sum(weights, axis=1, keepdims=True)
        mixed = jnp.where(lane == h, dot(weights.astype(BF), values) / total, mixed)
    out_ref[...] = dot(mixed.astype(BF), wo_ref[...])


def mlp_kernel(a_ref, b_ref, c_ref, d_ref, lat_ref, gain_ref, w1_ref, w2_ref, lat_out, out_ref):
    lat = lat_ref[...] + ((a_ref[...] + b_ref[...]) + (c_ref[...] + d_ref[...]))
    lat_out[...] = lat
    normed = layer_norm(lat, gain_ref[...]).astype(BF)
    hidden = jax.nn.gelu(dot(normed, w1_ref[...]), approximate=True).astype(BF)
    out_ref[...] = dot(hidden, w2_ref[...])


def last_kernel(a_ref, b_ref, c_ref, d_ref, lat_ref, gain_ref, out_ref):
    lat = lat_ref[...] + ((a_ref[...] + b_ref[...]) + (c_ref[...] + d_ref[...]))
    normed = layer_norm(lat, gain_ref[...]).astype(BF)
    for copy in range(out_ref.shape[0]):
        out_ref[copy] = normed


def query_kernel(
    heads,
    mod_ref,
    x_ref,
    table_ref,
    gain_ref,
    wq_ref,
    bias_ref,
    wo_ref,
    qt_ref,
    norm_ref,
    top_ref,
    bias_out,
    wot_ref,
    wqt_ref,
    bmax_ref,
    n_ref,
):
    step = pl.program_id(0)
    blocks = x_ref.shape[0] // MBLK
    lat_count = bias_ref.shape[2]

    @pl.when(step == 0)
    def _():
        wqt_ref[...] = wq_ref[...].T
        wot_ref[...] = wo_ref[...].T
        row = lax.broadcasted_iota(jnp.int32, (16, lat_count), 0)
        for part in range(heads // 8):
            block = []
            for h in range(8 * part, 8 * part + 8):
                rows = bias_rows(bias_ref[:, h, :] * LOG2E, 16)
                block.append(jnp.where(row == 3 * MODS + part, 1.0, rows))
            bias_out[part] = jnp.concatenate(block, axis=0).T.astype(BF)
        for m in range(MODS):
            top = jnp.max(bias_ref[m] * LOG2E, axis=1, keepdims=True)
            bmax_ref[m] = jnp.broadcast_to(top, (heads, MBLK))

    for b in range(blocks):
        n_ref[b * MBLK : (b + 1) * MBLK, :] = embed_norm(
            mod_ref, step * blocks, b, x_ref, table_ref, gain_ref[...]
        )
        mod = mod_ref[step * blocks + b]
        top_ref[:, b * MBLK : (b + 1) * MBLK] = bmax_ref[mod]
    query = dot_nt(wqt_ref[...], n_ref[...]) * SCALE2
    qt_ref[...] = query.astype(BF)
    for h in range(heads):
        own = query[h * HSZ : (h + 1) * HSZ, :]
        norm_ref[h : h + 1, :] = jnp.sqrt(jnp.sum(own * own, axis=0, keepdims=True))


def prepare_queries(queries, query_modality, table, gain, wq, bias, wo):
    count, width = queries.shape
    heads, lat_count = bias.shape[1:]
    cols = heads * HSZ
    tile = math.gcd(count, 512)
    whole = lambda *shape: pl.BlockSpec(shape, lambda i, mod: (0,) * len(shape))
    tiled = lambda rows: pl.BlockSpec((rows, tile), lambda i, mod: (0, i))
    return pl.pallas_call(
        functools.partial(query_kernel, heads),
        grid_spec=pltpu.PrefetchScalarGridSpec(
            num_scalar_prefetch=1,
            grid=(count // tile,),
            in_specs=[
                pl.BlockSpec((tile, width), lambda i, mod: (i, 0)),
                whole(MODS, width),
                whole(1, width),
                whole(width, cols),
                whole(MODS, heads, lat_count),
                whole(cols, width),
            ],
            out_specs=[
                tiled(cols),
                tiled(heads),
                tiled(heads),
                whole(heads // 8, lat_count, 128),
                whole(width, cols),
            ],
            scratch_shapes=[
                pltpu.VMEM((cols, width), BF),
                pltpu.VMEM((MODS, heads, MBLK), F32),
                pltpu.VMEM((tile, width), BF),
            ],
        ),
        out_shape=[
            jax.ShapeDtypeStruct((cols, count), BF),
            jax.ShapeDtypeStruct((heads, count), F32),
            jax.ShapeDtypeStruct((heads, count), F32),
            jax.ShapeDtypeStruct((heads // 8, lat_count, 128), BF),
            jax.ShapeDtypeStruct((width, cols), BF),
        ],
        compiler_params=pltpu.CompilerParams(vmem_limit_bytes=58 * MIB),
        name="queries",
    )(query_modality, queries, table, gain, wq, bias, wo)


def decode_kernel(
    heads,
    mod_ref,
    core_ref,
    x_ref,
    table_ref,
    own_ref,
    other_ref,
    wkv_ref,
    bias_ref,
    qt_ref,
    norm_ref,
    top_ref,
    wot_ref,
    out_ref,
    lat_ref,
    kx_ref,
    vx_ref,
    long_ref,
    hot_ref,
    p_ref,
    mix_ref,
):
    step = pl.program_id(0)
    tile = x_ref.shape[0]
    blocks = tile // MBLK
    lat_count = lat_ref.shape[0]

    @pl.when(step == 0)
    def _():
        join_rows(core_ref[0], own_ref, other_ref, lat_ref)
        normed = lat_ref[...]
        ones = jnp.ones((HSZ, lat_count), BF)
        lane = lax.broadcasted_iota(jnp.int32, (lat_count, 128), 1)
        sums = head_sums(4, 128)
        for quad in range(heads // 4):
            cols = slice(quad * 256, (quad + 1) * 256)
            keys = dot(normed, wkv_ref[0, :, cols])
            values = dot(normed, wkv_ref[1, :, cols]).astype(BF).T
            lengths = dot((keys * keys).astype(BF), sums)
            longest = jnp.sqrt(jnp.max(lengths, axis=0, keepdims=True))
            for at in range(4):
                h = 4 * quad + at
                pair = keys[:, at // 2 * 128 : at // 2 * 128 + 128]
                kx_ref[h, :, :128] = jnp.where(lane // HSZ == at % 2, pair, 0.0).astype(BF)
                extra = jnp.where(lane // 16 == h % 8, bias_ref[h // 8].astype(F32), 0.0)
                kx_ref[h, :, 128:] = extra.astype(BF)
                vx_ref[h, :HSZ, :] = values[at * HSZ : (at + 1) * HSZ, :]
                vx_ref[h, HSZ:, :] = ones
                long_ref[h : h + 1, :] = jnp.broadcast_to(
                    longest[:, at * 32 : at * 32 + 1], (1, 128)
                )

    bound = norm_ref[...] * long_ref[:, :1] + top_ref[...]
    row = lax.broadcasted_iota(jnp.int32, (16, MBLK), 0)
    for b in range(blocks):
        hit, _ = modality_hot(mod_ref[step * blocks + b], (16, MBLK), 0)
        onehot = jnp.where(hit, 1.0, 0.0)
        lanes = slice(b * MBLK, (b + 1) * MBLK)
        for group in range(8):
            rows = onehot
            for part in range(heads // 8):
                own = bound[8 * part + group : 8 * part + group + 1, lanes]
                rows = jnp.where(row == 3 * MODS + part, -own, rows)
            hot_ref[16 * group : 16 * group + 16, lanes] = rows.astype(BF)
    hot = hot_ref[...]
    least = jnp.full((1, tile), 1.0, F32)
    for h in range(heads + 1):
        if h < heads:
            pair = (h // 2) * 128
            right = jnp.concatenate([qt_ref[pair : pair + 128, :], hot], axis=0)
            p_ref[h % 2] = jnp.exp2(dot(kx_ref[h], right)).astype(BF)
        if h > 0:
            mixed = dot(vx_ref[h - 1], p_ref[(h - 1) % 2])
            least = jnp.minimum(least, mixed[HSZ : HSZ + 1, :])
            mix_ref[(h - 1) * HSZ : h * HSZ, :] = (mixed[:HSZ, :] / mixed[HSZ:, :]).astype(BF)

    @pl.when(jnp.min(least) < SMALL_TOTAL)
    def _():
        for b in range(blocks):
            hit, _ = modality_hot(mod_ref[step * blocks + b], (16, MBLK), 0)
            onehot = jnp.where(hit, 1.0, 0.0).astype(BF)
            for group in range(8):
                hot_ref[16 * group : 16 * group + 16, b * MBLK : (b + 1) * MBLK] = onehot

        def exact(h, _):
            pair = pl.multiple_of((h // 2) * 128, 128)
            right = jnp.concatenate([qt_ref[pl.ds(pair, 128), :], hot_ref[...]], axis=0)
            scores = dot(kx_ref[h], right)
            top = jnp.max(scores, axis=0, keepdims=True)
            mixed = dot(vx_ref[h], jnp.exp2(scores - top).astype(BF))
            mixed = (mixed[:HSZ, :] / mixed[HSZ:, :]).astype(BF)
            mix_ref[pl.ds(pl.multiple_of(h * HSZ, HSZ), HSZ), :] = mixed
            return 0

        lax.fori_loop(0, heads, exact, 0)

    decoded = dot(wot_ref[...], mix_ref[...]).T
    for b in range(blocks):
        rows = slice(b * MBLK, (b + 1) * MBLK)
        mod = mod_ref[step * blocks + b]
        embedded = x_ref[rows, :].astype(F32) + table_ref[pl.ds(mod, 1), :]
        out_ref[rows, :] = embedded + decoded[rows, :]


def decode(core, queries, query_modality, table, own, other, wkv, prepared):
    queries_t, norms, tops, bias, wo_t = prepared
    count, width = queries.shape
    lat_count = bias.shape[1]
    cols = queries_t.shape[0]
    heads = cols // HSZ
    tile = math.gcd(count, 512)
    lat_width = wkv.shape[1]
    held = pl.BlockSpec(memory_space=pltpu.VMEM)
    tiled = lambda rows: pl.BlockSpec((rows, tile), lambda i, *_: (0, i))
    return pl.pallas_call(
        functools.partial(decode_kernel, heads),
        grid_spec=pltpu.PrefetchScalarGridSpec(
            num_scalar_prefetch=2,
            grid=(count // tile,),
            in_specs=[
                pl.BlockSpec((tile, width), lambda i, *_: (i, 0)),
                held,
                held,
                held,
                held,
                held,
                tiled(cols),
                tiled(heads),
                tiled(heads),
                held,
            ],
            out_specs=pl.BlockSpec((tile, width), lambda i, *_: (i, 0)),
            scratch_shapes=[
                pltpu.VMEM((lat_count, lat_width), BF),
                pltpu.VMEM((heads, lat_count, 256), BF),
                pltpu.VMEM((heads, 128, lat_count), BF),
                pltpu.VMEM((heads, 128), F32),
                pltpu.VMEM((128, tile), BF),
                pltpu.VMEM((2, lat_count, tile), BF),
                pltpu.VMEM((cols, tile), BF),
            ],
        ),
        out_shape=jax.ShapeDtypeStruct((count, width), F32),
        compiler_params=pltpu.CompilerParams(vmem_limit_bytes=32 * MIB),
        name="decode",
    )(query_modality, core, queries, table, own, other, wkv, bias, queries_t, norms, tops, wo_t)


def trade(parts):
    size = lax.axis_size("inp")
    groups = [list(range(core, size, 2)) for core in range(2)]
    return lax.all_to_all(parts, "inp", 0, 0, axis_index_groups=groups)


def other_core(rows):
    return lax.ppermute(rows, "inp", [(i, i ^ 1) for i in range(lax.axis_size("inp"))])


def head_parts(part):
    size = lax.axis_size("head")
    moved = [
        lax.ppermute(part, "head", [(i, (i + k) % size) for i in range(size)])
        for k in range(1, size)
    ]
    return [part] + moved


def body(
    inputs,
    input_modality,
    queries,
    query_modality,
    modality_embed,
    latents,
    ln_in_gain,
    ln_lat_gain,
    enc_wq,
    enc_wkv,
    enc_bias,
    enc_wo,
    self_gain,
    self_wqkv,
    self_bias,
    self_wo,
    mlp_gain,
    mlp_w1,
    mlp_w2,
    dec_gain,
    dec_wkv,
    query_gain,
    dec_wq,
    dec_bias,
    dec_wo,
):
    lat_count, width = latents.shape
    lat_rows = lat_count // lax.axis_size("inp")
    row_first = lax.axis_index("inp") * lat_rows
    heads = enc_bias.shape[1]
    cols = heads * HSZ
    row = lambda v: v.reshape(1, -1)
    shape = jax.ShapeDtypeStruct

    core = (lax.axis_index("inp") % 2).astype(jnp.int32).reshape(1)
    chips = lax.axis_size("inp") // 2
    keep, send = encode(
        core,
        inputs,
        input_modality,
        modality_embed,
        row(ln_in_gain),
        latents,
        row(ln_lat_gain),
        enc_wq,
        enc_wkv,
        enc_bias,
    )
    joint = small_call(
        functools.partial(pair_kernel, heads),
        "pair",
        shape(keep.shape, BF),
        keep,
        other_core(send),
    )
    joint, early = lax.optimization_barrier((joint, queries))
    parts = trade(joint.reshape(chips, lat_rows, joint.shape[1]))
    prepared = prepare_queries(
        early, query_modality, modality_embed, row(query_gain), dec_wq, dec_bias, dec_wo
    )
    parts, prepared = lax.optimization_barrier((parts, prepared))
    enc_part = small_call(
        functools.partial(merge_kernel, heads), "merge", shape((lat_rows, width), F32), parts, enc_wo
    )
    latent_rows = lax.dynamic_slice_in_dim(latents, row_first, lat_rows, 0)
    lat_one, self_q, self_kv = small_call(
        project_kernel,
        "project",
        [
            shape((lat_rows, width), F32),
            shape((lat_rows, cols), BF),
            shape((chips, lat_rows, 2 * cols), BF),
        ],
        *head_parts(enc_part),
        latent_rows,
        row(self_gain),
        self_wqkv,
    )
    own_kv = trade(self_kv)
    self_part = small_call(
        functools.partial(attend_kernel, heads),
        "attend",
        shape((lat_rows, width), F32),
        core,
        self_q,
        own_kv,
        other_core(own_kv),
        self_bias,
        self_wo,
        scratch=[pltpu.VMEM((lat_count, 2 * cols), BF)],
    )
    lat_two, mlp_part = small_call(
        mlp_kernel,
        "mlp",
        [shape((lat_rows, width), F32), shape((lat_rows, width), F32)],
        *head_parts(self_part),
        lat_one,
        row(mlp_gain),
        mlp_w1,
        mlp_w2,
    )
    normed = small_call(
        last_kernel,
        "last",
        shape((chips, lat_rows, width), BF),
        *head_parts(mlp_part),
        lat_two,
        row(dec_gain),
    )
    own = trade(normed)
    return decode(
        core, queries, query_modality, modality_embed, own, other_core(own), dec_wkv, prepared
    )


def solution(mesh):
    placed = (
        P("inp", None),
        P("inp"),
        P(("inp", "head"), None),
        P(("inp", "head")),
        P(),
        P(),
        P(),
        P(),
        P(None, "head"),
        P(None, None, "head"),
        P(None, "head", None),
        P("head", None),
        P(),
        P(None, None, "head"),
        P("head", "inp", None),
        P("head", None),
        P(),
        P(None, "head"),
        P("head", None),
        P(),
        P(),
        P(),
        P(),
        P(),
        P(),
    )
    return jax.shard_map(
        body, mesh=mesh, in_specs=placed, out_specs=P(("inp", "head"), None), check_vma=False
    )
```

```python
import functools
import math

import jax
import jax.numpy as jnp
from jax import lax
from jax.experimental import pallas as pl
from jax.experimental.pallas import tpu as pltpu
from jax.sharding import PartitionSpec as P

HSZ = 64
MODS = 3
MBLK = 128
EPSILON = 1e-05
LOG2E = 1.4426950408889634
SCALE2 = LOG2E / math.sqrt(HSZ)
NEG_FLOOR = -1e30
BF = jnp.bfloat16
F32 = jnp.float32
MIB = 2**20
EXTRA = 128
SMALL_TOTAL = 2.0**-95


def dot(a, b):
    return jnp.dot(a, b, preferred_element_type=F32)


def dot_nt(a, b):
    return lax.dot_general(a, b, (((1,), (1,)), ((), ())), preferred_element_type=F32)


def layer_norm(values, gain):
    centered = values - jnp.mean(values, axis=-1, keepdims=True)
    variance = jnp.mean(centered * centered, axis=-1, keepdims=True)
    return centered * lax.rsqrt(variance + EPSILON) * gain


def three_parts(values):
    high = values.astype(BF)
    rest = values - high.astype(F32)
    mid = rest.astype(BF)
    low = (rest - mid.astype(F32)).astype(BF)
    return high.astype(F32), mid.astype(F32), low.astype(F32)


def bias_rows(bias, rows):
    index = lax.broadcasted_iota(jnp.int32, (rows, bias.shape[1]), 0)
    block = jnp.zeros((rows, bias.shape[1]), F32)
    for part, piece in enumerate(three_parts(bias)):
        for mod in range(MODS):
            block = jnp.where(index == MODS * part + mod, piece[mod : mod + 1, :], block)
    return block


def modality_hot(mod, shape, dim):
    index = lax.broadcasted_iota(jnp.int32, shape, dim)
    hit = (index == mod) | (index == mod + MODS) | (index == mod + 2 * MODS)
    return hit, index


def head_sums(count, lanes):
    row = lax.broadcasted_iota(jnp.int32, (count * HSZ, lanes), 0) // HSZ
    lane = lax.broadcasted_iota(jnp.int32, (count * HSZ, lanes), 1) // (lanes // count)
    return jnp.where(row == lane, 1.0, 0.0).astype(BF)


def embed_norm(mod_ref, first, b, x_ref, table_ref, gain):
    embedded = x_ref[b * MBLK : (b + 1) * MBLK, :].astype(F32)
    embedded = embedded + table_ref[pl.ds(mod_ref[first + b], 1), :]
    return layer_norm(embedded, gain).astype(BF)


def join_rows(core, own_ref, other_ref, all_ref):
    for held, refs in enumerate(((own_ref, other_ref), (other_ref, own_ref))):

        @pl.when(core == held)
        def _():
            for block in range(all_ref.shape[0] // 16):
                all_ref[block * 16 : block * 16 + 16, :] = refs[block % 2][block // 2]


def encode_kernel(
    heads,
    mod_ref,
    x_ref,
    next_ref,
    table_ref,
    gain_ref,
    lat_ref,
    lat_gain_ref,
    wq_ref,
    wkv_ref,
    bias_ref,
    out_ref,
    qx_ref,
    norm_ref,
    wvt_ref,
    n_ref,
    hot_ref,
    k_ref,
    vt_ref,
    p_ref,
    part_ref,
    shift_ref,
    m_ref,
    acc_ref,
):
    step = pl.program_id(0)
    last = pl.num_programs(0) - 1
    points = x_ref.shape[0]
    blocks = points // MBLK
    lat_count = lat_ref.shape[0]
    slot = lax.rem(step, 2)
    row16 = lax.broadcasted_iota(jnp.int32, (16, lat_count), 0)
    gain = gain_ref[...]

    def project(at, into):
        normed = n_ref[...]
        keys = dot(normed, wkv_ref[0])
        k_ref[into] = keys.astype(BF)
        vt_ref[into] = dot_nt(wvt_ref[...], normed).astype(BF)
        lengths = dot((keys * keys).astype(BF), head_sums(heads, 128))
        longest = jnp.sqrt(jnp.max(lengths, axis=0, keepdims=True))
        present = [jnp.bool_(False)] * MODS
        for b in range(blocks):
            mod = mod_ref[at * blocks + b]
            hit, index = modality_hot(mod, (MBLK, 128), 1)
            hit = jnp.where(hit | (index == 16), 1.0, 0.0)
            hot_ref[into, b * MBLK : (b + 1) * MBLK, :] = hit.astype(BF)
            present = [p | (mod == m) for m, p in enumerate(present)]
        for h in range(heads):
            bound = jnp.full((1, lat_count), NEG_FLOOR, F32)
            for m in range(MODS):
                held = jnp.where(present[m], bias_ref[m, h : h + 1, :] * LOG2E, NEG_FLOOR)
                bound = jnp.maximum(bound, held)
            lane = h * (128 // heads)
            bound = bound + norm_ref[h : h + 1, :] * longest[:, lane : lane + 1]
            shift_ref[into, h] = bound.astype(BF).astype(F32)

    @pl.when(step == 0)
    def _():
        normed = layer_norm(lat_ref[...], lat_gain_ref[...]).astype(BF)
        query = (dot(normed, wq_ref[...]) * SCALE2).T
        qx_ref[...] = jnp.zeros(qx_ref.shape, BF)
        for h in range(heads):
            half = (h % 2) * HSZ
            own = query[h * HSZ : (h + 1) * HSZ, :]
            qx_ref[h, half : half + HSZ, :] = own.astype(BF)
            qx_ref[h, 128:144, :] = bias_rows(bias_ref[:, h, :] * LOG2E, 16).astype(BF)
            norm_ref[h : h + 1, :] = jnp.sqrt(jnp.sum(own * own, axis=0, keepdims=True))
        wvt_ref[...] = wkv_ref[1].T
        m_ref[...] = jnp.full(m_ref.shape, NEG_FLOOR, F32)
        acc_ref[...] = jnp.zeros(acc_ref.shape, F32)
        for b in range(blocks):
            n_ref[b * MBLK : (b + 1) * MBLK, :] = embed_norm(
                mod_ref, 0, b, x_ref, table_ref, gain
            )
        project(0, 0)

    following = jnp.minimum(step + 1, last)

    def main(prepare):
        hot = hot_ref[slot]
        ones = jnp.ones((HSZ, points), BF)
        for h in range(heads):
            qx_ref[h, 144:160, :] = jnp.where(row16 == 0, -shift_ref[slot, h], 0.0).astype(BF)
        per_head = -(-blocks // 2)
        for h in range(heads + 1):
            if h < heads:
                pair = (h // 2) * 128
                left = jnp.concatenate([k_ref[slot, :, pair : pair + 128], hot], axis=1)
                p_ref[h % 2] = jnp.exp2(dot(left, qx_ref[h])).astype(BF)
            if h > 0:
                values_h = vt_ref[slot, (h - 1) * HSZ : h * HSZ, :]
                values_h = jnp.concatenate([values_h, ones], axis=0)
                part_ref[h - 1] = dot(values_h, p_ref[(h - 1) % 2])
            for b in range(h * per_head, min((h + 1) * per_head, blocks) if prepare else 0):
                n_ref[b * MBLK : (b + 1) * MBLK, :] = embed_norm(
                    mod_ref, following * blocks, b, next_ref, table_ref, gain
                )
            if h == 2 and prepare:
                project(following, 1 - slot)

    pl.when(step < last)(functools.partial(main, True))
    pl.when(step == last)(functools.partial(main, False))
    least = jnp.min(part_ref[:, HSZ : HSZ + 1, :])

    @pl.when(least < SMALL_TOTAL)
    def _():
        def exact(h, _):
            pair = pl.multiple_of((h // 2) * 128, 128)
            qx_ref[h, 144:160, :] = jnp.zeros((16, lat_count), BF)
            left = jnp.concatenate([k_ref[slot, :, pl.ds(pair, 128)], hot_ref[slot]], axis=1)
            scores = dot(left, qx_ref[h])
            top = jnp.max(scores, axis=0, keepdims=True)
            weights = jnp.exp2(scores - top).astype(BF)
            values_h = vt_ref[slot, pl.ds(pl.multiple_of(h * HSZ, HSZ), HSZ), :]
            values_h = jnp.concatenate([values_h, jnp.ones((HSZ, points), BF)], axis=0)
            part_ref[h] = dot(values_h, weights)
            shift_ref[slot, h] = top
            return 0

        lax.fori_loop(0, heads, exact, 0)

    for h in range(heads):
        old = m_ref[h]
        own = shift_ref[slot, h]
        new = jnp.maximum(old, own)
        m_ref[h] = new
        acc_ref[h] = acc_ref[h] * jnp.exp2(old - new) + part_ref[h] * jnp.exp2(own - new)

    @pl.when(step == last)
    def _():
        index = lax.broadcasted_iota(jnp.int32, (EXTRA, lat_count), 0)
        extra = jnp.zeros((EXTRA, lat_count), F32)
        pieces = []
        for h in range(heads):
            acc = acc_ref[h]
            total = acc[HSZ : HSZ + 1, :]
            pieces.append(acc[:HSZ, :] / total)
            for part, piece in enumerate(three_parts(m_ref[h] + jnp.log2(total))):
                extra = jnp.where(index == heads * part + h, piece, extra)
        out_ref[...] = jnp.concatenate(pieces + [extra], axis=0).T.astype(BF)


def encode(inputs, input_modality, table, gain, latents, lat_gain, wq, wkv, bias):
    points, width = inputs.shape
    heads = bias.shape[1]
    lat_count, lat_width = latents.shape
    cols = heads * HSZ
    tile = math.gcd(points, 2048)
    steps = points // tile
    whole = lambda *shape: pl.BlockSpec(shape, lambda i, *_: (0,) * len(shape))
    return pl.pallas_call(
        functools.partial(encode_kernel, heads),
        grid_spec=pltpu.PrefetchScalarGridSpec(
            num_scalar_prefetch=1,
            grid=(steps,),
            in_specs=[
                pl.BlockSpec((tile, width), lambda i, *_: (0, 0)),
                pl.BlockSpec((tile, width), lambda i, *_: (jnp.minimum(i + 1, steps - 1), 0)),
                whole(MODS, width),
                whole(1, width),
                whole(lat_count, lat_width),
                whole(1, lat_width),
                whole(lat_width, cols),
                whole(2, width, cols),
                whole(MODS, heads, lat_count),
            ],
            out_specs=whole(lat_count, cols + EXTRA),
            scratch_shapes=[
                pltpu.VMEM((heads, 256, lat_count), BF),
                pltpu.VMEM((heads, lat_count), F32),
                pltpu.VMEM((cols, width), BF),
                pltpu.VMEM((tile, width), BF),
                pltpu.VMEM((2, tile, 128), BF),
                pltpu.VMEM((2, tile, cols), BF),
                pltpu.VMEM((2, cols, tile), BF),
                pltpu.VMEM((2, tile, lat_count), BF),
                pltpu.VMEM((heads, 128, lat_count), F32),
                pltpu.VMEM((2, heads, 1, lat_count), F32),
                pltpu.VMEM((heads, 1, lat_count), F32),
                pltpu.VMEM((heads, 128, lat_count), F32),
            ],
        ),
        out_shape=jax.ShapeDtypeStruct((lat_count, cols + EXTRA), BF),
        compiler_params=pltpu.CompilerParams(vmem_limit_bytes=58 * MIB),
        cost_estimate=pl.CostEstimate(
            flops=2 * points * lat_count * heads * (256 + 128),
            transcendentals=points * lat_count * heads,
            bytes_accessed=2 * inputs.nbytes + latents.nbytes + wq.nbytes + wkv.nbytes,
        ),
        name="encode",
    )(input_modality, inputs, inputs, table, gain, latents, lat_gain, wq, wkv, bias)


def small_call(kernel, name, outs, *args, scratch=(), streamed=None):
    def space(a):
        if a is streamed:
            return pltpu.HBM
        return pltpu.SMEM if a.dtype == jnp.int32 else pltpu.VMEM

    if streamed is not None:
        scratch = (pltpu.VMEM(streamed.shape, streamed.dtype), pltpu.SemaphoreType.DMA(()))
        far = pltpu.with_memory_space_constraint(streamed, pltpu.HBM)
        args = [far if a is streamed else a for a in args]
        streamed = far
    return pl.pallas_call(
        kernel,
        out_shape=outs,
        in_specs=[pl.BlockSpec(memory_space=space(a)) for a in args],
        scratch_shapes=list(scratch),
        out_specs=jax.tree.map(lambda _: pl.BlockSpec(memory_space=pltpu.VMEM), outs),
        compiler_params=pltpu.CompilerParams(vmem_limit_bytes=14 * MIB),
        name=name,
    )(*args)


def log_totals(heads, extra):
    lse = extra[..., :heads]
    for part in range(1, 3):
        lse = lse + extra[..., heads * part : heads * (part + 1)]
    return lse


def per_head(heads, factor, shape):
    lane = lax.broadcasted_iota(jnp.int32, shape, len(shape) - 1) // HSZ
    spread = jnp.zeros(shape, F32)
    for h in range(heads):
        spread = jnp.where(lane == h, factor[..., h : h + 1], spread)
    return spread


def merge_kernel(heads, part_ref, wo_ref, out_ref):
    cols = heads * HSZ
    lse = log_totals(heads, part_ref[:, :, cols:].astype(F32))
    factor = jnp.exp2(lse - jnp.max(lse, axis=0, keepdims=True))
    factor = factor / jnp.sum(factor, axis=0, keepdims=True)
    spread = per_head(heads, factor, part_ref.shape[:2] + (cols,))
    attended = jnp.sum(part_ref[:, :, :cols].astype(F32) * spread, axis=0)
    out_ref[...] = dot(attended.astype(BF), wo_ref[...]).astype(BF)


def added(*refs):
    a, b, c, d = [ref[...].astype(F32) for ref in refs]
    return (a + b) + (c + d)


def project_kernel(
    a_ref, b_ref, c_ref, d_ref, lat_ref, gain_ref, far_ref, lat_out, q_out, kv_out, w_ref, sem
):
    copy = pltpu.make_async_copy(far_ref, w_ref, sem)
    copy.start()
    lat = lat_ref[...] + added(a_ref, b_ref, c_ref, d_ref)
    lat_out[...] = lat
    normed = layer_norm(lat, gain_ref[...]).astype(BF)
    cols = w_ref.shape[2]
    copy.wait()
    q_out[...] = (dot(normed, w_ref[0]) * SCALE2).astype(BF)
    keys = dot(normed, w_ref[1]).astype(BF)
    values = dot(normed, w_ref[2]).astype(BF)
    for copy in range(kv_out.shape[0]):
        kv_out[copy, :, :cols] = keys
        kv_out[copy, :, cols:] = values


def attend_kernel(heads, core_ref, q_ref, own_ref, other_ref, bias_ref, wo_ref, out_ref, kv_ref):
    join_rows(core_ref[0], own_ref, other_ref, kv_ref)
    cols = heads * HSZ
    query = q_ref[...]
    rows = query.shape[0]
    keys = kv_ref[:, :cols]
    values = kv_ref[:, cols:]
    lane = lax.broadcasted_iota(jnp.int32, (rows, cols), 1) // HSZ
    mixed = jnp.zeros((rows, cols), F32)
    for h in range(heads):
        own = jnp.where(lane == h, query.astype(F32), 0.0).astype(BF)
        scores = dot_nt(own, keys) + bias_ref[h] * LOG2E
        weights = jnp.exp2(scores - jnp.max(scores, axis=1, keepdims=True))
        total = jnp.sum(weights, axis=1, keepdims=True)
        mixed = jnp.where(lane == h, dot(weights.astype(BF), values) / total, mixed)
    out_ref[...] = dot(mixed.astype(BF), wo_ref[...]).astype(BF)


def mlp_kernel(
    a_ref, b_ref, c_ref, d_ref, lat_ref, gain_ref, w1_ref, far_ref, lat_out, out_ref, w2_ref, sem
):
    copy = pltpu.make_async_copy(far_ref, w2_ref, sem)
    copy.start()
    lat = lat_ref[...] + added(a_ref, b_ref, c_ref, d_ref)
    lat_out[...] = lat
    normed = layer_norm(lat, gain_ref[...]).astype(BF)
    hidden = jax.nn.gelu(dot(normed, w1_ref[...]), approximate=True).astype(BF)
    copy.wait()
    out_ref[...] = dot(hidden, w2_ref[...]).astype(BF)


def last_kernel(a_ref, b_ref, c_ref, d_ref, lat_ref, gain_ref, out_ref):
    lat = lat_ref[...] + added(a_ref, b_ref, c_ref, d_ref)
    normed = layer_norm(lat, gain_ref[...]).astype(BF)
    for copy in range(out_ref.shape[0]):
        out_ref[copy] = normed


def query_kernel(
    heads,
    mod_ref,
    x_ref,
    table_ref,
    gain_ref,
    wq_ref,
    bias_ref,
    wo_ref,
    qt_ref,
    norm_ref,
    top_ref,
    bias_out,
    wot_ref,
    wqt_ref,
    bmax_ref,
    n_ref,
):
    step = pl.program_id(0)
    blocks = x_ref.shape[0] // MBLK
    lat_count = bias_ref.shape[2]

    @pl.when(step == 0)
    def _():
        wqt_ref[...] = wq_ref[...].T
        wot_ref[...] = wo_ref[...].T
        row = lax.broadcasted_iota(jnp.int32, (16, lat_count), 0)
        for part in range(heads // 8):
            block = []
            for h in range(8 * part, 8 * part + 8):
                rows = bias_rows(bias_ref[:, h, :] * LOG2E, 16)
                block.append(jnp.where(row == 3 * MODS + part, 1.0, rows))
            bias_out[part] = jnp.concatenate(block, axis=0).T.astype(BF)
        for m in range(MODS):
            top = jnp.max(bias_ref[m] * LOG2E, axis=1, keepdims=True)
            bmax_ref[m] = jnp.broadcast_to(top, (heads, MBLK))

    for b in range(blocks):
        n_ref[b * MBLK : (b + 1) * MBLK, :] = embed_norm(
            mod_ref, step * blocks, b, x_ref, table_ref, gain_ref[...]
        )
        mod = mod_ref[step * blocks + b]
        top_ref[:, b * MBLK : (b + 1) * MBLK] = bmax_ref[mod]
    query = dot_nt(wqt_ref[...], n_ref[...]) * SCALE2
    qt_ref[...] = query.astype(BF)
    for h in range(heads):
        own = query[h * HSZ : (h + 1) * HSZ, :]
        norm_ref[h : h + 1, :] = jnp.sqrt(jnp.sum(own * own, axis=0, keepdims=True))


def prepare_queries(queries, query_modality, table, gain, wq, bias, wo):
    count, width = queries.shape
    heads, lat_count = bias.shape[1:]
    cols = heads * HSZ
    tile = math.gcd(count, 512)
    whole = lambda *shape: pl.BlockSpec(shape, lambda i, mod: (0,) * len(shape))
    tiled = lambda rows: pl.BlockSpec((rows, tile), lambda i, mod: (0, i))
    return pl.pallas_call(
        functools.partial(query_kernel, heads),
        grid_spec=pltpu.PrefetchScalarGridSpec(
            num_scalar_prefetch=1,
            grid=(count // tile,),
            in_specs=[
                pl.BlockSpec((tile, width), lambda i, mod: (i, 0)),
                whole(MODS, width),
                whole(1, width),
                whole(width, cols),
                whole(MODS, heads, lat_count),
                whole(cols, width),
            ],
            out_specs=[
                tiled(cols),
                tiled(heads),
                tiled(heads),
                whole(heads // 8, lat_count, 128),
                whole(width, cols),
            ],
            scratch_shapes=[
                pltpu.VMEM((cols, width), BF),
                pltpu.VMEM((MODS, heads, MBLK), F32),
                pltpu.VMEM((tile, width), BF),
            ],
        ),
        out_shape=[
            jax.ShapeDtypeStruct((cols, count), BF),
            jax.ShapeDtypeStruct((heads, count), F32),
            jax.ShapeDtypeStruct((heads, count), F32),
            jax.ShapeDtypeStruct((heads // 8, lat_count, 128), BF),
            jax.ShapeDtypeStruct((width, cols), BF),
        ],
        compiler_params=pltpu.CompilerParams(vmem_limit_bytes=58 * MIB),
        cost_estimate=pl.CostEstimate(
            flops=2 * count * width * cols,
            transcendentals=count * heads,
            bytes_accessed=queries.nbytes + wq.nbytes + wo.nbytes + 2 * count * cols,
        ),
        name="queries",
    )(query_modality, queries, table, gain, wq, bias, wo)


def decode_kernel(
    heads,
    mod_ref,
    core_ref,
    x_ref,
    table_ref,
    own_ref,
    other_ref,
    wkv_ref,
    bias_ref,
    qt_ref,
    norm_ref,
    top_ref,
    wot_ref,
    out_ref,
    lat_ref,
    kx_ref,
    vx_ref,
    long_ref,
    hot_ref,
    p_ref,
    mix_ref,
):
    step = pl.program_id(0)
    tile = x_ref.shape[0]
    blocks = tile // MBLK
    lat_count = lat_ref.shape[0]

    @pl.when(step == 0)
    def _():
        join_rows(core_ref[0], own_ref, other_ref, lat_ref)
        normed = lat_ref[...]
        ones = jnp.ones((HSZ, lat_count), BF)
        lane = lax.broadcasted_iota(jnp.int32, (lat_count, 128), 1)
        sums = head_sums(4, 128)
        for quad in range(heads // 4):
            cols = slice(quad * 256, (quad + 1) * 256)
            keys = dot(normed, wkv_ref[0, :, cols])
            values = dot(normed, wkv_ref[1, :, cols]).astype(BF).T
            lengths = dot((keys * keys).astype(BF), sums)
            longest = jnp.sqrt(jnp.max(lengths, axis=0, keepdims=True))
            for at in range(4):
                h = 4 * quad + at
                pair = keys[:, at // 2 * 128 : at // 2 * 128 + 128]
                kx_ref[h, :, :128] = jnp.where(lane // HSZ == at % 2, pair, 0.0).astype(BF)
                extra = jnp.where(lane // 16 == h % 8, bias_ref[h // 8].astype(F32), 0.0)
                kx_ref[h, :, 128:] = extra.astype(BF)
                vx_ref[h, :HSZ, :] = values[at * HSZ : (at + 1) * HSZ, :]
                vx_ref[h, HSZ:, :] = ones
                long_ref[h : h + 1, :] = jnp.broadcast_to(
                    longest[:, at * 32 : at * 32 + 1], (1, 128)
                )

    bound = norm_ref[...] * long_ref[:, :1] + top_ref[...]
    row = lax.broadcasted_iota(jnp.int32, (16, MBLK), 0)
    for b in range(blocks):
        hit, _ = modality_hot(mod_ref[step * blocks + b], (16, MBLK), 0)
        onehot = jnp.where(hit, 1.0, 0.0)
        lanes = slice(b * MBLK, (b + 1) * MBLK)
        for group in range(8):
            rows = onehot
            for part in range(heads // 8):
                own = bound[8 * part + group : 8 * part + group + 1, lanes]
                rows = jnp.where(row == 3 * MODS + part, -own, rows)
            hot_ref[16 * group : 16 * group + 16, lanes] = rows.astype(BF)
    hot = hot_ref[...]
    least = jnp.full((1, tile), 1.0, F32)
    for h in range(heads + 1):
        if h < heads:
            pair = (h // 2) * 128
            right = jnp.concatenate([qt_ref[pair : pair + 128, :], hot], axis=0)
            p_ref[h % 2] = jnp.exp2(dot(kx_ref[h], right)).astype(BF)
        if h > 0:
            mixed = dot(vx_ref[h - 1], p_ref[(h - 1) % 2])
            least = jnp.minimum(least, mixed[HSZ : HSZ + 1, :])
            mix_ref[(h - 1) * HSZ : h * HSZ, :] = (mixed[:HSZ, :] / mixed[HSZ:, :]).astype(BF)

    @pl.when(jnp.min(least) < SMALL_TOTAL)
    def _():
        for b in range(blocks):
            hit, _ = modality_hot(mod_ref[step * blocks + b], (16, MBLK), 0)
            onehot = jnp.where(hit, 1.0, 0.0).astype(BF)
            for group in range(8):
                hot_ref[16 * group : 16 * group + 16, b * MBLK : (b + 1) * MBLK] = onehot

        def exact(h, _):
            pair = pl.multiple_of((h // 2) * 128, 128)
            right = jnp.concatenate([qt_ref[pl.ds(pair, 128), :], hot_ref[...]], axis=0)
            scores = dot(kx_ref[h], right)
            top = jnp.max(scores, axis=0, keepdims=True)
            mixed = dot(vx_ref[h], jnp.exp2(scores - top).astype(BF))
            mixed = (mixed[:HSZ, :] / mixed[HSZ:, :]).astype(BF)
            mix_ref[pl.ds(pl.multiple_of(h * HSZ, HSZ), HSZ), :] = mixed
            return 0

        lax.fori_loop(0, heads, exact, 0)

    decoded = dot(wot_ref[...], mix_ref[...]).T
    for b in range(blocks):
        rows = slice(b * MBLK, (b + 1) * MBLK)
        mod = mod_ref[step * blocks + b]
        embedded = x_ref[rows, :].astype(F32) + table_ref[pl.ds(mod, 1), :]
        out_ref[rows, :] = embedded + decoded[rows, :]


def decode(core, queries, query_modality, table, own, other, wkv, prepared):
    queries_t, norms, tops, bias, wo_t = prepared
    count, width = queries.shape
    lat_count = bias.shape[1]
    cols = queries_t.shape[0]
    heads = cols // HSZ
    tile = math.gcd(count, 512)
    lat_width = wkv.shape[1]
    held = pl.BlockSpec(memory_space=pltpu.VMEM)
    tiled = lambda rows: pl.BlockSpec((rows, tile), lambda i, *_: (0, i))
    return pl.pallas_call(
        functools.partial(decode_kernel, heads),
        grid_spec=pltpu.PrefetchScalarGridSpec(
            num_scalar_prefetch=2,
            grid=(count // tile,),
            in_specs=[
                pl.BlockSpec((tile, width), lambda i, *_: (i, 0)),
                held,
                held,
                held,
                held,
                held,
                tiled(cols),
                tiled(heads),
                tiled(heads),
                held,
            ],
            out_specs=pl.BlockSpec((tile, width), lambda i, *_: (i, 0)),
            scratch_shapes=[
                pltpu.VMEM((lat_count, lat_width), BF),
                pltpu.VMEM((heads, lat_count, 256), BF),
                pltpu.VMEM((heads, 128, lat_count), BF),
                pltpu.VMEM((heads, 128), F32),
                pltpu.VMEM((128, tile), BF),
                pltpu.VMEM((2, lat_count, tile), BF),
                pltpu.VMEM((cols, tile), BF),
            ],
        ),
        out_shape=jax.ShapeDtypeStruct((count, width), F32),
        compiler_params=pltpu.CompilerParams(vmem_limit_bytes=32 * MIB),
        cost_estimate=pl.CostEstimate(
            flops=2 * count * lat_count * heads * (256 + 128) + 2 * count * width * cols,
            transcendentals=count * lat_count * heads,
            bytes_accessed=queries.nbytes + wkv.nbytes + queries_t.nbytes + 4 * queries.size,
        ),
        name="decode",
    )(query_modality, core, queries, table, own, other, wkv, bias, queries_t, norms, tops, wo_t)


def trade(parts):
    size = lax.axis_size("inp")
    groups = [list(range(core, size, 2)) for core in range(2)]
    return lax.all_to_all(parts, "inp", 0, 0, axis_index_groups=groups)


def other_core(rows):
    return lax.ppermute(rows, "inp", [(i, i ^ 1) for i in range(lax.axis_size("inp"))])


def head_parts(part):
    size = lax.axis_size("head")
    moved = [
        lax.ppermute(part, "head", [(i, (i + k) % size) for i in range(size)])
        for k in range(1, size)
    ]
    return [part] + moved


def body(
    inputs,
    input_modality,
    queries,
    query_modality,
    modality_embed,
    latents,
    ln_in_gain,
    ln_lat_gain,
    enc_wq,
    enc_wkv,
    enc_bias,
    enc_wo,
    self_gain,
    self_wqkv,
    self_bias,
    self_wo,
    mlp_gain,
    mlp_w1,
    mlp_w2,
    dec_gain,
    dec_wkv,
    query_gain,
    dec_wq,
    dec_bias,
    dec_wo,
):
    lat_count, width = latents.shape
    lat_rows = lat_count // lax.axis_size("inp")
    row_first = lax.axis_index("inp") * lat_rows
    heads = enc_bias.shape[1]
    cols = heads * HSZ
    row = lambda v: v.reshape(1, -1)
    shape = jax.ShapeDtypeStruct

    core = (lax.axis_index("inp") % 2).astype(jnp.int32).reshape(1)
    chips = lax.axis_size("inp") // 2
    partial = encode(
        inputs,
        input_modality,
        modality_embed,
        row(ln_in_gain),
        latents,
        row(ln_lat_gain),
        enc_wq,
        enc_wkv,
        enc_bias,
    )
    partial, early = lax.optimization_barrier((partial, queries))
    parts = lax.all_to_all(partial.reshape(-1, lat_rows, partial.shape[1]), "inp", 0, 0)
    prepared = prepare_queries(
        early, query_modality, modality_embed, row(query_gain), dec_wq, dec_bias, dec_wo
    )
    parts, prepared = lax.optimization_barrier((parts, prepared))
    enc_part = small_call(
        functools.partial(merge_kernel, heads), "merge", shape((lat_rows, width), BF), parts, enc_wo
    )
    latent_rows = lax.dynamic_slice_in_dim(latents, row_first, lat_rows, 0)
    lat_one, self_q, self_kv = small_call(
        project_kernel,
        "project",
        [
            shape((lat_rows, width), F32),
            shape((lat_rows, cols), BF),
            shape((chips, lat_rows, 2 * cols), BF),
        ],
        *head_parts(enc_part),
        latent_rows,
        row(self_gain),
        self_wqkv,
        streamed=self_wqkv,
    )
    own_kv = trade(self_kv)
    self_part = small_call(
        functools.partial(attend_kernel, heads),
        "attend",
        shape((lat_rows, width), BF),
        core,
        self_q,
        own_kv,
        other_core(own_kv),
        self_bias,
        self_wo,
        scratch=[pltpu.VMEM((lat_count, 2 * cols), BF)],
    )
    lat_two, mlp_part = small_call(
        mlp_kernel,
        "mlp",
        [shape((lat_rows, width), F32), shape((lat_rows, width), BF)],
        *head_parts(self_part),
        lat_one,
        row(mlp_gain),
        mlp_w1,
        mlp_w2,
        streamed=mlp_w2,
    )
    normed = small_call(
        last_kernel,
        "last",
        shape((chips, lat_rows, width), BF),
        *head_parts(mlp_part),
        lat_two,
        row(dec_gain),
    )
    own = trade(normed)
    prepared = (pltpu.with_memory_space_constraint(prepared[0], pltpu.HBM), *prepared[1:])
    return decode(
        core, queries, query_modality, modality_embed, own, other_core(own), dec_wkv, prepared
    )


def solution(mesh):
    placed = (
        P("inp", None),
        P("inp"),
        P(("inp", "head"), None),
        P(("inp", "head")),
        P(),
        P(),
        P(),
        P(),
        P(None, "head"),
        P(None, None, "head"),
        P(None, "head", None),
        P("head", None),
        P(),
        P(None, None, "head"),
        P("head", "inp", None),
        P("head", None),
        P(),
        P(None, "head"),
        P("head", None),
        P(),
        P(),
        P(),
        P(),
        P(),
        P(),
    )
    return jax.shard_map(
        body, mesh=mesh, in_specs=placed, out_specs=P(("inp", "head"), None), check_vma=False
    )
```

```python
import functools
import math

import jax
import jax.numpy as jnp
from jax import lax
from jax.experimental import pallas as pl
from jax.experimental.pallas import tpu as pltpu
from jax.sharding import PartitionSpec as P

HSZ = 64
MODS = 3
MBLK = 128
EPSILON = 1e-05
LOG2E = 1.4426950408889634
SCALE2 = LOG2E / math.sqrt(HSZ)
NEG_FLOOR = -1e30
BF = jnp.bfloat16
F32 = jnp.float32
MIB = 2**20
EXTRA = 128
SMALL_TOTAL = 2.0**-95


def dot(a, b):
    return jnp.dot(a, b, preferred_element_type=F32)


def dot_nt(a, b):
    return lax.dot_general(a, b, (((1,), (1,)), ((), ())), preferred_element_type=F32)


def layer_norm(values, gain):
    centered = values - jnp.mean(values, axis=-1, keepdims=True)
    variance = jnp.mean(centered * centered, axis=-1, keepdims=True)
    return centered * lax.rsqrt(variance + EPSILON) * gain


def three_parts(values):
    high = values.astype(BF)
    rest = values - high.astype(F32)
    mid = rest.astype(BF)
    low = (rest - mid.astype(F32)).astype(BF)
    return high.astype(F32), mid.astype(F32), low.astype(F32)


def bias_rows(bias, rows):
    index = lax.broadcasted_iota(jnp.int32, (rows, bias.shape[1]), 0)
    block = jnp.zeros((rows, bias.shape[1]), F32)
    for part, piece in enumerate(three_parts(bias)):
        for mod in range(MODS):
            block = jnp.where(index == MODS * part + mod, piece[mod : mod + 1, :], block)
    return block


def modality_hot(mod, shape, dim):
    index = lax.broadcasted_iota(jnp.int32, shape, dim)
    hit = (index == mod) | (index == mod + MODS) | (index == mod + 2 * MODS)
    return hit, index


def head_sums(count, lanes):
    row = lax.broadcasted_iota(jnp.int32, (count * HSZ, lanes), 0) // HSZ
    lane = lax.broadcasted_iota(jnp.int32, (count * HSZ, lanes), 1) // (lanes // count)
    return jnp.where(row == lane, 1.0, 0.0).astype(BF)


def embed_norm(mod_ref, first, b, x_ref, table_ref, gain):
    embedded = x_ref[b * MBLK : (b + 1) * MBLK, :].astype(F32)
    embedded = embedded + table_ref[pl.ds(mod_ref[first + b], 1), :]
    return layer_norm(embedded, gain).astype(BF)


def join_rows(core, own_ref, other_ref, all_ref):
    for held, refs in enumerate(((own_ref, other_ref), (other_ref, own_ref))):

        @pl.when(core == held)
        def _():
            for block in range(all_ref.shape[0] // 16):
                all_ref[block * 16 : block * 16 + 16, :] = refs[block % 2][block // 2]


def encode_kernel(
    heads,
    mod_ref,
    x_ref,
    next_ref,
    table_ref,
    gain_ref,
    lat_ref,
    lat_gain_ref,
    wq_ref,
    wkv_ref,
    bias_ref,
    out_ref,
    qx_ref,
    norm_ref,
    wvt_ref,
    n_ref,
    hot_ref,
    k_ref,
    vt_ref,
    p_ref,
    part_ref,
    shift_ref,
    m_ref,
    acc_ref,
):
    step = pl.program_id(0)
    last = pl.num_programs(0) - 1
    points = x_ref.shape[0]
    blocks = points // MBLK
    lat_count = lat_ref.shape[0]
    slot = lax.rem(step, 2)
    row16 = lax.broadcasted_iota(jnp.int32, (16, lat_count), 0)
    gain = gain_ref[...]

    def project(at, into):
        normed = n_ref[...]
        keys = dot(normed, wkv_ref[0])
        k_ref[into] = keys.astype(BF)
        vt_ref[into] = dot_nt(wvt_ref[...], normed).astype(BF)
        lengths = dot((keys * keys).astype(BF), head_sums(heads, 128))
        longest = jnp.sqrt(jnp.max(lengths, axis=0, keepdims=True))
        present = [jnp.bool_(False)] * MODS
        for b in range(blocks):
            mod = mod_ref[at * blocks + b]
            hit, index = modality_hot(mod, (MBLK, 128), 1)
            hit = jnp.where(hit | (index == 16), 1.0, 0.0)
            hot_ref[into, b * MBLK : (b + 1) * MBLK, :] = hit.astype(BF)
            present = [p | (mod == m) for m, p in enumerate(present)]
        for h in range(heads):
            bound = jnp.full((1, lat_count), NEG_FLOOR, F32)
            for m in range(MODS):
                held = jnp.where(present[m], bias_ref[m, h : h + 1, :] * LOG2E, NEG_FLOOR)
                bound = jnp.maximum(bound, held)
            lane = h * (128 // heads)
            bound = bound + norm_ref[h : h + 1, :] * longest[:, lane : lane + 1]
            shift_ref[into, h] = bound.astype(BF).astype(F32)

    @pl.when(step == 0)
    def _():
        normed = layer_norm(lat_ref[...], lat_gain_ref[...]).astype(BF)
        query = (dot(normed, wq_ref[...]) * SCALE2).T
        qx_ref[...] = jnp.zeros(qx_ref.shape, BF)
        for h in range(heads):
            half = (h % 2) * HSZ
            own = query[h * HSZ : (h + 1) * HSZ, :]
            qx_ref[h, half : half + HSZ, :] = own.astype(BF)
            qx_ref[h, 128:144, :] = bias_rows(bias_ref[:, h, :] * LOG2E, 16).astype(BF)
            norm_ref[h : h + 1, :] = jnp.sqrt(jnp.sum(own * own, axis=0, keepdims=True))
        wvt_ref[...] = wkv_ref[1].T
        m_ref[...] = jnp.full(m_ref.shape, NEG_FLOOR, F32)
        acc_ref[...] = jnp.zeros(acc_ref.shape, F32)
        for b in range(blocks):
            n_ref[b * MBLK : (b + 1) * MBLK, :] = embed_norm(
                mod_ref, 0, b, x_ref, table_ref, gain
            )
        project(0, 0)

    following = jnp.minimum(step + 1, last)

    def main(prepare):
        hot = hot_ref[slot]
        ones = jnp.ones((HSZ, points), BF)
        for h in range(heads):
            qx_ref[h, 144:160, :] = jnp.where(row16 == 0, -shift_ref[slot, h], 0.0).astype(BF)
        per_head = -(-blocks // 2)
        for h in range(heads + 1):
            if h < heads:
                pair = (h // 2) * 128
                left = jnp.concatenate([k_ref[slot, :, pair : pair + 128], hot], axis=1)
                p_ref[h % 2] = jnp.exp2(dot(left, qx_ref[h])).astype(BF)
            if h > 0:
                values_h = vt_ref[slot, (h - 1) * HSZ : h * HSZ, :]
                values_h = jnp.concatenate([values_h, ones], axis=0)
                part_ref[h - 1] = dot(values_h, p_ref[(h - 1) % 2])
            for b in range(h * per_head, min((h + 1) * per_head, blocks) if prepare else 0):
                n_ref[b * MBLK : (b + 1) * MBLK, :] = embed_norm(
                    mod_ref, following * blocks, b, next_ref, table_ref, gain
                )
            if h == 2 and prepare:
                project(following, 1 - slot)

    pl.when(step < last)(functools.partial(main, True))
    pl.when(step == last)(functools.partial(main, False))
    least = jnp.min(part_ref[:, HSZ : HSZ + 1, :])

    @pl.when(least < SMALL_TOTAL)
    def _():
        def exact(h, _):
            pair = pl.multiple_of((h // 2) * 128, 128)
            qx_ref[h, 144:160, :] = jnp.zeros((16, lat_count), BF)
            left = jnp.concatenate([k_ref[slot, :, pl.ds(pair, 128)], hot_ref[slot]], axis=1)
            scores = dot(left, qx_ref[h])
            top = jnp.max(scores, axis=0, keepdims=True)
            weights = jnp.exp2(scores - top).astype(BF)
            values_h = vt_ref[slot, pl.ds(pl.multiple_of(h * HSZ, HSZ), HSZ), :]
            values_h = jnp.concatenate([values_h, jnp.ones((HSZ, points), BF)], axis=0)
            part_ref[h] = dot(values_h, weights)
            shift_ref[slot, h] = top
            return 0

        lax.fori_loop(0, heads, exact, 0)

    for h in range(heads):
        old = m_ref[h]
        own = shift_ref[slot, h]
        new = jnp.maximum(old, own)
        m_ref[h] = new
        acc_ref[h] = acc_ref[h] * jnp.exp2(old - new) + part_ref[h] * jnp.exp2(own - new)

    @pl.when(step == last)
    def _():
        index = lax.broadcasted_iota(jnp.int32, (EXTRA, lat_count), 0)
        extra = jnp.zeros((EXTRA, lat_count), F32)
        pieces = []
        for h in range(heads):
            acc = acc_ref[h]
            total = acc[HSZ : HSZ + 1, :]
            pieces.append(acc[:HSZ, :] / total)
            for part, piece in enumerate(three_parts(m_ref[h] + jnp.log2(total))):
                extra = jnp.where(index == heads * part + h, piece, extra)
        out_ref[...] = jnp.concatenate(pieces + [extra], axis=0).T.astype(BF)


def encode(inputs, input_modality, table, gain, latents, lat_gain, wq, wkv, bias):
    points, width = inputs.shape
    heads = bias.shape[1]
    lat_count, lat_width = latents.shape
    cols = heads * HSZ
    tile = math.gcd(points, 2048)
    steps = points // tile
    whole = lambda *shape: pl.BlockSpec(shape, lambda i, *_: (0,) * len(shape))
    return pl.pallas_call(
        functools.partial(encode_kernel, heads),
        grid_spec=pltpu.PrefetchScalarGridSpec(
            num_scalar_prefetch=1,
            grid=(steps,),
            in_specs=[
                pl.BlockSpec((tile, width), lambda i, *_: (0, 0)),
                pl.BlockSpec((tile, width), lambda i, *_: (jnp.minimum(i + 1, steps - 1), 0)),
                whole(MODS, width),
                whole(1, width),
                whole(lat_count, lat_width),
                whole(1, lat_width),
                whole(lat_width, cols),
                whole(2, width, cols),
                whole(MODS, heads, lat_count),
            ],
            out_specs=whole(lat_count, cols + EXTRA),
            scratch_shapes=[
                pltpu.VMEM((heads, 256, lat_count), BF),
                pltpu.VMEM((heads, lat_count), F32),
                pltpu.VMEM((cols, width), BF),
                pltpu.VMEM((tile, width), BF),
                pltpu.VMEM((2, tile, 128), BF),
                pltpu.VMEM((2, tile, cols), BF),
                pltpu.VMEM((2, cols, tile), BF),
                pltpu.VMEM((2, tile, lat_count), BF),
                pltpu.VMEM((heads, 128, lat_count), F32),
                pltpu.VMEM((2, heads, 1, lat_count), F32),
                pltpu.VMEM((heads, 1, lat_count), F32),
                pltpu.VMEM((heads, 128, lat_count), F32),
            ],
        ),
        out_shape=jax.ShapeDtypeStruct((lat_count, cols + EXTRA), BF),
        compiler_params=pltpu.CompilerParams(vmem_limit_bytes=58 * MIB),
        cost_estimate=pl.CostEstimate(
            flops=2 * points * lat_count * heads * (256 + 128),
            transcendentals=points * lat_count * heads,
            bytes_accessed=2 * inputs.nbytes + latents.nbytes + wq.nbytes + wkv.nbytes,
        ),
        name="encode",
    )(input_modality, inputs, inputs, table, gain, latents, lat_gain, wq, wkv, bias)


def small_call(kernel, name, outs, *args, scratch=()):
    space = lambda a: pltpu.SMEM if a.dtype == jnp.int32 else pltpu.VMEM
    return pl.pallas_call(
        kernel,
        out_shape=outs,
        in_specs=[pl.BlockSpec(memory_space=space(a)) for a in args],
        scratch_shapes=list(scratch),
        out_specs=jax.tree.map(lambda _: pl.BlockSpec(memory_space=pltpu.VMEM), outs),
        compiler_params=pltpu.CompilerParams(vmem_limit_bytes=14 * MIB),
        name=name,
    )(*args)


def log_totals(heads, extra):
    lse = extra[..., :heads]
    for part in range(1, 3):
        lse = lse + extra[..., heads * part : heads * (part + 1)]
    return lse


def per_head(heads, factor, shape):
    lane = lax.broadcasted_iota(jnp.int32, shape, len(shape) - 1) // HSZ
    spread = jnp.zeros(shape, F32)
    for h in range(heads):
        spread = jnp.where(lane == h, factor[..., h : h + 1], spread)
    return spread


def merge_kernel(heads, part_ref, wo_ref, out_ref):
    cols = heads * HSZ
    lse = log_totals(heads, part_ref[:, :, cols:].astype(F32))
    factor = jnp.exp2(lse - jnp.max(lse, axis=0, keepdims=True))
    factor = factor / jnp.sum(factor, axis=0, keepdims=True)
    spread = per_head(heads, factor, part_ref.shape[:2] + (cols,))
    attended = jnp.sum(part_ref[:, :, :cols].astype(F32) * spread, axis=0)
    out_ref[...] = dot(attended.astype(BF), wo_ref[...]).astype(BF)


def added(*refs):
    a, b, c, d = [ref[...].astype(F32) for ref in refs]
    return (a + b) + (c + d)


def project_kernel(a_ref, b_ref, c_ref, d_ref, lat_ref, gain_ref, w_ref, lat_out, q_out, kv_out):
    lat = lat_ref[...] + added(a_ref, b_ref, c_ref, d_ref)
    lat_out[...] = lat
    normed = layer_norm(lat, gain_ref[...]).astype(BF)
    cols = w_ref.shape[2]
    q_out[...] = (dot(normed, w_ref[0]) * SCALE2).astype(BF)
    keys = dot(normed, w_ref[1]).astype(BF)
    values = dot(normed, w_ref[2]).astype(BF)
    for copy in range(kv_out.shape[0]):
        kv_out[copy, :, :cols] = keys
        kv_out[copy, :, cols:] = values


def attend_kernel(heads, core_ref, q_ref, own_ref, other_ref, bias_ref, wo_ref, out_ref, kv_ref):
    join_rows(core_ref[0], own_ref, other_ref, kv_ref)
    cols = heads * HSZ
    query = q_ref[...]
    rows = query.shape[0]
    keys = kv_ref[:, :cols]
    values = kv_ref[:, cols:]
    lane = lax.broadcasted_iota(jnp.int32, (rows, cols), 1) // HSZ
    mixed = jnp.zeros((rows, cols), F32)
    for h in range(heads):
        own = jnp.where(lane == h, query.astype(F32), 0.0).astype(BF)
        scores = dot_nt(own, keys) + bias_ref[h] * LOG2E
        weights = jnp.exp2(scores - jnp.max(scores, axis=1, keepdims=True))
        total = jnp.sum(weights, axis=1, keepdims=True)
        mixed = jnp.where(lane == h, dot(weights.astype(BF), values) / total, mixed)
    out_ref[...] = dot(mixed.astype(BF), wo_ref[...]).astype(BF)


def mlp_kernel(a_ref, b_ref, c_ref, d_ref, lat_ref, gain_ref, w1_ref, w2_ref, lat_out, out_ref):
    lat = lat_ref[...] + added(a_ref, b_ref, c_ref, d_ref)
    lat_out[...] = lat
    normed = layer_norm(lat, gain_ref[...]).astype(BF)
    hidden = jax.nn.gelu(dot(normed, w1_ref[...]), approximate=True).astype(BF)
    out_ref[...] = dot(hidden, w2_ref[...]).astype(BF)


def last_kernel(a_ref, b_ref, c_ref, d_ref, lat_ref, gain_ref, out_ref):
    lat = lat_ref[...] + added(a_ref, b_ref, c_ref, d_ref)
    normed = layer_norm(lat, gain_ref[...]).astype(BF)
    for copy in range(out_ref.shape[0]):
        out_ref[copy] = normed


def query_kernel(
    heads,
    mod_ref,
    x_ref,
    table_ref,
    gain_ref,
    wq_ref,
    bias_ref,
    wo_ref,
    qt_ref,
    norm_ref,
    top_ref,
    bias_out,
    wot_ref,
    wqt_ref,
    bmax_ref,
    n_ref,
):
    step = pl.program_id(0)
    blocks = x_ref.shape[0] // MBLK
    lat_count = bias_ref.shape[2]

    @pl.when(step == 0)
    def _():
        wqt_ref[...] = wq_ref[...].T
        wot_ref[...] = wo_ref[...].T
        row = lax.broadcasted_iota(jnp.int32, (16, lat_count), 0)
        for part in range(heads // 8):
            block = []
            for h in range(8 * part, 8 * part + 8):
                rows = bias_rows(bias_ref[:, h, :] * LOG2E, 16)
                block.append(jnp.where(row == 3 * MODS + part, 1.0, rows))
            bias_out[part] = jnp.concatenate(block, axis=0).T.astype(BF)
        for m in range(MODS):
            top = jnp.max(bias_ref[m] * LOG2E, axis=1, keepdims=True)
            bmax_ref[m] = jnp.broadcast_to(top, (heads, MBLK))

    for b in range(blocks):
        n_ref[b * MBLK : (b + 1) * MBLK, :] = embed_norm(
            mod_ref, step * blocks, b, x_ref, table_ref, gain_ref[...]
        )
        mod = mod_ref[step * blocks + b]
        top_ref[:, b * MBLK : (b + 1) * MBLK] = bmax_ref[mod]
    query = dot_nt(wqt_ref[...], n_ref[...]) * SCALE2
    qt_ref[...] = query.astype(BF)
    for h in range(heads):
        own = query[h * HSZ : (h + 1) * HSZ, :]
        norm_ref[h : h + 1, :] = jnp.sqrt(jnp.sum(own * own, axis=0, keepdims=True))


def prepare_queries(queries, query_modality, table, gain, wq, bias, wo):
    count, width = queries.shape
    heads, lat_count = bias.shape[1:]
    cols = heads * HSZ
    tile = math.gcd(count, 512)
    whole = lambda *shape: pl.BlockSpec(shape, lambda i, mod: (0,) * len(shape))
    tiled = lambda rows: pl.BlockSpec((rows, tile), lambda i, mod: (0, i))
    return pl.pallas_call(
        functools.partial(query_kernel, heads),
        grid_spec=pltpu.PrefetchScalarGridSpec(
            num_scalar_prefetch=1,
            grid=(count // tile,),
            in_specs=[
                pl.BlockSpec((tile, width), lambda i, mod: (i, 0)),
                whole(MODS, width),
                whole(1, width),
                whole(width, cols),
                whole(MODS, heads, lat_count),
                whole(cols, width),
            ],
            out_specs=[
                tiled(cols),
                tiled(heads),
                tiled(heads),
                whole(heads // 8, lat_count, 128),
                whole(width, cols),
            ],
            scratch_shapes=[
                pltpu.VMEM((cols, width), BF),
                pltpu.VMEM((MODS, heads, MBLK), F32),
                pltpu.VMEM((tile, width), BF),
            ],
        ),
        out_shape=[
            jax.ShapeDtypeStruct((cols, count), BF),
            jax.ShapeDtypeStruct((heads, count), F32),
            jax.ShapeDtypeStruct((heads, count), F32),
            jax.ShapeDtypeStruct((heads // 8, lat_count, 128), BF),
            jax.ShapeDtypeStruct((width, cols), BF),
        ],
        compiler_params=pltpu.CompilerParams(vmem_limit_bytes=58 * MIB),
        cost_estimate=pl.CostEstimate(
            flops=2 * count * width * cols,
            transcendentals=count * heads,
            bytes_accessed=queries.nbytes + wq.nbytes + wo.nbytes + 2 * count * cols,
        ),
        name="queries",
    )(query_modality, queries, table, gain, wq, bias, wo)


def decode_kernel(
    heads,
    mod_ref,
    core_ref,
    x_ref,
    table_ref,
    own_ref,
    other_ref,
    wkv_ref,
    bias_ref,
    qt_ref,
    norm_ref,
    top_ref,
    wot_ref,
    out_ref,
    lat_ref,
    kx_ref,
    vx_ref,
    long_ref,
    hot_ref,
    p_ref,
    mix_ref,
):
    step = pl.program_id(0)
    tile = x_ref.shape[0]
    blocks = tile // MBLK
    lat_count = lat_ref.shape[0]

    @pl.when(step == 0)
    def _():
        join_rows(core_ref[0], own_ref, other_ref, lat_ref)
        normed = lat_ref[...]
        ones = jnp.ones((HSZ, lat_count), BF)
        lane = lax.broadcasted_iota(jnp.int32, (lat_count, 128), 1)
        sums = head_sums(4, 128)
        for quad in range(heads // 4):
            cols = slice(quad * 256, (quad + 1) * 256)
            keys = dot(normed, wkv_ref[0, :, cols])
            values = dot(normed, wkv_ref[1, :, cols]).astype(BF).T
            lengths = dot((keys * keys).astype(BF), sums)
            longest = jnp.sqrt(jnp.max(lengths, axis=0, keepdims=True))
            for at in range(4):
                h = 4 * quad + at
                pair = keys[:, at // 2 * 128 : at // 2 * 128 + 128]
                kx_ref[h, :, :128] = jnp.where(lane // HSZ == at % 2, pair, 0.0).astype(BF)
                extra = jnp.where(lane // 16 == h % 8, bias_ref[h // 8].astype(F32), 0.0)
                kx_ref[h, :, 128:] = extra.astype(BF)
                vx_ref[h, :HSZ, :] = values[at * HSZ : (at + 1) * HSZ, :]
                vx_ref[h, HSZ:, :] = ones
                long_ref[h : h + 1, :] = jnp.broadcast_to(
                    longest[:, at * 32 : at * 32 + 1], (1, 128)
                )

    bound = norm_ref[...] * long_ref[:, :1] + top_ref[...]
    row = lax.broadcasted_iota(jnp.int32, (16, MBLK), 0)
    for b in range(blocks):
        hit, _ = modality_hot(mod_ref[step * blocks + b], (16, MBLK), 0)
        onehot = jnp.where(hit, 1.0, 0.0)
        lanes = slice(b * MBLK, (b + 1) * MBLK)
        for group in range(8):
            rows = onehot
            for part in range(heads // 8):
                own = bound[8 * part + group : 8 * part + group + 1, lanes]
                rows = jnp.where(row == 3 * MODS + part, -own, rows)
            hot_ref[16 * group : 16 * group + 16, lanes] = rows.astype(BF)
    hot = hot_ref[...]
    least = jnp.full((1, tile), 1.0, F32)
    for h in range(heads + 1):
        if h < heads:
            pair = (h // 2) * 128
            right = jnp.concatenate([qt_ref[pair : pair + 128, :], hot], axis=0)
            p_ref[h % 2] = jnp.exp2(dot(kx_ref[h], right)).astype(BF)
        if h > 0:
            mixed = dot(vx_ref[h - 1], p_ref[(h - 1) % 2])
            least = jnp.minimum(least, mixed[HSZ : HSZ + 1, :])
            mix_ref[(h - 1) * HSZ : h * HSZ, :] = (mixed[:HSZ, :] / mixed[HSZ:, :]).astype(BF)

    @pl.when(jnp.min(least) < SMALL_TOTAL)
    def _():
        for b in range(blocks):
            hit, _ = modality_hot(mod_ref[step * blocks + b], (16, MBLK), 0)
            onehot = jnp.where(hit, 1.0, 0.0).astype(BF)
            for group in range(8):
                hot_ref[16 * group : 16 * group + 16, b * MBLK : (b + 1) * MBLK] = onehot

        def exact(h, _):
            pair = pl.multiple_of((h // 2) * 128, 128)
            right = jnp.concatenate([qt_ref[pl.ds(pair, 128), :], hot_ref[...]], axis=0)
            scores = dot(kx_ref[h], right)
            top = jnp.max(scores, axis=0, keepdims=True)
            mixed = dot(vx_ref[h], jnp.exp2(scores - top).astype(BF))
            mixed = (mixed[:HSZ, :] / mixed[HSZ:, :]).astype(BF)
            mix_ref[pl.ds(pl.multiple_of(h * HSZ, HSZ), HSZ), :] = mixed
            return 0

        lax.fori_loop(0, heads, exact, 0)

    decoded = dot(wot_ref[...], mix_ref[...]).T
    for b in range(blocks):
        rows = slice(b * MBLK, (b + 1) * MBLK)
        mod = mod_ref[step * blocks + b]
        embedded = x_ref[rows, :].astype(F32) + table_ref[pl.ds(mod, 1), :]
        out_ref[rows, :] = embedded + decoded[rows, :]


def decode(core, queries, query_modality, table, own, other, wkv, prepared):
    queries_t, norms, tops, bias, wo_t = prepared
    count, width = queries.shape
    lat_count = bias.shape[1]
    cols = queries_t.shape[0]
    heads = cols // HSZ
    tile = math.gcd(count, 512)
    lat_width = wkv.shape[1]
    held = pl.BlockSpec(memory_space=pltpu.VMEM)
    tiled = lambda rows: pl.BlockSpec((rows, tile), lambda i, *_: (0, i))
    return pl.pallas_call(
        functools.partial(decode_kernel, heads),
        grid_spec=pltpu.PrefetchScalarGridSpec(
            num_scalar_prefetch=2,
            grid=(count // tile,),
            in_specs=[
                pl.BlockSpec((tile, width), lambda i, *_: (i, 0)),
                held,
                held,
                held,
                held,
                held,
                tiled(cols),
                tiled(heads),
                tiled(heads),
                held,
            ],
            out_specs=pl.BlockSpec((tile, width), lambda i, *_: (i, 0)),
            scratch_shapes=[
                pltpu.VMEM((lat_count, lat_width), BF),
                pltpu.VMEM((heads, lat_count, 256), BF),
                pltpu.VMEM((heads, 128, lat_count), BF),
                pltpu.VMEM((heads, 128), F32),
                pltpu.VMEM((128, tile), BF),
                pltpu.VMEM((2, lat_count, tile), BF),
                pltpu.VMEM((cols, tile), BF),
            ],
        ),
        out_shape=jax.ShapeDtypeStruct((count, width), F32),
        compiler_params=pltpu.CompilerParams(vmem_limit_bytes=32 * MIB),
        cost_estimate=pl.CostEstimate(
            flops=2 * count * lat_count * heads * (256 + 128) + 2 * count * width * cols,
            transcendentals=count * lat_count * heads,
            bytes_accessed=queries.nbytes + wkv.nbytes + queries_t.nbytes + 4 * queries.size,
        ),
        name="decode",
    )(query_modality, core, queries, table, own, other, wkv, bias, queries_t, norms, tops, wo_t)


def fetch_kernel(count, *refs):
    sems = refs[-1]
    copies = [
        pltpu.make_async_copy(refs[i], refs[count + i], sems.at[i]) for i in range(count)
    ]
    for copy in copies:
        copy.start()
    for copy in copies:
        copy.wait()


def fetch(after, *arrays):
    after, *arrays = lax.optimization_barrier((after, *arrays))
    arrays = [pltpu.with_memory_space_constraint(a, pltpu.HBM) for a in arrays]
    near = pl.pallas_call(
        functools.partial(fetch_kernel, len(arrays)),
        out_shape=[jax.ShapeDtypeStruct(a.shape, a.dtype) for a in arrays],
        in_specs=[pl.BlockSpec(memory_space=pltpu.HBM)] * len(arrays),
        out_specs=[pl.BlockSpec(memory_space=pltpu.VMEM)] * len(arrays),
        scratch_shapes=[pltpu.SemaphoreType.DMA((len(arrays),))],
        compiler_params=pltpu.CompilerParams(vmem_limit_bytes=14 * MIB),
        cost_estimate=pl.CostEstimate(
            flops=0, transcendentals=0, bytes_accessed=2 * sum(a.nbytes for a in arrays)
        ),
        name="fetch",
    )(*arrays)
    return after, *near


def trade(parts):
    size = lax.axis_size("inp")
    groups = [list(range(core, size, 2)) for core in range(2)]
    return lax.all_to_all(parts, "inp", 0, 0, axis_index_groups=groups)


def other_core(rows):
    return lax.ppermute(rows, "inp", [(i, i ^ 1) for i in range(lax.axis_size("inp"))])


def head_parts(part):
    size = lax.axis_size("head")
    moved = [
        lax.ppermute(part, "head", [(i, (i + k) % size) for i in range(size)])
        for k in range(1, size)
    ]
    return [part] + moved


def body(
    inputs,
    input_modality,
    queries,
    query_modality,
    modality_embed,
    latents,
    ln_in_gain,
    ln_lat_gain,
    enc_wq,
    enc_wkv,
    enc_bias,
    enc_wo,
    self_gain,
    self_wqkv,
    self_bias,
    self_wo,
    mlp_gain,
    mlp_w1,
    mlp_w2,
    dec_gain,
    dec_wkv,
    query_gain,
    dec_wq,
    dec_bias,
    dec_wo,
):
    lat_count, width = latents.shape
    lat_rows = lat_count // lax.axis_size("inp")
    row_first = lax.axis_index("inp") * lat_rows
    heads = enc_bias.shape[1]
    cols = heads * HSZ
    row = lambda v: v.reshape(1, -1)
    shape = jax.ShapeDtypeStruct

    core = (lax.axis_index("inp") % 2).astype(jnp.int32).reshape(1)
    chips = lax.axis_size("inp") // 2
    partial = encode(
        inputs,
        input_modality,
        modality_embed,
        row(ln_in_gain),
        latents,
        row(ln_lat_gain),
        enc_wq,
        enc_wkv,
        enc_bias,
    )
    partial, early = lax.optimization_barrier((partial, queries))
    parts = lax.all_to_all(partial.reshape(-1, lat_rows, partial.shape[1]), "inp", 0, 0)
    prepared = prepare_queries(
        early, query_modality, modality_embed, row(query_gain), dec_wq, dec_bias, dec_wo
    )
    parts, prepared = lax.optimization_barrier((parts, prepared))
    enc_part = small_call(
        functools.partial(merge_kernel, heads), "merge", shape((lat_rows, width), BF), parts, enc_wo
    )
    enc_part, weights, near_bias = fetch(enc_part, self_wqkv, self_bias)
    latent_rows = lax.dynamic_slice_in_dim(latents, row_first, lat_rows, 0)
    lat_one, self_q, self_kv = small_call(
        project_kernel,
        "project",
        [
            shape((lat_rows, width), F32),
            shape((lat_rows, cols), BF),
            shape((chips, lat_rows, 2 * cols), BF),
        ],
        *head_parts(enc_part),
        latent_rows,
        row(self_gain),
        weights,
    )
    own_kv = trade(self_kv)
    self_part = small_call(
        functools.partial(attend_kernel, heads),
        "attend",
        shape((lat_rows, width), BF),
        core,
        self_q,
        own_kv,
        other_core(own_kv),
        near_bias,
        self_wo,
        scratch=[pltpu.VMEM((lat_count, 2 * cols), BF)],
    )
    self_part, weights = fetch(self_part, mlp_w2)
    lat_two, mlp_part = small_call(
        mlp_kernel,
        "mlp",
        [shape((lat_rows, width), F32), shape((lat_rows, width), BF)],
        *head_parts(self_part),
        lat_one,
        row(mlp_gain),
        mlp_w1,
        weights,
    )
    normed = small_call(
        last_kernel,
        "last",
        shape((chips, lat_rows, width), BF),
        *head_parts(mlp_part),
        lat_two,
        row(dec_gain),
    )
    own = trade(normed)
    prepared = (pltpu.with_memory_space_constraint(prepared[0], pltpu.HBM), *prepared[1:])
    return decode(
        core, queries, query_modality, modality_embed, own, other_core(own), dec_wkv, prepared
    )


def solution(mesh):
    placed = (
        P("inp", None),
        P("inp"),
        P(("inp", "head"), None),
        P(("inp", "head")),
        P(),
        P(),
        P(),
        P(),
        P(None, "head"),
        P(None, None, "head"),
        P(None, "head", None),
        P("head", None),
        P(),
        P(None, None, "head"),
        P("head", "inp", None),
        P("head", None),
        P(),
        P(None, "head"),
        P("head", None),
        P(),
        P(),
        P(),
        P(),
        P(),
        P(),
    )
    return jax.shard_map(
        body, mesh=mesh, in_specs=placed, out_specs=P(("inp", "head"), None), check_vma=False
    )
```

```python
import functools
import math

import jax
import jax.numpy as jnp
from jax import lax
from jax.experimental import pallas as pl
from jax.experimental.pallas import tpu as pltpu
from jax.sharding import PartitionSpec as P

HSZ = 64
MODS = 3
MBLK = 128
EPSILON = 1e-05
LOG2E = 1.4426950408889634
SCALE2 = LOG2E / math.sqrt(HSZ)
NEG_FLOOR = -1e30
BF = jnp.bfloat16
F32 = jnp.float32
MIB = 2**20
EXTRA = 128
SMALL_TOTAL = 2.0**-95


def dot(a, b):
    return jnp.dot(a, b, preferred_element_type=F32)


def dot_nt(a, b):
    return lax.dot_general(a, b, (((1,), (1,)), ((), ())), preferred_element_type=F32)


def layer_norm(values, gain):
    centered = values - jnp.mean(values, axis=-1, keepdims=True)
    variance = jnp.mean(centered * centered, axis=-1, keepdims=True)
    return centered * lax.rsqrt(variance + EPSILON) * gain


def three_parts(values):
    high = values.astype(BF)
    rest = values - high.astype(F32)
    mid = rest.astype(BF)
    low = (rest - mid.astype(F32)).astype(BF)
    return high.astype(F32), mid.astype(F32), low.astype(F32)


def bias_rows(bias, rows):
    index = lax.broadcasted_iota(jnp.int32, (rows, bias.shape[1]), 0)
    block = jnp.zeros((rows, bias.shape[1]), F32)
    for part, piece in enumerate(three_parts(bias)):
        for mod in range(MODS):
            block = jnp.where(index == MODS * part + mod, piece[mod : mod + 1, :], block)
    return block


def modality_hot(mod, shape, dim):
    index = lax.broadcasted_iota(jnp.int32, shape, dim)
    hit = (index == mod) | (index == mod + MODS) | (index == mod + 2 * MODS)
    return hit, index


def head_sums(count, lanes):
    row = lax.broadcasted_iota(jnp.int32, (count * HSZ, lanes), 0) // HSZ
    lane = lax.broadcasted_iota(jnp.int32, (count * HSZ, lanes), 1) // (lanes // count)
    return jnp.where(row == lane, 1.0, 0.0).astype(BF)


def embed_norm(mod_ref, first, b, x_ref, table_ref, gain):
    embedded = x_ref[b * MBLK : (b + 1) * MBLK, :].astype(F32)
    embedded = embedded + table_ref[pl.ds(mod_ref[first + b], 1), :]
    return layer_norm(embedded, gain).astype(BF)


def join_rows(core, own_ref, other_ref, all_ref):
    for held, refs in enumerate(((own_ref, other_ref), (other_ref, own_ref))):

        @pl.when(core == held)
        def _():
            for block in range(all_ref.shape[0] // 16):
                all_ref[block * 16 : block * 16 + 16, :] = refs[block % 2][block // 2]


def encode_kernel(
    heads,
    mod_ref,
    x_ref,
    next_ref,
    table_ref,
    gain_ref,
    lat_ref,
    lat_gain_ref,
    wq_ref,
    wkv_ref,
    bias_ref,
    out_ref,
    qx_ref,
    norm_ref,
    wvt_ref,
    n_ref,
    hot_ref,
    k_ref,
    vt_ref,
    p_ref,
    part_ref,
    shift_ref,
    m_ref,
    acc_ref,
):
    step = pl.program_id(0)
    last = pl.num_programs(0) - 1
    points = x_ref.shape[0]
    blocks = points // MBLK
    lat_count = lat_ref.shape[0]
    slot = lax.rem(step, 2)
    row16 = lax.broadcasted_iota(jnp.int32, (16, lat_count), 0)
    gain = gain_ref[...]

    def project(at, into):
        normed = n_ref[...]
        keys = dot(normed, wkv_ref[0])
        k_ref[into] = keys.astype(BF)
        vt_ref[into] = dot_nt(wvt_ref[...], normed).astype(BF)
        lengths = dot((keys * keys).astype(BF), head_sums(heads, 128))
        longest = jnp.sqrt(jnp.max(lengths, axis=0, keepdims=True))
        present = [jnp.bool_(False)] * MODS
        for b in range(blocks):
            mod = mod_ref[at * blocks + b]
            hit, index = modality_hot(mod, (MBLK, 128), 1)
            hit = jnp.where(hit | (index == 16), 1.0, 0.0)
            hot_ref[into, b * MBLK : (b + 1) * MBLK, :] = hit.astype(BF)
            present = [p | (mod == m) for m, p in enumerate(present)]
        for h in range(heads):
            bound = jnp.full((1, lat_count), NEG_FLOOR, F32)
            for m in range(MODS):
                held = jnp.where(present[m], bias_ref[m, h : h + 1, :] * LOG2E, NEG_FLOOR)
                bound = jnp.maximum(bound, held)
            lane = h * (128 // heads)
            bound = bound + norm_ref[h : h + 1, :] * longest[:, lane : lane + 1]
            shift_ref[into, h] = bound.astype(BF).astype(F32)

    @pl.when(step == 0)
    def _():
        normed = layer_norm(lat_ref[...], lat_gain_ref[...]).astype(BF)
        query = (dot(normed, wq_ref[...]) * SCALE2).T
        qx_ref[...] = jnp.zeros(qx_ref.shape, BF)
        for h in range(heads):
            half = (h % 2) * HSZ
            own = query[h * HSZ : (h + 1) * HSZ, :]
            qx_ref[h, half : half + HSZ, :] = own.astype(BF)
            qx_ref[h, 128:144, :] = bias_rows(bias_ref[:, h, :] * LOG2E, 16).astype(BF)
            norm_ref[h : h + 1, :] = jnp.sqrt(jnp.sum(own * own, axis=0, keepdims=True))
        wvt_ref[...] = wkv_ref[1].T
        m_ref[...] = jnp.full(m_ref.shape, NEG_FLOOR, F32)
        acc_ref[...] = jnp.zeros(acc_ref.shape, F32)
        for b in range(blocks):
            n_ref[b * MBLK : (b + 1) * MBLK, :] = embed_norm(
                mod_ref, 0, b, x_ref, table_ref, gain
            )
        project(0, 0)

    following = jnp.minimum(step + 1, last)

    def main(prepare):
        hot = hot_ref[slot]
        ones = jnp.ones((HSZ, points), BF)
        for h in range(heads):
            qx_ref[h, 144:160, :] = jnp.where(row16 == 0, -shift_ref[slot, h], 0.0).astype(BF)
        per_head = -(-blocks // 2)
        for h in range(heads + 1):
            if h < heads:
                pair = (h // 2) * 128
                left = jnp.concatenate([k_ref[slot, :, pair : pair + 128], hot], axis=1)
                p_ref[h % 2] = jnp.exp2(dot(left, qx_ref[h])).astype(BF)
            if h > 0:
                values_h = vt_ref[slot, (h - 1) * HSZ : h * HSZ, :]
                values_h = jnp.concatenate([values_h, ones], axis=0)
                part_ref[h - 1] = dot(values_h, p_ref[(h - 1) % 2])
            for b in range(h * per_head, min((h + 1) * per_head, blocks) if prepare else 0):
                n_ref[b * MBLK : (b + 1) * MBLK, :] = embed_norm(
                    mod_ref, following * blocks, b, next_ref, table_ref, gain
                )
            if h == 2 and prepare:
                project(following, 1 - slot)

    pl.when(step < last)(functools.partial(main, True))
    pl.when(step == last)(functools.partial(main, False))
    least = jnp.min(part_ref[:, HSZ : HSZ + 1, :])

    @pl.when(least < SMALL_TOTAL)
    def _():
        def exact(h, _):
            pair = pl.multiple_of((h // 2) * 128, 128)
            qx_ref[h, 144:160, :] = jnp.zeros((16, lat_count), BF)
            left = jnp.concatenate([k_ref[slot, :, pl.ds(pair, 128)], hot_ref[slot]], axis=1)
            scores = dot(left, qx_ref[h])
            top = jnp.max(scores, axis=0, keepdims=True)
            weights = jnp.exp2(scores - top).astype(BF)
            values_h = vt_ref[slot, pl.ds(pl.multiple_of(h * HSZ, HSZ), HSZ), :]
            values_h = jnp.concatenate([values_h, jnp.ones((HSZ, points), BF)], axis=0)
            part_ref[h] = dot(values_h, weights)
            shift_ref[slot, h] = top
            return 0

        lax.fori_loop(0, heads, exact, 0)

    for h in range(heads):
        old = m_ref[h]
        own = shift_ref[slot, h]
        new = jnp.maximum(old, own)
        m_ref[h] = new
        acc_ref[h] = acc_ref[h] * jnp.exp2(old - new) + part_ref[h] * jnp.exp2(own - new)

    @pl.when(step == last)
    def _():
        index = lax.broadcasted_iota(jnp.int32, (EXTRA, lat_count), 0)
        extra = jnp.zeros((EXTRA, lat_count), F32)
        pieces = []
        for h in range(heads):
            acc = acc_ref[h]
            total = acc[HSZ : HSZ + 1, :]
            pieces.append(acc[:HSZ, :] / total)
            for part, piece in enumerate(three_parts(m_ref[h] + jnp.log2(total))):
                extra = jnp.where(index == heads * part + h, piece, extra)
        out_ref[...] = jnp.concatenate(pieces + [extra], axis=0).T.astype(BF)


def encode(inputs, input_modality, table, gain, latents, lat_gain, wq, wkv, bias):
    points, width = inputs.shape
    heads = bias.shape[1]
    lat_count, lat_width = latents.shape
    cols = heads * HSZ
    tile = math.gcd(points, 2048)
    steps = points // tile
    whole = lambda *shape: pl.BlockSpec(shape, lambda i, *_: (0,) * len(shape))
    return pl.pallas_call(
        functools.partial(encode_kernel, heads),
        grid_spec=pltpu.PrefetchScalarGridSpec(
            num_scalar_prefetch=1,
            grid=(steps,),
            in_specs=[
                pl.BlockSpec((tile, width), lambda i, *_: (0, 0)),
                pl.BlockSpec((tile, width), lambda i, *_: (jnp.minimum(i + 1, steps - 1), 0)),
                whole(MODS, width),
                whole(1, width),
                whole(lat_count, lat_width),
                whole(1, lat_width),
                whole(lat_width, cols),
                whole(2, width, cols),
                whole(MODS, heads, lat_count),
            ],
            out_specs=whole(lat_count, cols + EXTRA),
            scratch_shapes=[
                pltpu.VMEM((heads, 256, lat_count), BF),
                pltpu.VMEM((heads, lat_count), F32),
                pltpu.VMEM((cols, width), BF),
                pltpu.VMEM((tile, width), BF),
                pltpu.VMEM((2, tile, 128), BF),
                pltpu.VMEM((2, tile, cols), BF),
                pltpu.VMEM((2, cols, tile), BF),
                pltpu.VMEM((2, tile, lat_count), BF),
                pltpu.VMEM((heads, 128, lat_count), F32),
                pltpu.VMEM((2, heads, 1, lat_count), F32),
                pltpu.VMEM((heads, 1, lat_count), F32),
                pltpu.VMEM((heads, 128, lat_count), F32),
            ],
        ),
        out_shape=jax.ShapeDtypeStruct((lat_count, cols + EXTRA), BF),
        compiler_params=pltpu.CompilerParams(vmem_limit_bytes=58 * MIB),
        cost_estimate=pl.CostEstimate(
            flops=2 * points * lat_count * heads * (256 + 128),
            transcendentals=points * lat_count * heads,
            bytes_accessed=2 * inputs.nbytes + latents.nbytes + wq.nbytes + wkv.nbytes,
        ),
        name="encode",
    )(input_modality, inputs, inputs, table, gain, latents, lat_gain, wq, wkv, bias)


def small_call(kernel, name, outs, *args, scratch=()):
    space = lambda a: pltpu.SMEM if a.dtype == jnp.int32 else pltpu.VMEM
    return pl.pallas_call(
        kernel,
        out_shape=outs,
        in_specs=[pl.BlockSpec(memory_space=space(a)) for a in args],
        scratch_shapes=list(scratch),
        out_specs=jax.tree.map(lambda _: pl.BlockSpec(memory_space=pltpu.VMEM), outs),
        compiler_params=pltpu.CompilerParams(vmem_limit_bytes=14 * MIB),
        name=name,
    )(*args)


def log_totals(heads, extra):
    lse = extra[..., :heads]
    for part in range(1, 3):
        lse = lse + extra[..., heads * part : heads * (part + 1)]
    return lse


def per_head(heads, factor, shape):
    lane = lax.broadcasted_iota(jnp.int32, shape, len(shape) - 1) // HSZ
    spread = jnp.zeros(shape, F32)
    for h in range(heads):
        spread = jnp.where(lane == h, factor[..., h : h + 1], spread)
    return spread


def merge_kernel(heads, part_ref, wo_ref, out_ref):
    cols = heads * HSZ
    lse = log_totals(heads, part_ref[:, :, cols:].astype(F32))
    factor = jnp.exp2(lse - jnp.max(lse, axis=0, keepdims=True))
    factor = factor / jnp.sum(factor, axis=0, keepdims=True)
    spread = per_head(heads, factor, part_ref.shape[:2] + (cols,))
    attended = jnp.sum(part_ref[:, :, :cols].astype(F32) * spread, axis=0)
    out_ref[...] = dot(attended.astype(BF), wo_ref[...]).astype(BF)


def added(*refs):
    a, b, c, d = [ref[...].astype(F32) for ref in refs]
    return (a + b) + (c + d)


def project_kernel(a_ref, b_ref, c_ref, d_ref, lat_ref, gain_ref, w_ref, lat_out, q_out, kv_out):
    lat = lat_ref[...] + added(a_ref, b_ref, c_ref, d_ref)
    lat_out[...] = lat
    normed = layer_norm(lat, gain_ref[...]).astype(BF)
    cols = w_ref.shape[2]
    q_out[...] = (dot(normed, w_ref[0]) * SCALE2).astype(BF)
    keys = dot(normed, w_ref[1]).astype(BF)
    values = dot(normed, w_ref[2]).astype(BF)
    for copy in range(kv_out.shape[0]):
        kv_out[copy, :, :cols] = keys
        kv_out[copy, :, cols:] = values


def attend_kernel(heads, core_ref, q_ref, own_ref, other_ref, bias_ref, wo_ref, out_ref, kv_ref):
    join_rows(core_ref[0], own_ref, other_ref, kv_ref)
    cols = heads * HSZ
    query = q_ref[...]
    rows = query.shape[0]
    keys = kv_ref[:, :cols]
    values = kv_ref[:, cols:]
    lane = lax.broadcasted_iota(jnp.int32, (rows, cols), 1) // HSZ
    mixed = jnp.zeros((rows, cols), F32)
    for h in range(heads):
        own = jnp.where(lane == h, query.astype(F32), 0.0).astype(BF)
        scores = dot_nt(own, keys) + bias_ref[h] * LOG2E
        weights = jnp.exp2(scores - jnp.max(scores, axis=1, keepdims=True))
        total = jnp.sum(weights, axis=1, keepdims=True)
        mixed = jnp.where(lane == h, dot(weights.astype(BF), values) / total, mixed)
    out_ref[...] = dot(mixed.astype(BF), wo_ref[...]).astype(BF)


def mlp_kernel(a_ref, b_ref, c_ref, d_ref, lat_ref, gain_ref, w1_ref, w2_ref, lat_out, out_ref):
    lat = lat_ref[...] + added(a_ref, b_ref, c_ref, d_ref)
    lat_out[...] = lat
    normed = layer_norm(lat, gain_ref[...]).astype(BF)
    hidden = jax.nn.gelu(dot(normed, w1_ref[...]), approximate=True).astype(BF)
    out_ref[...] = dot(hidden, w2_ref[...]).astype(BF)


def last_kernel(a_ref, b_ref, c_ref, d_ref, lat_ref, gain_ref, out_ref):
    lat = lat_ref[...] + added(a_ref, b_ref, c_ref, d_ref)
    normed = layer_norm(lat, gain_ref[...]).astype(BF)
    for copy in range(out_ref.shape[0]):
        out_ref[copy] = normed


def query_kernel(
    heads,
    mod_ref,
    x_ref,
    table_ref,
    gain_ref,
    wq_ref,
    bias_ref,
    wo_ref,
    qt_ref,
    norm_ref,
    top_ref,
    bias_out,
    wot_ref,
    wqt_ref,
    bmax_ref,
    n_ref,
):
    step = pl.program_id(0)
    blocks = x_ref.shape[0] // MBLK
    lat_count = bias_ref.shape[2]

    @pl.when(step == 0)
    def _():
        wqt_ref[...] = wq_ref[...].T
        wot_ref[...] = wo_ref[...].T
        row = lax.broadcasted_iota(jnp.int32, (16, lat_count), 0)
        for part in range(heads // 8):
            block = []
            for h in range(8 * part, 8 * part + 8):
                rows = bias_rows(bias_ref[:, h, :] * LOG2E, 16)
                block.append(jnp.where(row == 3 * MODS + part, 1.0, rows))
            bias_out[part] = jnp.concatenate(block, axis=0).T.astype(BF)
        for m in range(MODS):
            top = jnp.max(bias_ref[m] * LOG2E, axis=1, keepdims=True)
            bmax_ref[m] = jnp.broadcast_to(top, (heads, MBLK))

    for b in range(blocks):
        n_ref[b * MBLK : (b + 1) * MBLK, :] = embed_norm(
            mod_ref, step * blocks, b, x_ref, table_ref, gain_ref[...]
        )
        mod = mod_ref[step * blocks + b]
        top_ref[:, b * MBLK : (b + 1) * MBLK] = bmax_ref[mod]
    query = dot_nt(wqt_ref[...], n_ref[...]) * SCALE2
    qt_ref[...] = query.astype(BF)
    for h in range(heads):
        own = query[h * HSZ : (h + 1) * HSZ, :]
        norm_ref[h : h + 1, :] = jnp.sqrt(jnp.sum(own * own, axis=0, keepdims=True))


def prepare_queries(queries, query_modality, table, gain, wq, bias, wo):
    count, width = queries.shape
    heads, lat_count = bias.shape[1:]
    cols = heads * HSZ
    tile = math.gcd(count, 512)
    whole = lambda *shape: pl.BlockSpec(shape, lambda i, mod: (0,) * len(shape))
    tiled = lambda rows: pl.BlockSpec((rows, tile), lambda i, mod: (0, i))
    return pl.pallas_call(
        functools.partial(query_kernel, heads),
        grid_spec=pltpu.PrefetchScalarGridSpec(
            num_scalar_prefetch=1,
            grid=(count // tile,),
            in_specs=[
                pl.BlockSpec((tile, width), lambda i, mod: (i, 0)),
                whole(MODS, width),
                whole(1, width),
                whole(width, cols),
                whole(MODS, heads, lat_count),
                whole(cols, width),
            ],
            out_specs=[
                tiled(cols),
                tiled(heads),
                tiled(heads),
                whole(heads // 8, lat_count, 128),
                whole(width, cols),
            ],
            scratch_shapes=[
                pltpu.VMEM((cols, width), BF),
                pltpu.VMEM((MODS, heads, MBLK), F32),
                pltpu.VMEM((tile, width), BF),
            ],
        ),
        out_shape=[
            jax.ShapeDtypeStruct((cols, count), BF),
            jax.ShapeDtypeStruct((heads, count), F32),
            jax.ShapeDtypeStruct((heads, count), F32),
            jax.ShapeDtypeStruct((heads // 8, lat_count, 128), BF),
            jax.ShapeDtypeStruct((width, cols), BF),
        ],
        compiler_params=pltpu.CompilerParams(vmem_limit_bytes=58 * MIB),
        cost_estimate=pl.CostEstimate(
            flops=2 * count * width * cols,
            transcendentals=count * heads,
            bytes_accessed=queries.nbytes + wq.nbytes + wo.nbytes + 2 * count * cols,
        ),
        name="queries",
    )(query_modality, queries, table, gain, wq, bias, wo)


def decode_kernel(
    heads,
    mod_ref,
    core_ref,
    x_ref,
    table_ref,
    own_ref,
    other_ref,
    wkv_ref,
    bias_ref,
    qt_ref,
    norm_ref,
    top_ref,
    wot_ref,
    out_ref,
    lat_ref,
    kx_ref,
    vx_ref,
    long_ref,
    hot_ref,
    p_ref,
    mix_ref,
):
    step = pl.program_id(0)
    tile = x_ref.shape[0]
    blocks = tile // MBLK
    lat_count = lat_ref.shape[0]

    @pl.when(step == 0)
    def _():
        join_rows(core_ref[0], own_ref, other_ref, lat_ref)
        normed = lat_ref[...]
        ones = jnp.ones((HSZ, lat_count), BF)
        lane = lax.broadcasted_iota(jnp.int32, (lat_count, 128), 1)
        sums = head_sums(4, 128)
        for quad in range(heads // 4):
            cols = slice(quad * 256, (quad + 1) * 256)
            keys = dot(normed, wkv_ref[0, :, cols])
            values = dot(normed, wkv_ref[1, :, cols]).astype(BF).T
            lengths = dot((keys * keys).astype(BF), sums)
            longest = jnp.sqrt(jnp.max(lengths, axis=0, keepdims=True))
            for at in range(4):
                h = 4 * quad + at
                pair = keys[:, at // 2 * 128 : at // 2 * 128 + 128]
                kx_ref[h, :, :128] = jnp.where(lane // HSZ == at % 2, pair, 0.0).astype(BF)
                extra = jnp.where(lane // 16 == h % 8, bias_ref[h // 8].astype(F32), 0.0)
                kx_ref[h, :, 128:] = extra.astype(BF)
                vx_ref[h, :HSZ, :] = values[at * HSZ : (at + 1) * HSZ, :]
                vx_ref[h, HSZ:, :] = ones
                long_ref[h : h + 1, :] = jnp.broadcast_to(
                    longest[:, at * 32 : at * 32 + 1], (1, 128)
                )

    bound = norm_ref[...] * long_ref[:, :1] + top_ref[...]
    row = lax.broadcasted_iota(jnp.int32, (16, MBLK), 0)
    for b in range(blocks):
        hit, _ = modality_hot(mod_ref[step * blocks + b], (16, MBLK), 0)
        onehot = jnp.where(hit, 1.0, 0.0)
        lanes = slice(b * MBLK, (b + 1) * MBLK)
        for group in range(8):
            rows = onehot
            for part in range(heads // 8):
                own = bound[8 * part + group : 8 * part + group + 1, lanes]
                rows = jnp.where(row == 3 * MODS + part, -own, rows)
            hot_ref[16 * group : 16 * group + 16, lanes] = rows.astype(BF)
    hot = hot_ref[...]
    least = jnp.full((1, tile), 1.0, F32)
    for h in range(heads + 1):
        if h < heads:
            pair = (h // 2) * 128
            right = jnp.concatenate([qt_ref[pair : pair + 128, :], hot], axis=0)
            p_ref[h % 2] = jnp.exp2(dot(kx_ref[h], right)).astype(BF)
        if h > 0:
            mixed = dot(vx_ref[h - 1], p_ref[(h - 1) % 2])
            least = jnp.minimum(least, mixed[HSZ : HSZ + 1, :])
            mix_ref[(h - 1) * HSZ : h * HSZ, :] = (mixed[:HSZ, :] / mixed[HSZ:, :]).astype(BF)

    @pl.when(jnp.min(least) < SMALL_TOTAL)
    def _():
        for b in range(blocks):
            hit, _ = modality_hot(mod_ref[step * blocks + b], (16, MBLK), 0)
            onehot = jnp.where(hit, 1.0, 0.0).astype(BF)
            for group in range(8):
                hot_ref[16 * group : 16 * group + 16, b * MBLK : (b + 1) * MBLK] = onehot

        def exact(h, _):
            pair = pl.multiple_of((h // 2) * 128, 128)
            right = jnp.concatenate([qt_ref[pl.ds(pair, 128), :], hot_ref[...]], axis=0)
            scores = dot(kx_ref[h], right)
            top = jnp.max(scores, axis=0, keepdims=True)
            mixed = dot(vx_ref[h], jnp.exp2(scores - top).astype(BF))
            mixed = (mixed[:HSZ, :] / mixed[HSZ:, :]).astype(BF)
            mix_ref[pl.ds(pl.multiple_of(h * HSZ, HSZ), HSZ), :] = mixed
            return 0

        lax.fori_loop(0, heads, exact, 0)

    decoded = dot(wot_ref[...], mix_ref[...]).T
    for b in range(blocks):
        rows = slice(b * MBLK, (b + 1) * MBLK)
        mod = mod_ref[step * blocks + b]
        embedded = x_ref[rows, :].astype(F32) + table_ref[pl.ds(mod, 1), :]
        out_ref[rows, :] = embedded + decoded[rows, :]


def decode(core, queries, query_modality, table, own, other, wkv, prepared):
    queries_t, norms, tops, bias, wo_t = prepared
    count, width = queries.shape
    lat_count = bias.shape[1]
    cols = queries_t.shape[0]
    heads = cols // HSZ
    tile = math.gcd(count, 512)
    lat_width = wkv.shape[1]
    held = pl.BlockSpec(memory_space=pltpu.VMEM)
    tiled = lambda rows: pl.BlockSpec((rows, tile), lambda i, *_: (0, i))
    return pl.pallas_call(
        functools.partial(decode_kernel, heads),
        grid_spec=pltpu.PrefetchScalarGridSpec(
            num_scalar_prefetch=2,
            grid=(count // tile,),
            in_specs=[
                pl.BlockSpec((tile, width), lambda i, *_: (i, 0)),
                held,
                held,
                held,
                held,
                held,
                tiled(cols),
                tiled(heads),
                tiled(heads),
                held,
            ],
            out_specs=pl.BlockSpec((tile, width), lambda i, *_: (i, 0)),
            scratch_shapes=[
                pltpu.VMEM((lat_count, lat_width), BF),
                pltpu.VMEM((heads, lat_count, 256), BF),
                pltpu.VMEM((heads, 128, lat_count), BF),
                pltpu.VMEM((heads, 128), F32),
                pltpu.VMEM((128, tile), BF),
                pltpu.VMEM((2, lat_count, tile), BF),
                pltpu.VMEM((cols, tile), BF),
            ],
        ),
        out_shape=jax.ShapeDtypeStruct((count, width), F32),
        compiler_params=pltpu.CompilerParams(vmem_limit_bytes=32 * MIB),
        cost_estimate=pl.CostEstimate(
            flops=2 * count * lat_count * heads * (256 + 128) + 2 * count * width * cols,
            transcendentals=count * lat_count * heads,
            bytes_accessed=queries.nbytes + wkv.nbytes + queries_t.nbytes + 4 * queries.size,
        ),
        name="decode",
    )(query_modality, core, queries, table, own, other, wkv, bias, queries_t, norms, tops, wo_t)


def fetch_kernel(count, *refs):
    sems = refs[-1]
    copies = [
        pltpu.make_async_copy(refs[i], refs[count + i], sems.at[i]) for i in range(count)
    ]
    for copy in copies:
        copy.start()
    for copy in copies:
        copy.wait()


def fetch(after, *arrays):
    after, *arrays = lax.optimization_barrier((after, *arrays))
    arrays = [pltpu.with_memory_space_constraint(a, pltpu.HBM) for a in arrays]
    near = pl.pallas_call(
        functools.partial(fetch_kernel, len(arrays)),
        out_shape=[jax.ShapeDtypeStruct(a.shape, a.dtype) for a in arrays],
        in_specs=[pl.BlockSpec(memory_space=pltpu.HBM)] * len(arrays),
        out_specs=[pl.BlockSpec(memory_space=pltpu.VMEM)] * len(arrays),
        scratch_shapes=[pltpu.SemaphoreType.DMA((len(arrays),))],
        compiler_params=pltpu.CompilerParams(vmem_limit_bytes=14 * MIB),
        cost_estimate=pl.CostEstimate(
            flops=0, transcendentals=0, bytes_accessed=2 * sum(a.nbytes for a in arrays)
        ),
        name="fetch",
    )(*arrays)
    return after, *near


def trade(parts):
    size = lax.axis_size("inp")
    groups = [list(range(core, size, 2)) for core in range(2)]
    return lax.all_to_all(parts, "inp", 0, 0, axis_index_groups=groups)


def other_core(rows):
    return lax.ppermute(rows, "inp", [(i, i ^ 1) for i in range(lax.axis_size("inp"))])


def head_parts(part):
    size = lax.axis_size("head")
    moved = [
        lax.ppermute(part, "head", [(i, (i + k) % size) for i in range(size)])
        for k in range(1, size)
    ]
    return [part] + moved


def body(
    inputs,
    input_modality,
    queries,
    query_modality,
    modality_embed,
    latents,
    ln_in_gain,
    ln_lat_gain,
    enc_wq,
    enc_wkv,
    enc_bias,
    enc_wo,
    self_gain,
    self_wqkv,
    self_bias,
    self_wo,
    mlp_gain,
    mlp_w1,
    mlp_w2,
    dec_gain,
    dec_wkv,
    query_gain,
    dec_wq,
    dec_bias,
    dec_wo,
):
    lat_count, width = latents.shape
    lat_rows = lat_count // lax.axis_size("inp")
    row_first = lax.axis_index("inp") * lat_rows
    heads = enc_bias.shape[1]
    cols = heads * HSZ
    row = lambda v: v.reshape(1, -1)
    shape = jax.ShapeDtypeStruct

    core = (lax.axis_index("inp") % 2).astype(jnp.int32).reshape(1)
    chips = lax.axis_size("inp") // 2
    partial = encode(
        inputs,
        input_modality,
        modality_embed,
        row(ln_in_gain),
        latents,
        row(ln_lat_gain),
        enc_wq,
        enc_wkv,
        enc_bias,
    )
    partial, early = lax.optimization_barrier((partial, queries))
    parts = lax.all_to_all(partial.reshape(-1, lat_rows, partial.shape[1]), "inp", 0, 0)
    prepared = prepare_queries(
        early, query_modality, modality_embed, row(query_gain), dec_wq, dec_bias, dec_wo
    )
    parts, prepared = lax.optimization_barrier((parts, prepared))
    enc_part = small_call(
        functools.partial(merge_kernel, heads), "merge", shape((lat_rows, width), BF), parts, enc_wo
    )
    enc_part, weights, near_bias = fetch(enc_part, self_wqkv, self_bias)
    latent_rows = lax.dynamic_slice_in_dim(latents, row_first, lat_rows, 0)
    lat_one, self_q, self_kv = small_call(
        project_kernel,
        "project",
        [
            shape((lat_rows, width), F32),
            shape((lat_rows, cols), BF),
            shape((chips, lat_rows, 2 * cols), BF),
        ],
        *head_parts(enc_part),
        latent_rows,
        row(self_gain),
        weights,
    )
    own_kv = trade(self_kv)
    self_part = small_call(
        functools.partial(attend_kernel, heads),
        "attend",
        shape((lat_rows, width), BF),
        core,
        self_q,
        own_kv,
        other_core(own_kv),
        near_bias,
        self_wo,
        scratch=[pltpu.VMEM((lat_count, 2 * cols), BF)],
    )
    self_part, weights = fetch(self_part, mlp_w2)
    lat_two, mlp_part = small_call(
        mlp_kernel,
        "mlp",
        [shape((lat_rows, width), F32), shape((lat_rows, width), BF)],
        *head_parts(self_part),
        lat_one,
        row(mlp_gain),
        mlp_w1,
        weights,
    )
    mlp_part, near_queries = fetch(mlp_part, prepared[0])
    mlp_parts, near_queries = lax.optimization_barrier((head_parts(mlp_part), near_queries))
    prepared = (near_queries, *prepared[1:])
    normed = small_call(
        last_kernel,
        "last",
        shape((chips, lat_rows, width), BF),
        *mlp_parts,
        lat_two,
        row(dec_gain),
    )
    own = trade(normed)
    return decode(
        core, queries, query_modality, modality_embed, own, other_core(own), dec_wkv, prepared
    )


def solution(mesh):
    placed = (
        P("inp", None),
        P("inp"),
        P(("inp", "head"), None),
        P(("inp", "head")),
        P(),
        P(),
        P(),
        P(),
        P(None, "head"),
        P(None, None, "head"),
        P(None, "head", None),
        P("head", None),
        P(),
        P(None, None, "head"),
        P("head", "inp", None),
        P("head", None),
        P(),
        P(None, "head"),
        P("head", None),
        P(),
        P(),
        P(),
        P(),
        P(),
        P(),
    )
    return jax.shard_map(
        body, mesh=mesh, in_specs=placed, out_specs=P(("inp", "head"), None), check_vma=False
    )
```
